32 devices in a mesh: col: 8 (over y, x, core), slab: 4 (over z).
Axes of the slice: x: 2, y: 2, z: 4, core: 2. Of those that a mesh axis runs over, the one named last changes fastest.
Arguments:
- offsets: float32 [2, 16, 256, 128], P(None, 'col', 'slab'), may hold values from 0 to 1
- velocity: float32 [2, 16, 256, 128], P(None, 'col', 'slab'), may hold values from -8 to 8
- particle_mass: float32 [16, 256, 128], P('col', 'slab'), may hold values from 0.5 to 2
- pressure_start: float32 [16, 256, 128], P('col', 'slab'), may hold values from -4 to 4
- counts: int32 [16, 256], P('col', 'slab'), may hold values from 1 to 128
- leaving_slot: int32 [64, 4, 128], P('col', 'slab'), may hold values from 0 to 16383
- leaving_count: int32 [64, 4], P('col', 'slab'), may hold values from 1 to 128
- leaving_side: int32 [64, 4], P('col', 'slab'), may hold values from 0 to 1
Outputs:
- density_ratio: float32 [16, 256, 128], P('col', 'slab')
- pressure: float32 [16, 256, 128], P('col', 'slab')
- acceleration: float32 [2, 16, 256, 128], P(None, 'col', 'slab')
- velocity_new: float32 [2, 16, 256, 128], P(None, 'col', 'slab')
- offsets_new: float32 [2, 16, 256, 128], P(None, 'col', 'slab')
- arrived: float32 [2, 6, 64, 4, 128], P(None, None, 'col', 'slab')
The draws below stay inside these ranges and needn't reach their ends.
Inputs may be any that keep to these rules, and one draw needn't show every extreme that they name: `counts`: a cell's particles fill its slots 0 to count - 1. `leaving_slot`: a slot of the sending device's own block of cells. `leaving_count`: the block's slots 0 to count - 1 carry particles. `leaving_side`: 0 sends the block to the lower col index, 1 to the higher.
All inputs are finite; a program needn't handle non-finite values.
Results may differ from the reference program's by a relative error of at most 0.0001.
Values sent between devices are 32-bit elements; how exact they have to be, the bound alone decides.
No kernel may reach another device: no remote copies, remote signals or barrier semaphores. Data moves between devices by JAX's collectives and lax.ppermute only.
A program may use at most 64 MiB of HBM per device.

```python
import math
import jax
import jax.numpy as jnp
from jax import lax

SLOTS = 128
CX = 2
CZ = 64
MIGB = 8
ITERS = 3
NXC = 16
NZC = 256
N_COL = 8
N_SLAB = 4


def set_ends(array, rng, low, top_value):
    longest = array.shape.index(max(array.shape))
    spots = []
    for shift in (0, 1):
        where = [jax.random.randint(jax.random.fold_in(rng, axis), (), 0, length) for axis, length in enumerate(array.shape)]
        where[longest] = (where[longest] + shift) % array.shape[longest]
        spots.append(tuple(where))
    return array.at[spots[0]].set(low).at[spots[1]].set(top_value)


def block_levels(rng, extent, cuts, least, high):
    gain, own = 1.0, jax.random.fold_in(rng, 6)
    for axis_at, parts in cuts:
        heights = jnp.exp(jax.random.uniform(jax.random.fold_in(own, axis_at), (parts,), jnp.float32, least / len(cuts), high / len(cuts)))
        gain = gain * jnp.repeat(heights, extent[axis_at] // parts).reshape([-1 if axis == axis_at else 1 for axis in range(len(extent))])
    return gain


def bell_draw(stream_key, shape, scale, reach, split=(), held_as=jnp.bfloat16):
    array = scale * jax.random.normal(stream_key, shape, jnp.float32)
    if split:
        array = array * block_levels(stream_key, shape, split, -0.22, 0.18)
    return jnp.clip(array, -reach, reach).astype(held_as)


def setup_inputs(seed: int = 0) -> dict:
    streams_of = jax.random.split(jax.random.key(seed), 9)
    return {
        "offsets": jnp.clip(1.0 * jax.random.uniform(streams_of[0], (2, NXC, NZC, SLOTS), jnp.float32) ** block_levels(streams_of[0], (2, NXC, NZC, SLOTS), ((1, 8), (2, 4)), -0.2, 0.2), 0.0, 1.0),
        "velocity": bell_draw(streams_of[1], (2, NXC, NZC, SLOTS), 2.0, 8.0, ((1, 8), (2, 4)), jnp.float32),
        "particle_mass": jnp.clip(jnp.exp(math.log(2.0) - 1.3862944 * jax.random.uniform(streams_of[2], (NXC, NZC, SLOTS), jnp.float32) ** block_levels(streams_of[2], (NXC, NZC, SLOTS), ((0, 8), (1, 4)), -0.2, 0.2)), 0.5, 2.0),
        "pressure_start": bell_draw(streams_of[3], (NXC, NZC, SLOTS), 1.0, 4.0, ((0, 8), (1, 4)), jnp.float32),
        "counts": set_ends(jax.random.randint(streams_of[4], (NXC, NZC), 1, SLOTS + 1), jax.random.fold_in(streams_of[4], 1), 1, SLOTS).astype(jnp.int32),
        "leaving_slot": set_ends(jax.random.randint(streams_of[5], (MIGB * N_COL, N_SLAB, SLOTS), 0, CX * CZ * SLOTS), jax.random.fold_in(streams_of[5], 1), 0, (CX * CZ * SLOTS) - 1).astype(jnp.int32),
        "leaving_count": set_ends(jax.random.randint(streams_of[6], (MIGB * N_COL, N_SLAB), 1, SLOTS + 1), jax.random.fold_in(streams_of[6], 1), 1, SLOTS).astype(jnp.int32),
        "leaving_side": set_ends(jax.random.randint(streams_of[7], (MIGB * N_COL, N_SLAB), 0, 2), jax.random.fold_in(streams_of[7], 1), 0, 1).astype(jnp.int32),
    }


TIME_STEP = 0.1
REST_DENSITY = 50.0
COMPRESSION = 2.0
RELAXATION = 0.5
GRAVITY = 1.0


def geometry(center, neighbor, shift_x, shift_z):
    delta_x = center[0][:, :, None] - neighbor[0][:, None, :] - shift_x
    delta_z = center[1][:, :, None] - neighbor[1][:, None, :] - shift_z
    support = jnp.maximum(1.0 - delta_x * delta_x - delta_z * delta_z, 0.0)
    return delta_x, delta_z, support


def density_terms(center, neighbor, shift_x, shift_z):
    delta_x, delta_z, support = geometry(center, neighbor, shift_x, shift_z)
    kernel = support * support * support
    slope = 6.0 * support * support
    masses = neighbor[4][:, None, :]
    approach = (center[2][:, :, None] - neighbor[2][:, None, :]) * delta_x + (center[3][:, :, None] - neighbor[3][:, None, :]) * delta_z
    return jnp.stack([jnp.sum(masses * kernel, -1), -jnp.sum(masses * slope * approach, -1)])


def jacobi_terms(center, neighbor, shift_x, shift_z):
    delta_x, delta_z, support = geometry(center, neighbor, shift_x, shift_z)
    slope = 6.0 * support * support
    return jnp.stack([jnp.sum(neighbor[2][:, None, :] * slope, -1), jnp.sum(neighbor[3][:, None, :] * slope, -1)])


def force_terms(center, neighbor, shift_x, shift_z):
    delta_x, delta_z, support = geometry(center, neighbor, shift_x, shift_z)
    slope = 6.0 * support * support
    lifted = neighbor[2][:, None, :] * (neighbor[3][:, None, :] - center[3][:, :, None]) * slope
    return jnp.stack([jnp.sum(lifted * delta_x, -1), jnp.sum(lifted * delta_z, -1)])


def column_pass(extended, column_index, depth_cells, pair_terms):
    column_block = lax.dynamic_slice_in_dim(extended, column_index, 3, 1)
    center = column_block[:, 1, 1:depth_cells + 1]
    totals = None
    for shift_x in (-1, 0, 1):
        for shift_z in (-1, 0, 1):
            neighbor = column_block[:, 1 + shift_x, 1 + shift_z:1 + shift_z + depth_cells]
            term = pair_terms(center, neighbor, float(shift_x), float(shift_z))
            totals = term if totals is None else totals + term
    return totals


def sweep(extended, columns, depth_cells, pair_terms):
    def one_column(column_index):
        return column_pass(extended, column_index, depth_cells, pair_terms)

    totals = lax.map(one_column, jnp.arange(columns, dtype=jnp.int32))
    return jnp.moveaxis(totals, 0, 1)


def pad_cells(fields):
    return jnp.pad(fields, ((0, 0), (1, 1), (1, 1), (0, 0)))


def reference(offsets, velocity, particle_mass, pressure_start, counts, leaving_slot, leaving_count, leaving_side):
    columns, depth_cells, slot_count = counts.shape[0], counts.shape[1], offsets.shape[-1]
    alive_mask = jnp.arange(slot_count, dtype=jnp.int32)[None, None, :] < counts[:, :, None]
    live_mass = jnp.where(alive_mask, particle_mass, 0.0)
    base_fields = jnp.concatenate([offsets, velocity, live_mass[None]], 0)
    totals = sweep(pad_cells(base_fields), columns, depth_cells, density_terms)
    density = jnp.where(alive_mask, totals[0], 0.0)
    diverge = totals[1]
    density_ratio = density / REST_DENSITY
    weight = jnp.where(alive_mask, live_mass / jnp.where(alive_mask, density, 1.0), 0.0)
    source = jnp.where(alive_mask, (density + TIME_STEP * diverge - REST_DENSITY) / REST_DENSITY, 0.0)
    pressure = jnp.where(alive_mask, pressure_start, 0.0)
    for sweep_index in range(ITERS):
        stacked = jnp.concatenate([offsets, weight[None], (weight * pressure)[None]], 0)
        totals = sweep(pad_cells(stacked), columns, depth_cells, jacobi_terms)
        diagonal = COMPRESSION + totals[0]
        updated = (1.0 - RELAXATION) * pressure + RELAXATION * (source + totals[1]) / diagonal
        pressure = jnp.where(alive_mask, updated, 0.0)
    stacked = jnp.concatenate([offsets, weight[None], pressure[None]], 0)
    acceleration = jnp.where(alive_mask[None], sweep(pad_cells(stacked), columns, depth_cells, force_terms), 0.0)
    pulled = jnp.stack([acceleration[0], acceleration[1] - GRAVITY])
    velocity_new = jnp.where(alive_mask[None], velocity + TIME_STEP * pulled, 0.0)
    offsets_new = jnp.where(alive_mask[None], offsets + TIME_STEP * velocity_new, 0.0)
    state = jnp.concatenate([offsets_new, velocity_new, pressure[None], live_mass[None]], 0)
    tiles = state.reshape(6, N_COL, CX, N_SLAB, CZ, SLOTS).transpose(1, 3, 0, 2, 4, 5).reshape(N_COL, N_SLAB, 6, CX * CZ * SLOTS)
    chosen = leaving_slot.reshape(N_COL, MIGB, N_SLAB, SLOTS).transpose(0, 2, 1, 3).reshape(N_COL, N_SLAB, 1, MIGB * SLOTS)
    chosen = jnp.broadcast_to(chosen, (N_COL, N_SLAB, 6, MIGB * SLOTS))
    blocks = jnp.take_along_axis(tiles, chosen, axis=3).reshape(N_COL, N_SLAB, 6, MIGB, SLOTS)
    block_count = leaving_count.reshape(N_COL, MIGB, N_SLAB).transpose(0, 2, 1)[:, :, None, :, None]
    block_side = leaving_side.reshape(N_COL, MIGB, N_SLAB).transpose(0, 2, 1)[:, :, None, :, None]
    filled = jnp.arange(SLOTS, dtype=jnp.int32)[None, None, None, None, :] < block_count
    upward = jnp.where(filled & (block_side == 1), blocks, 0.0)
    downward = jnp.where(filled & (block_side == 0), blocks, 0.0)
    from_lower = jnp.concatenate([jnp.zeros_like(upward[:1]), upward[:-1]], 0)
    from_higher = jnp.concatenate([downward[1:], jnp.zeros_like(downward[:1])], 0)
    arrived = jnp.stack([from_lower, from_higher]).transpose(0, 3, 1, 4, 2, 5).reshape(2, 6, N_COL * MIGB, N_SLAB, SLOTS)
    return density_ratio, pressure, acceleration, velocity_new, offsets_new, arrived
```

```python
import functools

import jax
import jax.numpy as jnp
import numpy as np
from jax import lax
from jax.experimental import pallas as pl
from jax.experimental.pallas import tpu as pltpu
from jax.sharding import PartitionSpec as P

ITERS = 3
TIME_STEP = 0.1
REST_DENSITY = 50.0
COMPRESSION = 2.0
RELAXATION = 0.5
GRAVITY = 1.0

HALO = 8
KP = 32
KD = 48
KE = 16
FAR = -64.0
SHIFTS = [(sx, sz) for sx in (-1, 0, 1) for sz in (-1, 0, 1)]
F32 = jnp.float32
BF16 = jnp.bfloat16
VMEM_LIMIT = 56 * 1024 * 1024


def split3(value):
    high = value.astype(BF16).astype(F32)
    rest = value - high
    mid = rest.astype(BF16).astype(F32)
    return [high, mid, rest - mid]


def left_six(parts):
    h, m, l = parts
    return [h, h, h, m, m, l]


def right_six(parts):
    h, m, l = parts
    return [h, m, l, h, m, h]


def position_rows(x, z):
    one, zero = jnp.ones_like(x), jnp.zeros_like(x)
    x, z = x - 0.5, z - 0.5
    xs, zs = split3(x), split3(z)
    square = x * x + z * z
    x2, z2 = [2.0 * v for v in xs], [2.0 * v for v in zs]
    ones = [one] * 3
    target = (
        left_six(x2) + x2 + ones + left_six(z2) + z2 + ones + split3(1.0 - square) + ones + [one, zero]
    )
    source = (
        right_six(xs) + ones + x2 + right_six(zs) + ones + z2 + ones + split3(-square) + [one, zero]
    )
    return target, source


def position_signs(sx, sz):
    return [1] * 6 + [sx] * 3 + [-sx] * 3 + [1] * 6 + [sz] * 3 + [-sz] * 3 + [1] * 6 + [-(sx * sx + sz * sz), 0]


def velocity_rows(x, z, vx, vz):
    one, zero = jnp.ones_like(x), jnp.zeros_like(x)
    x, z = x - 0.5, z - 0.5
    xs, zs, vxs, vzs = split3(x), split3(z), split3(vx), split3(vz)
    dots = split3(vx * x + vz * z)
    ones = [one] * 3
    pad = [zero] * 6
    minus = lambda rows: [-v for v in rows]
    target = dots + left_six(vxs) + left_six(vzs) + left_six(xs) + left_six(zs) + ones + vxs + vzs + ones + ones + pad
    source = (
        ones
        + minus(right_six(xs) + right_six(zs) + right_six(vxs) + right_six(vzs))
        + dots
        + ones
        + ones
        + vxs
        + vzs
        + pad
    )
    return target, source


def velocity_signs(sx, sz):
    return [1] * 30 + [-sx] * 3 + [-sz] * 3 + [sx] * 3 + [sz] * 3 + [0] * 6


def pressure_rows(weight, lifted, pressure):
    one, zero = jnp.ones_like(weight), jnp.zeros_like(weight)
    pad = [zero] * 7
    target = [one] * 3 + left_six(split3(pressure)) + pad
    source = split3(lifted) + [-v for v in right_six(split3(weight))] + pad
    return target, source


def sign_table(signs):
    table = np.asarray([signs(sx, sz) for sx, sz in SHIFTS], np.float32)
    return jnp.broadcast_to(jnp.asarray(table)[:, :, None], (*table.shape, 128)).astype(BF16)


def position_table(cut_first, cut_second):
    table = np.asarray([position_signs(sx, sz) for sx, sz in SHIFTS] * 2, np.float32)
    constant = np.arange(KP) == KP - 2
    sides = np.asarray([sx for sx, _ in SHIFTS] * 2)
    target = np.repeat([0, 1], 9)
    spots = lambda t, side: jnp.asarray(((target == t) & (sides == side))[:, None] & constant)
    table = jnp.where(spots(0, cut_first[1]) & cut_first[0], FAR, jnp.asarray(table))
    table = jnp.where(spots(1, cut_second[1]) & cut_second[0], FAR, table)
    return jnp.broadcast_to(table[:, :, None], (18, KP, 128)).astype(BF16)


def store_rows(rows, stage, dest, cell):
    count = len(rows)
    for index, value in enumerate(rows):
        stage[pl.ds(index, 8, stride=count), :] = value
    dest[pl.ds(cell, 8)] = stage[...].reshape(8, count, 128).astype(BF16)


def pair_tile(left, right, signs):
    return lax.dot_general(
        left, right * signs, (((0,), (0,)), ((), ())), preferred_element_type=F32
    )


def fold(total):
    return jnp.sum(total.T, axis=0, keepdims=True)


def density_kernel(
    low, high, left, own, right, posc, velc,
    out_r, out_l, out_w, out_density, out_source, out_send,
    stage_p, stage_d, vel_r, vel_l, acc,
):
    depth = own.shape[2]
    groups = depth // 8
    blocks = [(left, 0), (left, 1), (own, 0), (own, 1), (right, 0)]

    def prepare(group, carry):
        rows = pl.ds(pl.multiple_of(group * 8, 8), 8)
        for col, (ref, at) in enumerate(blocks):
            x, z, vx, vz = (ref[f, at, rows, :] for f in range(4))
            cell = pl.multiple_of(col * depth + group * 8, 8)
            target, source = position_rows(x, z)
            store_rows(source, stage_p, out_r, cell)
            if 1 <= col <= 3:
                store_rows(target, stage_p, out_l, pl.multiple_of((col - 1) * depth + group * 8, 8))
            if col >= 1:
                target, source = velocity_rows(x, z, vx, vz)
                store_rows(source, stage_d, vel_r, pl.multiple_of((col - 1) * depth + group * 8, 8))
                if 2 <= col <= 3:
                    store_rows(target, stage_d, vel_l, pl.multiple_of((col - 2) * depth + group * 8, 8))
        return carry

    lax.fori_loop(0, groups, prepare, 0)
    acc[...] = jnp.zeros_like(acc)

    def row(k, carry):
        for t in range(2):
            pos_l, vel_l_t = out_l[(t + 1) * depth + k], vel_l[t * depth + k]
            rho = jnp.zeros((128, 128), F32)
            div = jnp.zeros((128, 128), F32)
            for n, (sx, sz) in enumerate(SHIFTS):
                col = t + 1 + sx
                cell = col * depth + k + sz
                s = jnp.maximum(pair_tile(pos_l, out_r[cell + depth], posc[9 * t + n]), 0.0)
                d = pair_tile(vel_l_t, vel_r[cell], velc[n])
                ref, at = blocks[col + 1]
                q = s * s * ref[4, at, pl.ds(k + sz, 1), :]
                rho = rho + q * s
                div = div + q * d
            acc[0, t, pl.ds(k, 1), :] = fold(rho)
            acc[1, t, pl.ds(k, 1), :] = fold(div)
        return carry

    lax.fori_loop(low, high, row, 0)
    mass = own[4]
    alive = mass > 0.0
    density = jnp.where(alive, acc[0], 0.0)
    weight = jnp.where(alive, mass / jnp.where(alive, density, 1.0), 0.0)
    source = jnp.where(
        alive, (density - TIME_STEP * 6.0 * acc[1] - REST_DENSITY) / REST_DENSITY, 0.0
    )
    out_w[...] = weight
    out_density[...] = density / REST_DENSITY
    out_source[...] = source
    out_send[0:2] = weight
    out_send[2] = source[1]


def column_update(alive, pressure, source, pulled, diagonal):
    updated = (1.0 - RELAXATION) * pressure + RELAXATION * (source + 6.0 * pulled) / diagonal
    return jnp.where(alive, updated, 0.0)


def jacobi_rows(low, high, first_col, feat_r, feat_l, posc, wide_u, acc, depth):
    def row(k, carry):
        for t in range(2):
            pos_l = feat_l[(first_col + t) * depth + k]
            total = jnp.zeros((128, 128), F32)
            for n, (sx, sz) in enumerate(SHIFTS):
                col = t + 1 + sx
                cell = (first_col + col) * depth + k + sz
                s = jnp.maximum(pair_tile(pos_l, feat_r[cell], posc[9 * t + n]), 0.0)
                total = total + s * s * wide_u[col, pl.ds(k + sz, 1), :]
            acc[t, pl.ds(k, 1), :] = fold(total)
        return carry

    lax.fori_loop(low, high, row, 0)


def sweep1_kernel(
    low, high, feat_r, feat_l, left, own, recv, weight_own, source_own, posc,
    out_p, out_diag, out_send, wide_w, wide_u, acc,
):
    depth = weight_own.shape[1]
    start_l = jnp.where(left[4] > 0.0, left[5], 0.0)
    start_o = jnp.where(own[4] > 0.0, own[5], 0.0)
    wide_w[0:2] = recv[0:2]
    wide_w[2:4] = weight_own[...]
    wide_u[0:2] = recv[0:2] * start_l
    wide_u[2:4] = weight_own[...] * start_o
    acc[...] = jnp.zeros_like(acc)

    def row(k, carry):
        for t in range(2):
            pos_l = feat_l[t * depth + k]
            total_w = jnp.zeros((128, 128), F32)
            total_u = jnp.zeros((128, 128), F32)
            for n, (sx, sz) in enumerate(SHIFTS):
                col = t + 1 + sx
                s = jnp.maximum(pair_tile(pos_l, feat_r[col * depth + k + sz], posc[9 * t + n]), 0.0)
                q = s * s
                total_w = total_w + q * wide_w[col, pl.ds(k + sz, 1), :]
                total_u = total_u + q * wide_u[col, pl.ds(k + sz, 1), :]
            acc[0, t, pl.ds(k, 1), :] = fold(total_w)
            acc[1, t, pl.ds(k, 1), :] = fold(total_u)
        return carry

    lax.fori_loop(low, high, row, 0)
    diagonal = COMPRESSION + 6.0 * acc[0]
    out_diag[...] = diagonal
    below = column_update(left[4, 1] > 0.0, start_l[1], recv[2], acc[1, 0], diagonal[0])
    here = column_update(own[4, 0] > 0.0, start_o[0], source_own[0], acc[1, 1], diagonal[1])
    out_p[0] = below
    out_p[1] = here
    out_send[0] = below
    out_send[1] = here
    out_send[2] = weight_own[0]
    out_send[3] = diagonal[0]


def sweep2_kernel(
    low, high, feat_r, feat_l, own, recv1, recv2, weight_own, source_own, diag, p1, posc,
    out_p, wide_u, acc,
):
    depth = weight_own.shape[1]
    wide_u[0] = recv1[1] * p1[0]
    wide_u[1] = weight_own[0] * p1[1]
    wide_u[2] = weight_own[1] * recv2[0]
    wide_u[3] = recv2[2] * recv2[1]
    acc[...] = jnp.zeros_like(acc)
    jacobi_rows(low, high, 1, feat_r, feat_l, posc, wide_u, acc, depth)
    out_p[0] = column_update(own[4, 0] > 0.0, p1[1], source_own[0], acc[0], diag[1])
    out_p[1] = column_update(own[4, 1] > 0.0, recv2[0], source_own[1], acc[1], recv2[3])


def sweep3_kernel(
    low, high, feat_r, feat_l, left, own, recv1, recv3, weight_own, source_own, diag, p2, posc,
    out_p, wide_u, acc,
):
    depth = weight_own.shape[1]
    wide_u[0:2] = recv1[0:2] * recv3[...]
    wide_u[2:4] = weight_own[...] * p2[...]
    acc[...] = jnp.zeros_like(acc)
    jacobi_rows(low, high, 0, feat_r, feat_l, posc, wide_u, acc, depth)
    out_p[0] = column_update(left[4, 1] > 0.0, recv3[1], recv1[2], acc[0], diag[0])
    out_p[1] = column_update(own[4, 0] > 0.0, p2[0], source_own[0], acc[1], diag[1])


def force_kernel(
    low, high, feat_r, feat_l, own, recv1, recv2, recv4, left, right, weight_own, p3, posc,
    out_pressure, out_acc, out_velocity, out_offsets,
    wide_p, wide_w, wide_x, wide_z, pres_r, pres_l, stage, acc,
):
    depth = weight_own.shape[1]
    wide_p[0:2] = p3[...]
    wide_p[2:4] = recv4[...]
    wide_w[0] = recv1[1]
    wide_w[1:3] = weight_own[...]
    wide_w[3] = recv2[2]
    for field, wide in ((0, wide_x), (1, wide_z)):
        wide[0] = left[field, 1] - 0.5
        wide[1:3] = own[field] - 0.5
        wide[3] = right[field, 0] - 0.5

    def prepare(group, carry):
        rows = pl.ds(pl.multiple_of(group * 8, 8), 8)
        for col in range(4):
            pressure, weight = wide_p[col, rows, :], wide_w[col, rows, :]
            target, source = pressure_rows(weight, weight * pressure, pressure)
            store_rows(source, stage, pres_r, pl.multiple_of(col * depth + group * 8, 8))
            if 1 <= col <= 2:
                store_rows(target, stage, pres_l, pl.multiple_of((col - 1) * depth + group * 8, 8))
        return carry

    lax.fori_loop(0, depth // 8, prepare, 0)

    def row(k, carry):
        for t in range(2):
            pos_l, pres_l_t = feat_l[(t + 1) * depth + k], pres_l[t * depth + k]
            plain = jnp.zeros((128, 128), F32)
            by_x = jnp.zeros((128, 128), F32)
            by_z = jnp.zeros((128, 128), F32)
            for n, (sx, sz) in enumerate(SHIFTS):
                col = t + 1 + sx
                s = jnp.maximum(pair_tile(pos_l, feat_r[(col + 1) * depth + k + sz], posc[9 * t + n]), 0.0)
                e = lax.dot_general(
                    pres_l_t, pres_r[col * depth + k + sz], (((0,), (0,)), ((), ())),
                    preferred_element_type=F32,
                )
                g = s * s * e
                plain = plain + g
                by_x = by_x + g * (wide_x[col, pl.ds(k + sz, 1), :] + float(sx))
                by_z = by_z + g * (wide_z[col, pl.ds(k + sz, 1), :] + float(sz))
            acc[0, t, pl.ds(k, 1), :] = fold(plain)
            acc[1, t, pl.ds(k, 1), :] = fold(by_x)
            acc[2, t, pl.ds(k, 1), :] = fold(by_z)
        return carry

    lax.fori_loop(low, high, row, 0)
    inner = slice(low, high)
    alive = own[4, :, inner] > 0.0
    out_pressure[0] = p3[1, inner]
    out_pressure[1] = recv4[0, inner]
    for axis, wide, pull in ((0, wide_x, 0.0), (1, wide_z, GRAVITY)):
        force = 6.0 * (wide[1:3, inner] * acc[0, :, inner] - acc[axis + 1, :, inner])
        force = jnp.where(alive, force, 0.0)
        velocity = jnp.where(alive, own[axis + 2, :, inner] + TIME_STEP * (force - pull), 0.0)
        out_acc[axis] = force
        out_velocity[axis] = velocity
        out_offsets[axis] = jnp.where(alive, own[axis, :, inner] + TIME_STEP * velocity, 0.0)


def local_call(kernel, out_shapes, scratch, *operands):
    vmem = pl.BlockSpec(memory_space=pltpu.VMEM)
    return pl.pallas_call(
        kernel,
        out_shape=[jax.ShapeDtypeStruct(shape, dtype) for shape, dtype in out_shapes],
        in_specs=[vmem] * len(operands),
        out_specs=[vmem] * len(out_shapes),
        scratch_shapes=[pltpu.VMEM(shape, dtype) for shape, dtype in scratch],
        compiler_params=pltpu.CompilerParams(vmem_limit_bytes=VMEM_LIMIT),
    )(*operands)


def from_behind(block, axis, distance):
    devices = range(lax.axis_size(axis))
    route = [(i - distance, i) for i in devices if i - distance in devices]
    return lax.ppermute(block, axis, route)


def around(block, axis, distance):
    peers = lax.axis_size(axis)
    return lax.ppermute(block, axis, [(i, (i + distance) % peers) for i in range(peers)])


def per_device(
    offsets, velocity, particle_mass, pressure_start, counts, leaving_slot, leaving_count, leaving_side
):
    cells, slots = counts.shape[1], offsets.shape[-1]
    alive = jnp.arange(slots, dtype=jnp.int32)[None, None, :] < counts[:, :, None]
    live_mass = jnp.where(alive, particle_mass, 0.0)
    base = jnp.concatenate([offsets, velocity, live_mass[None], pressure_start[None]], 0)
    above = from_behind(base[:, :, cells - HALO :], "slab", 1)
    below = from_behind(base[:, :, :HALO], "slab", -1)
    own = jnp.concatenate([above, base, below], 2)
    left = around(own, "col", 1)
    right = around(own[:5, :1], "col", -1)
    depth = cells + 2 * HALO
    first = lax.axis_index("col") == 0
    last = lax.axis_index("col") == lax.axis_size("col") - 1
    here = position_table((first, -1), (last, 1))
    back = position_table((first, 1), (first, -1))
    velc = sign_table(velocity_signs)
    plane = (2, depth, slots)

    def rows(level):
        reach = ITERS + 2 - level
        return HALO - reach, HALO + cells + reach

    feat_r, feat_l, weight, density_ratio, source, send1 = local_call(
        functools.partial(density_kernel, *rows(1)),
        [
            ((5 * depth, KP, slots), BF16),
            ((3 * depth, KP, slots), BF16),
            (plane, F32),
            (plane, F32),
            (plane, F32),
            ((3, depth, slots), F32),
        ],
        [
            ((8 * KP, slots), F32),
            ((8 * KD, slots), F32),
            ((4 * depth, KD, slots), BF16),
            ((2 * depth, KD, slots), BF16),
            ((2, 2, depth, slots), F32),
        ],
        left, own, right, here, velc,
    )
    recv1 = around(send1, "col", 1)
    p1, diag, send2 = local_call(
        functools.partial(sweep1_kernel, *rows(2)),
        [(plane, F32), (plane, F32), ((4, depth, slots), F32)],
        [((4, depth, slots), F32), ((4, depth, slots), F32), ((2, 2, depth, slots), F32)],
        feat_r, feat_l, left, own, recv1, weight, source, back,
    )
    recv2 = around(send2, "col", -1)
    (p2,) = local_call(
        functools.partial(sweep2_kernel, *rows(3)),
        [(plane, F32)],
        [((4, depth, slots), F32), (plane, F32)],
        feat_r, feat_l, own, recv1, recv2, weight, source, diag, p1, here,
    )
    recv3 = around(p2, "col", 1)
    (p3,) = local_call(
        functools.partial(sweep3_kernel, *rows(4)),
        [(plane, F32)],
        [((4, depth, slots), F32), (plane, F32)],
        feat_r, feat_l, left, own, recv1, recv3, weight, source, diag, p2, back,
    )
    recv4 = around(p3, "col", -1)
    inner = (2, cells, slots)
    pressure, acceleration, velocity_new, offsets_new = local_call(
        functools.partial(force_kernel, *rows(5)),
        [(inner, F32), ((2, *inner), F32), ((2, *inner), F32), ((2, *inner), F32)],
        [((4, depth, slots), F32)] * 4
        + [
            ((4 * depth, KE, slots), BF16),
            ((2 * depth, KE, slots), BF16),
            ((8 * KE, slots), F32),
            ((3, *plane), F32),
        ],
        feat_r, feat_l, own, recv1, recv2, recv4, left, right, weight, p3, here,
    )
    density_ratio = density_ratio[:, HALO : HALO + cells]
    state = jnp.concatenate([offsets_new, velocity_new, pressure[None], live_mass[None]], 0).reshape(6, -1)
    block_rows = leaving_slot.shape[0]
    blocks = state[:, leaving_slot.reshape(-1)].reshape(6, block_rows, 1, slots)
    filled = jnp.arange(slots, dtype=jnp.int32)[None, None, :] < leaving_count[:, :, None]
    upward = jnp.where(filled & (leaving_side[:, :, None] == 1), blocks, 0.0)
    downward = jnp.where(filled & (leaving_side[:, :, None] == 0), blocks, 0.0)
    arrived = jnp.stack([from_behind(upward, "col", 1), from_behind(downward, "col", -1)])
    return (density_ratio, pressure, acceleration, velocity_new, offsets_new, arrived)


def solution(mesh):
    return jax.shard_map(
        per_device,
        mesh=mesh,
        in_specs=(
            P(None, "col", "slab", None),
            P(None, "col", "slab", None),
            P("col", "slab", None),
            P("col", "slab", None),
            P("col", "slab"),
            P("col", "slab", None),
            P("col", "slab"),
            P("col", "slab"),
        ),
        out_specs=(
            P("col", "slab", None),
            P("col", "slab", None),
            P(None, "col", "slab", None),
            P(None, "col", "slab", None),
            P(None, "col", "slab", None),
            P(None, None, "col", "slab", None),
        ),
        check_vma=False,
    )
```

```python
import functools

import jax
import jax.numpy as jnp
import numpy as np
from jax import lax
from jax.experimental import pallas as pl
from jax.experimental.pallas import tpu as pltpu
from jax.sharding import PartitionSpec as P

ITERS = 3
TIME_STEP = 0.1
REST_DENSITY = 50.0
COMPRESSION = 2.0
RELAXATION = 0.5
GRAVITY = 1.0

HALO = 8
UNROLL = 2
KP = 32
KD = 48
KE = 16
FAR = -64.0
SHIFTS = [(sx, sz) for sx in (-1, 0, 1) for sz in (-1, 0, 1)]
F32 = jnp.float32
BF16 = jnp.bfloat16
VMEM_LIMIT = 56 * 1024 * 1024


def split3(value):
    high = value.astype(BF16).astype(F32)
    rest = value - high
    mid = rest.astype(BF16).astype(F32)
    return [high, mid, rest - mid]


def left_six(parts):
    h, m, l = parts
    return [h, h, h, m, m, l]


def right_six(parts):
    h, m, l = parts
    return [h, m, l, h, m, h]


def position_rows(x, z):
    one, zero = jnp.ones_like(x), jnp.zeros_like(x)
    x, z = x - 0.5, z - 0.5
    xs, zs = split3(x), split3(z)
    square = x * x + z * z
    x2, z2 = [2.0 * v for v in xs], [2.0 * v for v in zs]
    ones = [one] * 3
    target = (
        left_six(x2) + x2 + ones + left_six(z2) + z2 + ones + split3(1.0 - square) + ones + [one, zero]
    )
    source = (
        right_six(xs) + ones + x2 + right_six(zs) + ones + z2 + ones + split3(-square) + [one, zero]
    )
    return target, source


def position_signs(sx, sz):
    return [1] * 6 + [sx] * 3 + [-sx] * 3 + [1] * 6 + [sz] * 3 + [-sz] * 3 + [1] * 6 + [-(sx * sx + sz * sz), 0]


def velocity_rows(x, z, vx, vz):
    one, zero = jnp.ones_like(x), jnp.zeros_like(x)
    x, z = x - 0.5, z - 0.5
    xs, zs, vxs, vzs = split3(x), split3(z), split3(vx), split3(vz)
    dots = split3(vx * x + vz * z)
    ones = [one] * 3
    pad = [zero] * 6
    minus = lambda rows: [-v for v in rows]
    target = dots + left_six(vxs) + left_six(vzs) + left_six(xs) + left_six(zs) + ones + vxs + vzs + ones + ones + pad
    source = (
        ones
        + minus(right_six(xs) + right_six(zs) + right_six(vxs) + right_six(vzs))
        + dots
        + ones
        + ones
        + vxs
        + vzs
        + pad
    )
    return target, source


def velocity_signs(sx, sz):
    return [1] * 30 + [-sx] * 3 + [-sz] * 3 + [sx] * 3 + [sz] * 3 + [0] * 6


def pressure_rows(weight, lifted, pressure):
    one, zero = jnp.ones_like(weight), jnp.zeros_like(weight)
    pad = [zero] * 7
    target = [one] * 3 + left_six(split3(pressure)) + pad
    source = split3(lifted) + [-v for v in right_six(split3(weight))] + pad
    return target, source


def sign_table(signs):
    table = np.asarray([signs(sx, sz) for sx, sz in SHIFTS], np.float32)
    return jnp.broadcast_to(jnp.asarray(table)[:, :, None], (*table.shape, 128)).astype(BF16)


def position_table(cut_first, cut_second):
    table = np.asarray([position_signs(sx, sz) for sx, sz in SHIFTS] * 2, np.float32)
    constant = np.arange(KP) == KP - 2
    sides = np.asarray([sx for sx, _ in SHIFTS] * 2)
    target = np.repeat([0, 1], 9)
    spots = lambda t, side: jnp.asarray(((target == t) & (sides == side))[:, None] & constant)
    table = jnp.where(spots(0, cut_first[1]) & cut_first[0], FAR, jnp.asarray(table))
    table = jnp.where(spots(1, cut_second[1]) & cut_second[0], FAR, table)
    return jnp.broadcast_to(table[:, :, None], (18, KP, 128)).astype(BF16)


def store_rows(rows, stage, dest, cell):
    count = len(rows)
    for index, value in enumerate(rows):
        stage[pl.ds(index, 8, stride=count), :] = value
    dest[pl.ds(cell, 8)] = stage[...].reshape(8, count, 128).astype(BF16)


def upright(rows):
    return rows.astype(F32).T.astype(BF16)


def tiles(left, sources):
    product = jnp.dot(left, jnp.concatenate(sources, axis=1), preferred_element_type=F32)
    return [product[:, 128 * i : 128 * (i + 1)] for i in range(3)]


def signed(feat, cell, table, first):
    return [feat[cell + sz] * table[first + sz + 1] for sz in (-1, 0, 1)]


def fold(total):
    return jnp.sum(total.T, axis=0, keepdims=True)


def each_row(low, high, row):
    def step(i, carry):
        for u in range(UNROLL):
            row(low + i * UNROLL + u)
        return carry

    lax.fori_loop(0, (high - low) // UNROLL, step, 0)


def density_kernel(
    low, high, left, own, right, posc, velc,
    out_r, out_l, out_w, out_density, out_source, out_send,
    stage_p, stage_d, vel_r, vel_l, acc,
):
    depth = own.shape[2]
    groups = depth // 8
    blocks = [(left, 0), (left, 1), (own, 0), (own, 1), (right, 0)]

    def prepare(group, carry):
        rows = pl.ds(pl.multiple_of(group * 8, 8), 8)
        for col, (ref, at) in enumerate(blocks):
            x, z, vx, vz = (ref[f, at, rows, :] for f in range(4))
            cell = pl.multiple_of(col * depth + group * 8, 8)
            target, source = position_rows(x, z)
            store_rows(source, stage_p, out_r, cell)
            if 1 <= col <= 3:
                store_rows(target, stage_p, out_l, pl.multiple_of((col - 1) * depth + group * 8, 8))
            if col >= 1:
                target, source = velocity_rows(x, z, vx, vz)
                store_rows(source, stage_d, vel_r, pl.multiple_of((col - 1) * depth + group * 8, 8))
                if 2 <= col <= 3:
                    store_rows(target, stage_d, vel_l, pl.multiple_of((col - 2) * depth + group * 8, 8))
        return carry

    lax.fori_loop(0, groups, prepare, 0)
    acc[...] = jnp.zeros_like(acc)

    def row(k):
        for t in range(2):
            pos_l, vel_l_t = upright(out_l[(t + 1) * depth + k]), upright(vel_l[t * depth + k])
            rho = jnp.zeros((128, 128), F32)
            div = jnp.zeros((128, 128), F32)
            for sx in range(3):
                cell = (t + sx) * depth + k
                reach = tiles(pos_l, signed(out_r, cell + depth, posc, 9 * t + 3 * sx))
                closing = tiles(vel_l_t, signed(vel_r, cell, velc, 3 * sx))
                ref, at = blocks[t + sx + 1]
                for sz in range(3):
                    s = jnp.maximum(reach[sz], 0.0)
                    q = s * s * ref[4, at, pl.ds(k + sz - 1, 1), :]
                    rho = rho + q * s
                    div = div + q * closing[sz]
            acc[0, t, pl.ds(k, 1), :] = fold(rho)
            acc[1, t, pl.ds(k, 1), :] = fold(div)

    each_row(low, high, row)
    mass = own[4]
    alive = mass > 0.0
    density = jnp.where(alive, acc[0], 0.0)
    weight = jnp.where(alive, mass / jnp.where(alive, density, 1.0), 0.0)
    source = jnp.where(
        alive, (density - TIME_STEP * 6.0 * acc[1] - REST_DENSITY) / REST_DENSITY, 0.0
    )
    out_w[...] = weight
    out_density[...] = density / REST_DENSITY
    out_source[...] = source
    out_send[0:2] = weight
    out_send[2] = source[1]


def column_update(alive, pressure, source, pulled, diagonal):
    updated = (1.0 - RELAXATION) * pressure + RELAXATION * (source + 6.0 * pulled) / diagonal
    return jnp.where(alive, updated, 0.0)


def jacobi_rows(low, high, first_col, feat_r, feat_l, posc, wide_u, acc, depth):
    def row(k):
        for t in range(2):
            pos_l = upright(feat_l[(first_col + t) * depth + k])
            total = jnp.zeros((128, 128), F32)
            for sx in range(3):
                cell = (first_col + t + sx) * depth + k
                reach = tiles(pos_l, signed(feat_r, cell, posc, 9 * t + 3 * sx))
                for sz in range(3):
                    s = jnp.maximum(reach[sz], 0.0)
                    total = total + s * s * wide_u[t + sx, pl.ds(k + sz - 1, 1), :]
            acc[t, pl.ds(k, 1), :] = fold(total)

    each_row(low, high, row)


def sweep1_kernel(
    low, high, feat_r, feat_l, left, own, recv, weight_own, source_own, posc,
    out_p, out_diag, out_send, wide_w, wide_u, acc,
):
    depth = weight_own.shape[1]
    start_l = jnp.where(left[4] > 0.0, left[5], 0.0)
    start_o = jnp.where(own[4] > 0.0, own[5], 0.0)
    wide_w[0:2] = recv[0:2]
    wide_w[2:4] = weight_own[...]
    wide_u[0:2] = recv[0:2] * start_l
    wide_u[2:4] = weight_own[...] * start_o
    acc[...] = jnp.zeros_like(acc)

    def row(k):
        for t in range(2):
            pos_l = upright(feat_l[t * depth + k])
            total_w = jnp.zeros((128, 128), F32)
            total_u = jnp.zeros((128, 128), F32)
            for sx in range(3):
                col = t + sx
                reach = tiles(pos_l, signed(feat_r, col * depth + k, posc, 9 * t + 3 * sx))
                for sz in range(3):
                    s = jnp.maximum(reach[sz], 0.0)
                    q = s * s
                    total_w = total_w + q * wide_w[col, pl.ds(k + sz - 1, 1), :]
                    total_u = total_u + q * wide_u[col, pl.ds(k + sz - 1, 1), :]
            acc[0, t, pl.ds(k, 1), :] = fold(total_w)
            acc[1, t, pl.ds(k, 1), :] = fold(total_u)

    each_row(low, high, row)
    diagonal = COMPRESSION + 6.0 * acc[0]
    out_diag[...] = diagonal
    below = column_update(left[4, 1] > 0.0, start_l[1], recv[2], acc[1, 0], diagonal[0])
    here = column_update(own[4, 0] > 0.0, start_o[0], source_own[0], acc[1, 1], diagonal[1])
    out_p[0] = below
    out_p[1] = here
    out_send[0] = below
    out_send[1] = here
    out_send[2] = weight_own[0]
    out_send[3] = diagonal[0]


def sweep2_kernel(
    low, high, feat_r, feat_l, own, recv1, recv2, weight_own, source_own, diag, p1, posc,
    out_p, wide_u, acc,
):
    depth = weight_own.shape[1]
    wide_u[0] = recv1[1] * p1[0]
    wide_u[1] = weight_own[0] * p1[1]
    wide_u[2] = weight_own[1] * recv2[0]
    wide_u[3] = recv2[2] * recv2[1]
    acc[...] = jnp.zeros_like(acc)
    jacobi_rows(low, high, 1, feat_r, feat_l, posc, wide_u, acc, depth)
    out_p[0] = column_update(own[4, 0] > 0.0, p1[1], source_own[0], acc[0], diag[1])
    out_p[1] = column_update(own[4, 1] > 0.0, recv2[0], source_own[1], acc[1], recv2[3])


def sweep3_kernel(
    low, high, feat_r, feat_l, left, own, recv1, recv3, weight_own, source_own, diag, p2, posc,
    out_p, wide_u, acc,
):
    depth = weight_own.shape[1]
    wide_u[0:2] = recv1[0:2] * recv3[...]
    wide_u[2:4] = weight_own[...] * p2[...]
    acc[...] = jnp.zeros_like(acc)
    jacobi_rows(low, high, 0, feat_r, feat_l, posc, wide_u, acc, depth)
    out_p[0] = column_update(left[4, 1] > 0.0, recv3[1], recv1[2], acc[0], diag[0])
    out_p[1] = column_update(own[4, 0] > 0.0, p2[0], source_own[0], acc[1], diag[1])


def force_kernel(
    low, high, feat_r, feat_l, own, recv1, recv2, recv4, left, right, weight_own, p3, posc,
    out_pressure, out_acc, out_velocity, out_offsets,
    wide_p, wide_w, wide_x, wide_z, pres_r, pres_l, stage, acc,
):
    depth = weight_own.shape[1]
    wide_p[0:2] = p3[...]
    wide_p[2:4] = recv4[...]
    wide_w[0] = recv1[1]
    wide_w[1:3] = weight_own[...]
    wide_w[3] = recv2[2]
    for field, wide in ((0, wide_x), (1, wide_z)):
        wide[0] = left[field, 1] - 0.5
        wide[1:3] = own[field] - 0.5
        wide[3] = right[field, 0] - 0.5

    def prepare(group, carry):
        rows = pl.ds(pl.multiple_of(group * 8, 8), 8)
        for col in range(4):
            pressure, weight = wide_p[col, rows, :], wide_w[col, rows, :]
            target, source = pressure_rows(weight, weight * pressure, pressure)
            store_rows(source, stage, pres_r, pl.multiple_of(col * depth + group * 8, 8))
            if 1 <= col <= 2:
                store_rows(target, stage, pres_l, pl.multiple_of((col - 1) * depth + group * 8, 8))
        return carry

    lax.fori_loop(0, depth // 8, prepare, 0)

    def row(k):
        for t in range(2):
            pos_l, pres_l_t = upright(feat_l[(t + 1) * depth + k]), upright(pres_l[t * depth + k])
            plain = jnp.zeros((128, 128), F32)
            by_x = jnp.zeros((128, 128), F32)
            by_z = jnp.zeros((128, 128), F32)
            for sx in range(3):
                col = t + sx
                cell = col * depth + k
                reach = tiles(pos_l, signed(feat_r, cell + depth, posc, 9 * t + 3 * sx))
                lift = tiles(pres_l_t, [pres_r[cell + sz] for sz in (-1, 0, 1)])
                for sz in range(3):
                    s = jnp.maximum(reach[sz], 0.0)
                    g = s * s * lift[sz]
                    at = pl.ds(k + sz - 1, 1)
                    plain = plain + g
                    by_x = by_x + g * (wide_x[col, at, :] + float(sx - 1))
                    by_z = by_z + g * (wide_z[col, at, :] + float(sz - 1))
            acc[0, t, pl.ds(k, 1), :] = fold(plain)
            acc[1, t, pl.ds(k, 1), :] = fold(by_x)
            acc[2, t, pl.ds(k, 1), :] = fold(by_z)

    each_row(low, high, row)
    inner = slice(HALO, depth - HALO)
    alive = own[4, :, inner] > 0.0
    out_pressure[0] = p3[1, inner]
    out_pressure[1] = recv4[0, inner]
    for axis, wide, pull in ((0, wide_x, 0.0), (1, wide_z, GRAVITY)):
        force = 6.0 * (wide[1:3, inner] * acc[0, :, inner] - acc[axis + 1, :, inner])
        force = jnp.where(alive, force, 0.0)
        velocity = jnp.where(alive, own[axis + 2, :, inner] + TIME_STEP * (force - pull), 0.0)
        out_acc[axis] = force
        out_velocity[axis] = velocity
        out_offsets[axis] = jnp.where(alive, own[axis, :, inner] + TIME_STEP * velocity, 0.0)


def local_call(kernel, out_shapes, scratch, *operands):
    vmem = pl.BlockSpec(memory_space=pltpu.VMEM)
    return pl.pallas_call(
        kernel,
        out_shape=[jax.ShapeDtypeStruct(shape, dtype) for shape, dtype in out_shapes],
        in_specs=[vmem] * len(operands),
        out_specs=[vmem] * len(out_shapes),
        scratch_shapes=[pltpu.VMEM(shape, dtype) for shape, dtype in scratch],
        compiler_params=pltpu.CompilerParams(vmem_limit_bytes=VMEM_LIMIT),
    )(*operands)


def from_behind(block, axis, distance):
    devices = range(lax.axis_size(axis))
    route = [(i - distance, i) for i in devices if i - distance in devices]
    return lax.ppermute(block, axis, route)


def around(block, axis, distance):
    peers = lax.axis_size(axis)
    return lax.ppermute(block, axis, [(i, (i + distance) % peers) for i in range(peers)])


def per_device(
    offsets, velocity, particle_mass, pressure_start, counts, leaving_slot, leaving_count, leaving_side
):
    cells, slots = counts.shape[1], offsets.shape[-1]
    alive = jnp.arange(slots, dtype=jnp.int32)[None, None, :] < counts[:, :, None]
    live_mass = jnp.where(alive, particle_mass, 0.0)
    base = jnp.concatenate([offsets, velocity, live_mass[None], pressure_start[None]], 0)
    above = from_behind(base[:, :, cells - HALO :], "slab", 1)
    below = from_behind(base[:, :, :HALO], "slab", -1)
    own = jnp.concatenate([above, base, below], 2)
    left = around(own, "col", 1)
    right = around(own[:5, :1], "col", -1)
    depth = cells + 2 * HALO
    first = lax.axis_index("col") == 0
    last = lax.axis_index("col") == lax.axis_size("col") - 1
    here = position_table((first, -1), (last, 1))
    back = position_table((first, 1), (first, -1))
    velc = sign_table(velocity_signs)
    plane = (2, depth, slots)

    def rows(level):
        reach = ITERS + 2 - level
        low = HALO - reach
        steps = -(-(cells + 2 * reach) // UNROLL)
        assert low + steps * UNROLL < depth
        return low, low + steps * UNROLL

    feat_r, feat_l, weight, density_ratio, source, send1 = local_call(
        functools.partial(density_kernel, *rows(1)),
        [
            ((5 * depth, KP, slots), BF16),
            ((3 * depth, KP, slots), BF16),
            (plane, F32),
            (plane, F32),
            (plane, F32),
            ((3, depth, slots), F32),
        ],
        [
            ((8 * KP, slots), F32),
            ((8 * KD, slots), F32),
            ((4 * depth, KD, slots), BF16),
            ((2 * depth, KD, slots), BF16),
            ((2, 2, depth, slots), F32),
        ],
        left, own, right, here, velc,
    )
    recv1 = around(send1, "col", 1)
    p1, diag, send2 = local_call(
        functools.partial(sweep1_kernel, *rows(2)),
        [(plane, F32), (plane, F32), ((4, depth, slots), F32)],
        [((4, depth, slots), F32), ((4, depth, slots), F32), ((2, 2, depth, slots), F32)],
        feat_r, feat_l, left, own, recv1, weight, source, back,
    )
    recv2 = around(send2, "col", -1)
    (p2,) = local_call(
        functools.partial(sweep2_kernel, *rows(3)),
        [(plane, F32)],
        [((4, depth, slots), F32), (plane, F32)],
        feat_r, feat_l, own, recv1, recv2, weight, source, diag, p1, here,
    )
    recv3 = around(p2, "col", 1)
    (p3,) = local_call(
        functools.partial(sweep3_kernel, *rows(4)),
        [(plane, F32)],
        [((4, depth, slots), F32), (plane, F32)],
        feat_r, feat_l, left, own, recv1, recv3, weight, source, diag, p2, back,
    )
    recv4 = around(p3, "col", -1)
    inner = (2, cells, slots)
    pressure, acceleration, velocity_new, offsets_new = local_call(
        functools.partial(force_kernel, *rows(5)),
        [(inner, F32), ((2, *inner), F32), ((2, *inner), F32), ((2, *inner), F32)],
        [((4, depth, slots), F32)] * 4
        + [
            ((4 * depth, KE, slots), BF16),
            ((2 * depth, KE, slots), BF16),
            ((8 * KE, slots), F32),
            ((3, *plane), F32),
        ],
        feat_r, feat_l, own, recv1, recv2, recv4, left, right, weight, p3, here,
    )
    density_ratio = density_ratio[:, HALO : HALO + cells]
    state = jnp.concatenate([offsets_new, velocity_new, pressure[None], live_mass[None]], 0).reshape(6, -1)
    block_rows = leaving_slot.shape[0]
    blocks = state[:, leaving_slot.reshape(-1)].reshape(6, block_rows, 1, slots)
    filled = jnp.arange(slots, dtype=jnp.int32)[None, None, :] < leaving_count[:, :, None]
    upward = jnp.where(filled & (leaving_side[:, :, None] == 1), blocks, 0.0)
    downward = jnp.where(filled & (leaving_side[:, :, None] == 0), blocks, 0.0)
    arrived = jnp.stack([from_behind(upward, "col", 1), from_behind(downward, "col", -1)])
    return (density_ratio, pressure, acceleration, velocity_new, offsets_new, arrived)


def solution(mesh):
    return jax.shard_map(
        per_device,
        mesh=mesh,
        in_specs=(
            P(None, "col", "slab", None),
            P(None, "col", "slab", None),
            P("col", "slab", None),
            P("col", "slab", None),
            P("col", "slab"),
            P("col", "slab", None),
            P("col", "slab"),
            P("col", "slab"),
        ),
        out_specs=(
            P("col", "slab", None),
            P("col", "slab", None),
            P(None, "col", "slab", None),
            P(None, "col", "slab", None),
            P(None, "col", "slab", None),
            P(None, None, "col", "slab", None),
        ),
        check_vma=False,
    )
```

```python
import functools

import jax
import jax.numpy as jnp
import numpy as np
from jax import lax
from jax.experimental import pallas as pl
from jax.experimental.pallas import tpu as pltpu
from jax.sharding import PartitionSpec as P

ITERS = 3
TIME_STEP = 0.1
REST_DENSITY = 50.0
COMPRESSION = 2.0
RELAXATION = 0.5
GRAVITY = 1.0

HALO = 8
CLASSES = ((32, 16), (64, 8), (96, 6), (128, 6))
KP = 32
KD = 48
KE = 16
FAR = -64.0
SHIFTS = [(sx, sz) for sx in (-1, 0, 1) for sz in (-1, 0, 1)]
F32 = jnp.float32
BF16 = jnp.bfloat16
VMEM_LIMIT = 56 * 1024 * 1024


def split3(value):
    high = value.astype(BF16).astype(F32)
    rest = value - high
    mid = rest.astype(BF16).astype(F32)
    return [high, mid, rest - mid]


def left_six(parts):
    h, m, l = parts
    return [h, h, h, m, m, l]


def right_six(parts):
    h, m, l = parts
    return [h, m, l, h, m, h]


def position_rows(x, z):
    one, zero = jnp.ones_like(x), jnp.zeros_like(x)
    x, z = x - 0.5, z - 0.5
    xs, zs = split3(x), split3(z)
    square = x * x + z * z
    x2, z2 = [2.0 * v for v in xs], [2.0 * v for v in zs]
    ones = [one] * 3
    target = (
        left_six(x2) + x2 + ones + left_six(z2) + z2 + ones + split3(1.0 - square) + ones + [one, zero]
    )
    source = (
        right_six(xs) + ones + x2 + right_six(zs) + ones + z2 + ones + split3(-square) + [one, zero]
    )
    return target, source


def position_signs(sx, sz):
    return [1] * 6 + [sx] * 3 + [-sx] * 3 + [1] * 6 + [sz] * 3 + [-sz] * 3 + [1] * 6 + [-(sx * sx + sz * sz), 0]


def velocity_rows(x, z, vx, vz):
    one, zero = jnp.ones_like(x), jnp.zeros_like(x)
    x, z = x - 0.5, z - 0.5
    xs, zs, vxs, vzs = split3(x), split3(z), split3(vx), split3(vz)
    dots = split3(vx * x + vz * z)
    ones = [one] * 3
    pad = [zero] * 6
    minus = lambda rows: [-v for v in rows]
    target = dots + left_six(vxs) + left_six(vzs) + left_six(xs) + left_six(zs) + ones + vxs + vzs + ones + ones + pad
    source = (
        ones
        + minus(right_six(xs) + right_six(zs) + right_six(vxs) + right_six(vzs))
        + dots
        + ones
        + ones
        + vxs
        + vzs
        + pad
    )
    return target, source


def velocity_signs(sx, sz):
    return [1] * 30 + [-sx] * 3 + [-sz] * 3 + [sx] * 3 + [sz] * 3 + [0] * 6


def pressure_rows(weight, lifted, pressure):
    one, zero = jnp.ones_like(weight), jnp.zeros_like(weight)
    pad = [zero] * 7
    target = [one] * 3 + left_six(split3(pressure)) + pad
    source = split3(lifted) + [-v for v in right_six(split3(weight))] + pad
    return target, source


def sign_table(signs):
    table = np.asarray([signs(sx, sz) for sx, sz in SHIFTS], np.float32)
    return jnp.broadcast_to(jnp.asarray(table)[:, :, None], (*table.shape, 128)).astype(BF16)


def position_table(cut_first, cut_second):
    table = np.asarray([position_signs(sx, sz) for sx, sz in SHIFTS] * 2, np.float32)
    constant = np.arange(KP) == KP - 2
    sides = np.asarray([sx for sx, _ in SHIFTS] * 2)
    target = np.repeat([0, 1], 9)
    spots = lambda t, side: jnp.asarray(((target == t) & (sides == side))[:, None] & constant)
    table = jnp.where(spots(0, cut_first[1]) & cut_first[0], FAR, jnp.asarray(table))
    table = jnp.where(spots(1, cut_second[1]) & cut_second[0], FAR, table)
    return jnp.broadcast_to(table[:, :, None], (18, KP, 128)).astype(BF16)


def store_rows(rows, stage, dest, cell):
    count = len(rows)
    for index, value in enumerate(rows):
        stage[pl.ds(index, 8, stride=count), :] = value
    dest[pl.ds(cell, 8)] = stage[...].reshape(8, count, 128).astype(BF16)


def upright(rows, slots):
    return rows.astype(F32).T[:slots].astype(BF16)


def tiles(left, sources):
    product = jnp.dot(left, jnp.concatenate(sources, axis=1), preferred_element_type=F32)
    return [product[:, 128 * i : 128 * (i + 1)] for i in range(3)]


def signed(feat, cell, table, first):
    return [feat[cell + sz] * table[first + sz + 1] for sz in (-1, 0, 1)]


def fold(total):
    return jnp.sum(total.T, axis=0, keepdims=True)


def each_target(level, order, bounds, target):
    for index, (slots, cells) in enumerate(CLASSES):
        start = bounds[level, index]
        steps = (bounds[level, index + 1] - start + cells - 1) // cells

        def step(i, carry, slots=slots, cells=cells, start=start):
            for u in range(cells):
                target(order[level, start + i * cells + u], slots)
            return carry

        lax.fori_loop(0, steps, step, 0)


def density_kernel(
    level, order, bounds, left, own, right, posc, velc,
    out_r, out_l, out_w, out_density, out_source, out_send,
    stage_p, stage_d, vel_r, vel_l, wide_m, acc,
):
    depth = own.shape[2]
    groups = depth // 8
    blocks = [(left, 0), (left, 1), (own, 0), (own, 1), (right, 0)]

    def prepare(group, carry):
        rows = pl.ds(pl.multiple_of(group * 8, 8), 8)
        for col, (ref, at) in enumerate(blocks):
            x, z, vx, vz = (ref[f, at, rows, :] for f in range(4))
            cell = pl.multiple_of(col * depth + group * 8, 8)
            target, source = position_rows(x, z)
            store_rows(source, stage_p, out_r, cell)
            if 1 <= col <= 3:
                store_rows(target, stage_p, out_l, pl.multiple_of((col - 1) * depth + group * 8, 8))
            if col >= 1:
                target, source = velocity_rows(x, z, vx, vz)
                store_rows(source, stage_d, vel_r, pl.multiple_of((col - 1) * depth + group * 8, 8))
                if 2 <= col <= 3:
                    store_rows(target, stage_d, vel_l, pl.multiple_of((col - 2) * depth + group * 8, 8))
        return carry

    lax.fori_loop(0, groups, prepare, 0)
    acc[...] = jnp.zeros_like(acc)

    wide_m[0:depth] = left[4, 1]
    wide_m[depth : 2 * depth] = own[4, 0]
    wide_m[2 * depth : 3 * depth] = own[4, 1]
    wide_m[3 * depth : 4 * depth] = right[4, 0]

    def target(cell, slots):
        sign = 9 * (cell >= depth).astype(jnp.int32)
        pos_l, vel_l_t = upright(out_l[cell + depth], slots), upright(vel_l[cell], slots)
        rho = jnp.zeros((slots, 128), F32)
        div = jnp.zeros((slots, 128), F32)
        for sx in range(3):
            source = cell + sx * depth
            reach = tiles(pos_l, signed(out_r, source + depth, posc, sign + 3 * sx))
            closing = tiles(vel_l_t, signed(vel_r, source, velc, 3 * sx))
            for sz in range(3):
                s = jnp.maximum(reach[sz], 0.0)
                q = s * s * wide_m[pl.ds(source + sz - 1, 1), :]
                rho = rho + q * s
                div = div + q * closing[sz]
        acc[0, pl.ds(cell, 1), 0:slots] = fold(rho)
        acc[1, pl.ds(cell, 1), 0:slots] = fold(div)

    each_target(level, order, bounds, target)
    density = acc[0].reshape(2, depth, 128)
    div = -6.0 * acc[1].reshape(2, depth, 128)
    mass = own[4]
    alive = mass > 0.0
    density = jnp.where(alive, density, 0.0)
    weight = jnp.where(alive, mass / jnp.where(alive, density, 1.0), 0.0)
    source = jnp.where(
        alive, (density + TIME_STEP * div - REST_DENSITY) / REST_DENSITY, 0.0
    )
    out_w[...] = weight
    out_density[...] = density / REST_DENSITY
    out_source[...] = source
    out_send[0:2] = weight
    out_send[2] = source[1]


def column_update(alive, pressure, source, pulled, diagonal):
    updated = (1.0 - RELAXATION) * pressure + RELAXATION * (source + 6.0 * pulled) / diagonal
    return jnp.where(alive, updated, 0.0)


def jacobi_sums(level, order, bounds, first_col, feat_r, feat_l, posc, wide_u, acc, depth):
    def target(cell, slots):
        sign = 9 * (cell >= depth).astype(jnp.int32)
        at = cell + first_col * depth
        pos_l = upright(feat_l[at], slots)
        total = jnp.zeros((slots, 128), F32)
        for sx in range(3):
            reach = tiles(pos_l, signed(feat_r, at + sx * depth, posc, sign + 3 * sx))
            for sz in range(3):
                s = jnp.maximum(reach[sz], 0.0)
                total = total + s * s * wide_u[pl.ds(cell + sx * depth + sz - 1, 1), :]
        acc[pl.ds(cell, 1), 0:slots] = fold(total)

    acc[...] = jnp.zeros_like(acc)
    each_target(level, order, bounds, target)
    return acc[...].reshape(2, depth, 128)


def sweep1_kernel(
    level, order, bounds, feat_r, feat_l, left, own, recv, weight_own, source_own, posc,
    out_p, out_diag, out_send, wide_w, wide_u, acc,
):
    depth = weight_own.shape[1]
    start_l = jnp.where(left[4] > 0.0, left[5], 0.0)
    start_o = jnp.where(own[4] > 0.0, own[5], 0.0)
    for col in range(4):
        rows = slice(col * depth, (col + 1) * depth)
        weight = recv[col] if col < 2 else weight_own[col - 2]
        wide_w[rows] = weight
        wide_u[rows] = weight * (start_l if col < 2 else start_o)[col % 2]
    acc[...] = jnp.zeros_like(acc)

    def target(cell, slots):
        sign = 9 * (cell >= depth).astype(jnp.int32)
        pos_l = upright(feat_l[cell], slots)
        total_w = jnp.zeros((slots, 128), F32)
        total_u = jnp.zeros((slots, 128), F32)
        for sx in range(3):
            source = cell + sx * depth
            reach = tiles(pos_l, signed(feat_r, source, posc, sign + 3 * sx))
            for sz in range(3):
                s = jnp.maximum(reach[sz], 0.0)
                q = s * s
                total_w = total_w + q * wide_w[pl.ds(source + sz - 1, 1), :]
                total_u = total_u + q * wide_u[pl.ds(source + sz - 1, 1), :]
        acc[0, pl.ds(cell, 1), 0:slots] = fold(total_w)
        acc[1, pl.ds(cell, 1), 0:slots] = fold(total_u)

    each_target(level, order, bounds, target)
    diagonal = COMPRESSION + 6.0 * acc[0].reshape(2, depth, 128)
    pulled = acc[1].reshape(2, depth, 128)
    out_diag[...] = diagonal
    below = column_update(left[4, 1] > 0.0, start_l[1], recv[2], pulled[0], diagonal[0])
    here = column_update(own[4, 0] > 0.0, start_o[0], source_own[0], pulled[1], diagonal[1])
    out_p[0] = below
    out_p[1] = here
    out_send[0] = below
    out_send[1] = here
    out_send[2] = weight_own[0]
    out_send[3] = diagonal[0]


def sweep2_kernel(
    level, order, bounds, feat_r, feat_l, own, recv1, recv2, weight_own, source_own, diag, p1, posc,
    out_p, wide_u, acc,
):
    depth = weight_own.shape[1]
    wide_u[0:depth] = recv1[1] * p1[0]
    wide_u[depth : 2 * depth] = weight_own[0] * p1[1]
    wide_u[2 * depth : 3 * depth] = weight_own[1] * recv2[0]
    wide_u[3 * depth : 4 * depth] = recv2[2] * recv2[1]
    pulled = jacobi_sums(level, order, bounds, 1, feat_r, feat_l, posc, wide_u, acc, depth)
    out_p[0] = column_update(own[4, 0] > 0.0, p1[1], source_own[0], pulled[0], diag[1])
    out_p[1] = column_update(own[4, 1] > 0.0, recv2[0], source_own[1], pulled[1], recv2[3])


def sweep3_kernel(
    level, order, bounds, feat_r, feat_l, left, own, recv1, recv3, weight_own, source_own, diag, p2, posc,
    out_p, wide_u, acc,
):
    depth = weight_own.shape[1]
    wide_u[0 : 2 * depth] = (recv1[0:2] * recv3[...]).reshape(2 * depth, 128)
    wide_u[2 * depth : 4 * depth] = (weight_own[...] * p2[...]).reshape(2 * depth, 128)
    pulled = jacobi_sums(level, order, bounds, 0, feat_r, feat_l, posc, wide_u, acc, depth)
    out_p[0] = column_update(left[4, 1] > 0.0, recv3[1], recv1[2], pulled[0], diag[0])
    out_p[1] = column_update(own[4, 0] > 0.0, p2[0], source_own[0], pulled[1], diag[1])


def force_kernel(
    level, order, bounds, feat_r, feat_l, own, recv1, recv2, recv4, left, right, weight_own, p3, posc,
    out_pressure, out_acc, out_velocity, out_offsets,
    wide_p, wide_w, wide_x, wide_z, pres_r, pres_l, stage, acc,
):
    depth = weight_own.shape[1]
    wide_p[0:2] = p3[...]
    wide_p[2:4] = recv4[...]
    wide_w[0] = recv1[1]
    wide_w[1:3] = weight_own[...]
    wide_w[3] = recv2[2]
    for field, wide in ((0, wide_x), (1, wide_z)):
        wide[0:depth] = left[field, 1] - 0.5
        wide[depth : 3 * depth] = own[field].reshape(2 * depth, 128) - 0.5
        wide[3 * depth : 4 * depth] = right[field, 0] - 0.5

    def prepare(group, carry):
        rows = pl.ds(pl.multiple_of(group * 8, 8), 8)
        for col in range(4):
            pressure, weight = wide_p[col, rows, :], wide_w[col, rows, :]
            target, source = pressure_rows(weight, weight * pressure, pressure)
            store_rows(source, stage, pres_r, pl.multiple_of(col * depth + group * 8, 8))
            if 1 <= col <= 2:
                store_rows(target, stage, pres_l, pl.multiple_of((col - 1) * depth + group * 8, 8))
        return carry

    lax.fori_loop(0, depth // 8, prepare, 0)

    def target(cell, slots):
        sign = 9 * (cell >= depth).astype(jnp.int32)
        pos_l, pres_l_t = upright(feat_l[cell + depth], slots), upright(pres_l[cell], slots)
        plain = jnp.zeros((slots, 128), F32)
        by_x = jnp.zeros((slots, 128), F32)
        by_z = jnp.zeros((slots, 128), F32)
        for sx in range(3):
            source = cell + sx * depth
            reach = tiles(pos_l, signed(feat_r, source + depth, posc, sign + 3 * sx))
            lift = tiles(pres_l_t, [pres_r[source + sz] for sz in (-1, 0, 1)])
            for sz in range(3):
                s = jnp.maximum(reach[sz], 0.0)
                g = s * s * lift[sz]
                at = pl.ds(source + sz - 1, 1)
                plain = plain + g
                by_x = by_x + g * (wide_x[at, :] + float(sx - 1))
                by_z = by_z + g * (wide_z[at, :] + float(sz - 1))
        acc[0, pl.ds(cell, 1), 0:slots] = fold(plain)
        acc[1, pl.ds(cell, 1), 0:slots] = fold(by_x)
        acc[2, pl.ds(cell, 1), 0:slots] = fold(by_z)

    acc[...] = jnp.zeros_like(acc)
    each_target(level, order, bounds, target)
    sums = acc[...].reshape(3, 2, depth, 128)
    inner = slice(HALO, depth - HALO)
    alive = own[4, :, inner] > 0.0
    out_pressure[0] = p3[1, inner]
    out_pressure[1] = recv4[0, inner]
    for axis, wide, pull in ((0, wide_x, 0.0), (1, wide_z, GRAVITY)):
        here = wide[depth : 3 * depth].reshape(2, depth, 128)
        force = 6.0 * (here[:, inner] * sums[0, :, inner] - sums[axis + 1, :, inner])
        force = jnp.where(alive, force, 0.0)
        velocity = jnp.where(alive, own[axis + 2, :, inner] + TIME_STEP * (force - pull), 0.0)
        out_acc[axis] = force
        out_velocity[axis] = velocity
        out_offsets[axis] = jnp.where(alive, own[axis, :, inner] + TIME_STEP * velocity, 0.0)


def target_lists(count, cells):
    depth = count.shape[1]
    number = jnp.arange(2 * depth, dtype=jnp.int32)
    kinds = []
    for level in range(1, ITERS + 3):
        window = count[1:3] if level % 2 else count[0:2]
        kind = sum((window > slots).astype(jnp.int32) for slots, _ in CLASSES[:-1])
        reach = ITERS + 2 - level
        row = jnp.arange(depth, dtype=jnp.int32)[None]
        kind = jnp.where((row >= HALO - reach) & (row < HALO + cells + reach), kind, len(CLASSES))
        kinds.append(kind.reshape(-1))
    kinds = jnp.stack(kinds)
    key = kinds * (2 * depth) + number
    rank = jnp.sum((key[:, None, :] < key[:, :, None]).astype(jnp.int32), 2)
    bounds = jnp.stack([jnp.sum((kinds < c).astype(jnp.int32), 1) for c in range(len(CLASSES) + 1)], 1)
    place = jnp.arange(2 * depth + max(c for _, c in CLASSES), dtype=jnp.int32)
    order = jnp.sum(jnp.where(rank[:, None, :] == place[None, :, None], number, 0), 2)
    return jnp.where(place < bounds[:, -1:], order, HALO), bounds


def local_call(kernel, out_shapes, scratch, order, bounds, *operands):
    vmem = pl.BlockSpec(memory_space=pltpu.VMEM)
    smem = pl.BlockSpec(memory_space=pltpu.SMEM)
    return pl.pallas_call(
        kernel,
        out_shape=[jax.ShapeDtypeStruct(shape, dtype) for shape, dtype in out_shapes],
        in_specs=[smem] * 2 + [vmem] * len(operands),
        out_specs=[vmem] * len(out_shapes),
        scratch_shapes=[pltpu.VMEM(shape, dtype) for shape, dtype in scratch],
        compiler_params=pltpu.CompilerParams(vmem_limit_bytes=VMEM_LIMIT),
    )(order, bounds, *operands)


def from_behind(block, axis, distance):
    devices = range(lax.axis_size(axis))
    route = [(i - distance, i) for i in devices if i - distance in devices]
    return lax.ppermute(block, axis, route)


def around(block, axis, distance):
    peers = lax.axis_size(axis)
    return lax.ppermute(block, axis, [(i, (i + distance) % peers) for i in range(peers)])


def per_device(
    offsets, velocity, particle_mass, pressure_start, counts, leaving_slot, leaving_count, leaving_side
):
    cells, slots = counts.shape[1], offsets.shape[-1]
    alive = jnp.arange(slots, dtype=jnp.int32)[None, None, :] < counts[:, :, None]
    live_mass = jnp.where(alive, particle_mass, 0.0)
    base = jnp.concatenate([offsets, velocity, live_mass[None], pressure_start[None]], 0)
    above = from_behind(base[:, :, cells - HALO :], "slab", 1)
    below = from_behind(base[:, :, :HALO], "slab", -1)
    own = jnp.concatenate([above, base, below], 2)
    left = around(own, "col", 1)
    right = around(own[:5, :1], "col", -1)
    depth = cells + 2 * HALO
    first = lax.axis_index("col") == 0
    last = lax.axis_index("col") == lax.axis_size("col") - 1
    here = position_table((first, -1), (last, 1))
    back = position_table((first, 1), (first, -1))
    velc = sign_table(velocity_signs)
    plane = (2, depth, slots)

    live = jnp.stack([left[4, 1], own[4, 0], own[4, 1]]) > 0.0
    lists = target_lists(jnp.sum(live.astype(jnp.int32), -1), cells)
    long = (4 * depth, slots)
    sums = (2 * depth, slots)

    feat_r, feat_l, weight, density_ratio, source, send1 = local_call(
        functools.partial(density_kernel, 0),
        [
            ((5 * depth, KP, slots), BF16),
            ((3 * depth, KP, slots), BF16),
            (plane, F32),
            (plane, F32),
            (plane, F32),
            ((3, depth, slots), F32),
        ],
        [
            ((8 * KP, slots), F32),
            ((8 * KD, slots), F32),
            ((4 * depth, KD, slots), BF16),
            ((2 * depth, KD, slots), BF16),
            (long, F32),
            ((2, *sums), F32),
        ],
        *lists, left, own, right, here, velc,
    )
    recv1 = around(send1, "col", 1)
    p1, diag, send2 = local_call(
        functools.partial(sweep1_kernel, 1),
        [(plane, F32), (plane, F32), ((4, depth, slots), F32)],
        [(long, F32), (long, F32), ((2, *sums), F32)],
        *lists, feat_r, feat_l, left, own, recv1, weight, source, back,
    )
    recv2 = around(send2, "col", -1)
    (p2,) = local_call(
        functools.partial(sweep2_kernel, 2),
        [(plane, F32)],
        [(long, F32), (sums, F32)],
        *lists, feat_r, feat_l, own, recv1, recv2, weight, source, diag, p1, here,
    )
    recv3 = around(p2, "col", 1)
    (p3,) = local_call(
        functools.partial(sweep3_kernel, 3),
        [(plane, F32)],
        [(long, F32), (sums, F32)],
        *lists, feat_r, feat_l, left, own, recv1, recv3, weight, source, diag, p2, back,
    )
    recv4 = around(p3, "col", -1)
    inner = (2, cells, slots)
    pressure, acceleration, velocity_new, offsets_new = local_call(
        functools.partial(force_kernel, 4),
        [(inner, F32), ((2, *inner), F32), ((2, *inner), F32), ((2, *inner), F32)],
        [((4, depth, slots), F32)] * 2
        + [(long, F32)] * 2
        + [
            ((4 * depth, KE, slots), BF16),
            ((2 * depth, KE, slots), BF16),
            ((8 * KE, slots), F32),
            ((3, *sums), F32),
        ],
        *lists, feat_r, feat_l, own, recv1, recv2, recv4, left, right, weight, p3, here,
    )
    density_ratio = density_ratio[:, HALO : HALO + cells]
    state = jnp.concatenate([offsets_new, velocity_new, pressure[None], live_mass[None]], 0).reshape(6, -1)
    block_rows = leaving_slot.shape[0]
    blocks = state[:, leaving_slot.reshape(-1)].reshape(6, block_rows, 1, slots)
    filled = jnp.arange(slots, dtype=jnp.int32)[None, None, :] < leaving_count[:, :, None]
    upward = jnp.where(filled & (leaving_side[:, :, None] == 1), blocks, 0.0)
    downward = jnp.where(filled & (leaving_side[:, :, None] == 0), blocks, 0.0)
    arrived = jnp.stack([from_behind(upward, "col", 1), from_behind(downward, "col", -1)])
    return (density_ratio, pressure, acceleration, velocity_new, offsets_new, arrived)


def solution(mesh):
    return jax.shard_map(
        per_device,
        mesh=mesh,
        in_specs=(
            P(None, "col", "slab", None),
            P(None, "col", "slab", None),
            P("col", "slab", None),
            P("col", "slab", None),
            P("col", "slab"),
            P("col", "slab", None),
            P("col", "slab"),
            P("col", "slab"),
        ),
        out_specs=(
            P("col", "slab", None),
            P("col", "slab", None),
            P(None, "col", "slab", None),
            P(None, "col", "slab", None),
            P(None, "col", "slab", None),
            P(None, None, "col", "slab", None),
        ),
        check_vma=False,
    )
```

```python
import functools

import jax
import jax.numpy as jnp
import numpy as np
from jax import lax
from jax.experimental import pallas as pl
from jax.experimental.pallas import tpu as pltpu
from jax.sharding import PartitionSpec as P

ITERS = 3
TIME_STEP = 0.1
REST_DENSITY = 50.0
COMPRESSION = 2.0
RELAXATION = 0.5
GRAVITY = 1.0

HALO = 8
CLASSES = ((32, 16), (64, 8), (96, 6), (128, 6))
CHUNKS = ((0, 1), (2, 3), (4, 5), (6, 7), (8,))
AHEAD = 2
KP = 32
KD = 48
KE = 16
FAR = -64.0
SHIFTS = [(sx, sz) for sx in (-1, 0, 1) for sz in (-1, 0, 1)]
F32 = jnp.float32
BF16 = jnp.bfloat16
VMEM_LIMIT = 56 * 1024 * 1024


def split3(value):
    high = value.astype(BF16).astype(F32)
    rest = value - high
    mid = rest.astype(BF16).astype(F32)
    return [high, mid, rest - mid]


def left_six(parts):
    h, m, l = parts
    return [h, h, h, m, m, l]


def right_six(parts):
    h, m, l = parts
    return [h, m, l, h, m, h]


def position_rows(x, z):
    one, zero = jnp.ones_like(x), jnp.zeros_like(x)
    x, z = x - 0.5, z - 0.5
    xs, zs = split3(x), split3(z)
    square = x * x + z * z
    x2, z2 = [2.0 * v for v in xs], [2.0 * v for v in zs]
    ones = [one] * 3
    target = (
        left_six(x2) + x2 + ones + left_six(z2) + z2 + ones + split3(1.0 - square) + ones + [one, zero]
    )
    source = (
        right_six(xs) + ones + x2 + right_six(zs) + ones + z2 + ones + split3(-square) + [one, zero]
    )
    return target, source


def position_signs(sx, sz):
    return [1] * 6 + [sx] * 3 + [-sx] * 3 + [1] * 6 + [sz] * 3 + [-sz] * 3 + [1] * 6 + [-(sx * sx + sz * sz), 0]


def velocity_rows(x, z, vx, vz):
    one, zero = jnp.ones_like(x), jnp.zeros_like(x)
    x, z = x - 0.5, z - 0.5
    xs, zs, vxs, vzs = split3(x), split3(z), split3(vx), split3(vz)
    dots = split3(vx * x + vz * z)
    ones = [one] * 3
    pad = [zero] * 6
    minus = lambda rows: [-v for v in rows]
    target = dots + left_six(vxs) + left_six(vzs) + left_six(xs) + left_six(zs) + ones + vxs + vzs + ones + ones + pad
    source = (
        ones
        + minus(right_six(xs) + right_six(zs) + right_six(vxs) + right_six(vzs))
        + dots
        + ones
        + ones
        + vxs
        + vzs
        + pad
    )
    return target, source


def velocity_signs(sx, sz):
    return [1] * 30 + [-sx] * 3 + [-sz] * 3 + [sx] * 3 + [sz] * 3 + [0] * 6


def pressure_rows(weight, lifted, pressure):
    one, zero = jnp.ones_like(weight), jnp.zeros_like(weight)
    pad = [zero] * 7
    target = [one] * 3 + left_six(split3(pressure)) + pad
    source = split3(lifted) + [-v for v in right_six(split3(weight))] + pad
    return target, source


def sign_table(signs):
    table = np.asarray([signs(sx, sz) for sx, sz in SHIFTS], np.float32)
    return jnp.broadcast_to(jnp.asarray(table)[:, :, None], (*table.shape, 128)).astype(BF16)


def position_table(cut_first, cut_second):
    table = np.asarray([position_signs(sx, sz) for sx, sz in SHIFTS] * 2, np.float32)
    constant = np.arange(KP) == KP - 2
    sides = np.asarray([sx for sx, _ in SHIFTS] * 2)
    target = np.repeat([0, 1], 9)
    spots = lambda t, side: jnp.asarray(((target == t) & (sides == side))[:, None] & constant)
    table = jnp.where(spots(0, cut_first[1]) & cut_first[0], FAR, jnp.asarray(table))
    table = jnp.where(spots(1, cut_second[1]) & cut_second[0], FAR, table)
    return jnp.broadcast_to(table[:, :, None], (18, KP, 128)).astype(BF16)


def store_rows(rows, stage, dest, cell):
    count = len(rows)
    for index, value in enumerate(rows):
        stage[pl.ds(index, 8, stride=count), :] = value
    dest[pl.ds(cell, 8)] = stage[...].reshape(8, count, 128).astype(BF16)


def upright(rows, slots):
    return rows.astype(F32).T[:slots].astype(BF16)


def sources_of(feat, cell, depth, chunk, table=None, first=0):
    parts = []
    for n in chunk:
        part = feat[cell + (n // 3) * depth + n % 3 - 1]
        parts.append(part if table is None else part * table[first + n])
    return jnp.concatenate(parts, axis=1) if len(parts) > 1 else parts[0]


def product(left, right):
    return jnp.dot(left, right, preferred_element_type=F32)


def fold(total):
    return jnp.sum(total.T, axis=0, keepdims=True)


def each_target(level, order, bounds, target):
    for index, (slots, cells) in enumerate(CLASSES):
        start = bounds[level, index]
        steps = (bounds[level, index + 1] - start + cells - 1) // cells

        def step(i, carry, slots=slots, cells=cells, start=start):
            waiting = []
            for u in range(cells):
                issue, consume, finish = target(order[level, start + i * cells + u], slots)
                for chunk in CHUNKS:
                    waiting.append((consume, chunk, issue(chunk), finish))
                    if len(waiting) > AHEAD:
                        take(waiting.pop(0))
            for entry in waiting:
                take(entry)
            return carry

        lax.fori_loop(0, steps, step, 0)


def take(entry):
    consume, chunk, products, finish = entry
    consume(chunk, products)
    if chunk is CHUNKS[-1]:
        finish()


def density_kernel(
    level, order, bounds, left, own, right, posc, velc,
    out_r, out_l, out_w, out_density, out_source, out_send,
    stage_p, stage_d, vel_r, vel_l, wide_m, acc,
):
    depth = own.shape[2]
    groups = depth // 8
    blocks = [(left, 0), (left, 1), (own, 0), (own, 1), (right, 0)]

    def prepare(group, carry):
        rows = pl.ds(pl.multiple_of(group * 8, 8), 8)
        for col, (ref, at) in enumerate(blocks):
            x, z, vx, vz = (ref[f, at, rows, :] for f in range(4))
            cell = pl.multiple_of(col * depth + group * 8, 8)
            target, source = position_rows(x, z)
            store_rows(source, stage_p, out_r, cell)
            if 1 <= col <= 3:
                store_rows(target, stage_p, out_l, pl.multiple_of((col - 1) * depth + group * 8, 8))
            if col >= 1:
                target, source = velocity_rows(x, z, vx, vz)
                store_rows(source, stage_d, vel_r, pl.multiple_of((col - 1) * depth + group * 8, 8))
                if 2 <= col <= 3:
                    store_rows(target, stage_d, vel_l, pl.multiple_of((col - 2) * depth + group * 8, 8))
        return carry

    lax.fori_loop(0, groups, prepare, 0)
    acc[...] = jnp.zeros_like(acc)

    wide_m[0:depth] = left[4, 1]
    wide_m[depth : 2 * depth] = own[4, 0]
    wide_m[2 * depth : 3 * depth] = own[4, 1]
    wide_m[3 * depth : 4 * depth] = right[4, 0]

    def target(cell, slots):
        sign = 9 * (cell >= depth).astype(jnp.int32)
        pos_l, vel_l_t = upright(out_l[cell + depth], slots), upright(vel_l[cell], slots)
        sums = [jnp.zeros((slots, 128), F32)] * 2

        def issue(chunk):
            return (
                product(pos_l, sources_of(out_r, cell + depth, depth, chunk, posc, sign)),
                product(vel_l_t, sources_of(vel_r, cell, depth, chunk, velc)),
            )

        def consume(chunk, products):
            for i, n in enumerate(chunk):
                lanes = slice(128 * i, 128 * (i + 1))
                s = jnp.maximum(products[0][:, lanes], 0.0)
                q = s * s * wide_m[pl.ds(cell + (n // 3) * depth + n % 3 - 1, 1), :]
                sums[0] = sums[0] + q * s
                sums[1] = sums[1] + q * products[1][:, lanes]

        def finish():
            for i in range(2):
                acc[i, pl.ds(cell, 1), 0:slots] = fold(sums[i])

        return issue, consume, finish

    each_target(level, order, bounds, target)
    density = acc[0].reshape(2, depth, 128)
    div = -6.0 * acc[1].reshape(2, depth, 128)
    mass = own[4]
    alive = mass > 0.0
    density = jnp.where(alive, density, 0.0)
    weight = jnp.where(alive, mass / jnp.where(alive, density, 1.0), 0.0)
    source = jnp.where(
        alive, (density + TIME_STEP * div - REST_DENSITY) / REST_DENSITY, 0.0
    )
    out_w[...] = weight
    out_density[...] = density / REST_DENSITY
    out_source[...] = source
    out_send[0:2] = weight
    out_send[2] = source[1]


def column_update(alive, pressure, source, pulled, diagonal):
    updated = (1.0 - RELAXATION) * pressure + RELAXATION * (source + 6.0 * pulled) / diagonal
    return jnp.where(alive, updated, 0.0)


def jacobi_sums(level, order, bounds, first_col, feat_r, feat_l, posc, wide_u, acc, depth):
    def target(cell, slots):
        sign = 9 * (cell >= depth).astype(jnp.int32)
        at = cell + first_col * depth
        pos_l = upright(feat_l[at], slots)
        sums = [jnp.zeros((slots, 128), F32)]

        def issue(chunk):
            return product(pos_l, sources_of(feat_r, at, depth, chunk, posc, sign))

        def consume(chunk, products):
            for i, n in enumerate(chunk):
                s = jnp.maximum(products[:, 128 * i : 128 * (i + 1)], 0.0)
                lifted = wide_u[pl.ds(cell + (n // 3) * depth + n % 3 - 1, 1), :]
                sums[0] = sums[0] + s * s * lifted

        def finish():
            acc[pl.ds(cell, 1), 0:slots] = fold(sums[0])

        return issue, consume, finish

    acc[...] = jnp.zeros_like(acc)
    each_target(level, order, bounds, target)
    return acc[...].reshape(2, depth, 128)


def sweep1_kernel(
    level, order, bounds, feat_r, feat_l, left, own, recv, weight_own, source_own, posc,
    out_p, out_diag, out_send, wide_w, wide_u, acc,
):
    depth = weight_own.shape[1]
    start_l = jnp.where(left[4] > 0.0, left[5], 0.0)
    start_o = jnp.where(own[4] > 0.0, own[5], 0.0)
    for col in range(4):
        rows = slice(col * depth, (col + 1) * depth)
        weight = recv[col] if col < 2 else weight_own[col - 2]
        wide_w[rows] = weight
        wide_u[rows] = weight * (start_l if col < 2 else start_o)[col % 2]
    acc[...] = jnp.zeros_like(acc)

    def target(cell, slots):
        sign = 9 * (cell >= depth).astype(jnp.int32)
        pos_l = upright(feat_l[cell], slots)
        sums = [jnp.zeros((slots, 128), F32)] * 2

        def issue(chunk):
            return product(pos_l, sources_of(feat_r, cell, depth, chunk, posc, sign))

        def consume(chunk, products):
            for i, n in enumerate(chunk):
                s = jnp.maximum(products[:, 128 * i : 128 * (i + 1)], 0.0)
                q = s * s
                at = pl.ds(cell + (n // 3) * depth + n % 3 - 1, 1)
                sums[0] = sums[0] + q * wide_w[at, :]
                sums[1] = sums[1] + q * wide_u[at, :]

        def finish():
            for i in range(2):
                acc[i, pl.ds(cell, 1), 0:slots] = fold(sums[i])

        return issue, consume, finish

    each_target(level, order, bounds, target)
    diagonal = COMPRESSION + 6.0 * acc[0].reshape(2, depth, 128)
    pulled = acc[1].reshape(2, depth, 128)
    out_diag[...] = diagonal
    below = column_update(left[4, 1] > 0.0, start_l[1], recv[2], pulled[0], diagonal[0])
    here = column_update(own[4, 0] > 0.0, start_o[0], source_own[0], pulled[1], diagonal[1])
    out_p[0] = below
    out_p[1] = here
    out_send[0] = below
    out_send[1] = here
    out_send[2] = weight_own[0]
    out_send[3] = diagonal[0]


def sweep2_kernel(
    level, order, bounds, feat_r, feat_l, own, recv1, recv2, weight_own, source_own, diag, p1, posc,
    out_p, wide_u, acc,
):
    depth = weight_own.shape[1]
    wide_u[0:depth] = recv1[1] * p1[0]
    wide_u[depth : 2 * depth] = weight_own[0] * p1[1]
    wide_u[2 * depth : 3 * depth] = weight_own[1] * recv2[0]
    wide_u[3 * depth : 4 * depth] = recv2[2] * recv2[1]
    pulled = jacobi_sums(level, order, bounds, 1, feat_r, feat_l, posc, wide_u, acc, depth)
    out_p[0] = column_update(own[4, 0] > 0.0, p1[1], source_own[0], pulled[0], diag[1])
    out_p[1] = column_update(own[4, 1] > 0.0, recv2[0], source_own[1], pulled[1], recv2[3])


def sweep3_kernel(
    level, order, bounds, feat_r, feat_l, left, own, recv1, recv3, weight_own, source_own, diag, p2, posc,
    out_p, wide_u, acc,
):
    depth = weight_own.shape[1]
    wide_u[0 : 2 * depth] = (recv1[0:2] * recv3[...]).reshape(2 * depth, 128)
    wide_u[2 * depth : 4 * depth] = (weight_own[...] * p2[...]).reshape(2 * depth, 128)
    pulled = jacobi_sums(level, order, bounds, 0, feat_r, feat_l, posc, wide_u, acc, depth)
    out_p[0] = column_update(left[4, 1] > 0.0, recv3[1], recv1[2], pulled[0], diag[0])
    out_p[1] = column_update(own[4, 0] > 0.0, p2[0], source_own[0], pulled[1], diag[1])


def force_kernel(
    level, order, bounds, feat_r, feat_l, own, recv1, recv2, recv4, left, right, weight_own, p3, posc,
    out_pressure, out_acc, out_velocity, out_offsets,
    wide_p, wide_w, wide_x, wide_z, pres_r, pres_l, stage, acc,
):
    depth = weight_own.shape[1]
    wide_p[0:2] = p3[...]
    wide_p[2:4] = recv4[...]
    wide_w[0] = recv1[1]
    wide_w[1:3] = weight_own[...]
    wide_w[3] = recv2[2]
    for field, wide in ((0, wide_x), (1, wide_z)):
        wide[0:depth] = left[field, 1] - 0.5
        wide[depth : 3 * depth] = own[field].reshape(2 * depth, 128) - 0.5
        wide[3 * depth : 4 * depth] = right[field, 0] - 0.5

    def prepare(group, carry):
        rows = pl.ds(pl.multiple_of(group * 8, 8), 8)
        for col in range(4):
            pressure, weight = wide_p[col, rows, :], wide_w[col, rows, :]
            target, source = pressure_rows(weight, weight * pressure, pressure)
            store_rows(source, stage, pres_r, pl.multiple_of(col * depth + group * 8, 8))
            if 1 <= col <= 2:
                store_rows(target, stage, pres_l, pl.multiple_of((col - 1) * depth + group * 8, 8))
        return carry

    lax.fori_loop(0, depth // 8, prepare, 0)

    def target(cell, slots):
        sign = 9 * (cell >= depth).astype(jnp.int32)
        pos_l, pres_l_t = upright(feat_l[cell + depth], slots), upright(pres_l[cell], slots)
        sums = [jnp.zeros((slots, 128), F32)] * 3

        def issue(chunk):
            return (
                product(pos_l, sources_of(feat_r, cell + depth, depth, chunk, posc, sign)),
                product(pres_l_t, sources_of(pres_r, cell, depth, chunk)),
            )

        def consume(chunk, products):
            for i, n in enumerate(chunk):
                lanes = slice(128 * i, 128 * (i + 1))
                s = jnp.maximum(products[0][:, lanes], 0.0)
                g = s * s * products[1][:, lanes]
                at = pl.ds(cell + (n // 3) * depth + n % 3 - 1, 1)
                sums[0] = sums[0] + g
                sums[1] = sums[1] + g * (wide_x[at, :] + float(n // 3 - 1))
                sums[2] = sums[2] + g * (wide_z[at, :] + float(n % 3 - 1))

        def finish():
            for i in range(3):
                acc[i, pl.ds(cell, 1), 0:slots] = fold(sums[i])

        return issue, consume, finish

    acc[...] = jnp.zeros_like(acc)
    each_target(level, order, bounds, target)
    sums = acc[...].reshape(3, 2, depth, 128)
    inner = slice(HALO, depth - HALO)
    alive = own[4, :, inner] > 0.0
    out_pressure[0] = p3[1, inner]
    out_pressure[1] = recv4[0, inner]
    for axis, wide, pull in ((0, wide_x, 0.0), (1, wide_z, GRAVITY)):
        here = wide[depth : 3 * depth].reshape(2, depth, 128)
        force = 6.0 * (here[:, inner] * sums[0, :, inner] - sums[axis + 1, :, inner])
        force = jnp.where(alive, force, 0.0)
        velocity = jnp.where(alive, own[axis + 2, :, inner] + TIME_STEP * (force - pull), 0.0)
        out_acc[axis] = force
        out_velocity[axis] = velocity
        out_offsets[axis] = jnp.where(alive, own[axis, :, inner] + TIME_STEP * velocity, 0.0)


def leaving_kernel(
    slot, count, side, offsets, velocity, pressure, mass, out_up, out_down, hot
):
    blocks, slots = slot.shape
    fields = [offsets[0], offsets[1], velocity[0], velocity[1], pressure[...], mass[...]]
    fields = [f.reshape(-1, slots) for f in fields]
    cells = fields[0].shape[0]
    number = lax.broadcasted_iota(jnp.int32, (cells, slots), 0)
    place = lax.broadcasted_iota(jnp.int32, (slots, slots), 0)
    for b in range(blocks):
        one_hot = (number == slot[b : b + 1, :] // slots).astype(F32).astype(BF16)
        for part in range(3):
            hot[part * cells : (part + 1) * cells, b * slots : (b + 1) * slots] = one_hot
    filled = lax.broadcasted_iota(jnp.int32, (blocks, slots), 1) < count[...]
    up = side[...] == 1
    for index, field in enumerate(fields):
        parts = jnp.concatenate([v.astype(BF16) for v in split3(field.T)], axis=1)
        rows = []
        for b in range(blocks):
            picked = product(parts, hot[:, b * slots : (b + 1) * slots])
            here = place == slot[b : b + 1, :] % slots
            rows.append(jnp.sum(jnp.where(here, picked, 0.0), axis=0, keepdims=True))
        block = jnp.where(filled, jnp.concatenate(rows, axis=0), 0.0)
        out_up[index] = jnp.where(up, block, 0.0)
        out_down[index] = jnp.where(up, 0.0, block)


def target_lists(count, cells):
    depth = count.shape[1]
    number = jnp.arange(2 * depth, dtype=jnp.int32)
    kinds = []
    for level in range(1, ITERS + 3):
        window = count[1:3] if level % 2 else count[0:2]
        kind = sum((window > slots).astype(jnp.int32) for slots, _ in CLASSES[:-1])
        reach = ITERS + 2 - level
        row = jnp.arange(depth, dtype=jnp.int32)[None]
        kind = jnp.where((row >= HALO - reach) & (row < HALO + cells + reach), kind, len(CLASSES))
        kinds.append(kind.reshape(-1))
    kinds = jnp.stack(kinds)
    key = kinds * (2 * depth) + number
    rank = jnp.sum((key[:, None, :] < key[:, :, None]).astype(jnp.int32), 2)
    bounds = jnp.stack([jnp.sum((kinds < c).astype(jnp.int32), 1) for c in range(len(CLASSES) + 1)], 1)
    place = jnp.arange(2 * depth + max(c for _, c in CLASSES), dtype=jnp.int32)
    order = jnp.sum(jnp.where(rank[:, None, :] == place[None, :, None], number, 0), 2)
    return jnp.where(place < bounds[:, -1:], order, HALO), bounds


def local_call(kernel, out_shapes, scratch, scalars, *operands):
    vmem = pl.BlockSpec(memory_space=pltpu.VMEM)
    smem = pl.BlockSpec(memory_space=pltpu.SMEM)
    return pl.pallas_call(
        kernel,
        out_shape=[jax.ShapeDtypeStruct(shape, dtype) for shape, dtype in out_shapes],
        in_specs=[smem] * len(scalars) + [vmem] * len(operands),
        out_specs=[vmem] * len(out_shapes),
        scratch_shapes=[pltpu.VMEM(shape, dtype) for shape, dtype in scratch],
        compiler_params=pltpu.CompilerParams(vmem_limit_bytes=VMEM_LIMIT),
    )(*scalars, *operands)


def from_behind(block, axis, distance):
    devices = range(lax.axis_size(axis))
    route = [(i - distance, i) for i in devices if i - distance in devices]
    return lax.ppermute(block, axis, route)


def around(block, axis, distance):
    peers = lax.axis_size(axis)
    return lax.ppermute(block, axis, [(i, (i + distance) % peers) for i in range(peers)])


def per_device(
    offsets, velocity, particle_mass, pressure_start, counts, leaving_slot, leaving_count, leaving_side
):
    cells, slots = counts.shape[1], offsets.shape[-1]
    alive = jnp.arange(slots, dtype=jnp.int32)[None, None, :] < counts[:, :, None]
    live_mass = jnp.where(alive, particle_mass, 0.0)
    base = jnp.concatenate([offsets, velocity, live_mass[None], pressure_start[None]], 0)
    above = from_behind(base[:, :, cells - HALO :], "slab", 1)
    below = from_behind(base[:, :, :HALO], "slab", -1)
    own = jnp.concatenate([above, base, below], 2)
    left = around(own, "col", 1)
    right = around(own[:5, :1], "col", -1)
    depth = cells + 2 * HALO
    first = lax.axis_index("col") == 0
    last = lax.axis_index("col") == lax.axis_size("col") - 1
    here = position_table((first, -1), (last, 1))
    back = position_table((first, 1), (first, -1))
    velc = sign_table(velocity_signs)
    plane = (2, depth, slots)

    live = jnp.stack([left[4, 1], own[4, 0], own[4, 1]]) > 0.0
    lists = target_lists(jnp.sum(live.astype(jnp.int32), -1), cells)
    long = (4 * depth, slots)
    sums = (2 * depth, slots)

    feat_r, feat_l, weight, density_ratio, source, send1 = local_call(
        functools.partial(density_kernel, 0),
        [
            ((5 * depth, KP, slots), BF16),
            ((3 * depth, KP, slots), BF16),
            (plane, F32),
            (plane, F32),
            (plane, F32),
            ((3, depth, slots), F32),
        ],
        [
            ((8 * KP, slots), F32),
            ((8 * KD, slots), F32),
            ((4 * depth, KD, slots), BF16),
            ((2 * depth, KD, slots), BF16),
            (long, F32),
            ((2, *sums), F32),
        ],
        lists, left, own, right, here, velc,
    )
    recv1 = around(send1, "col", 1)
    p1, diag, send2 = local_call(
        functools.partial(sweep1_kernel, 1),
        [(plane, F32), (plane, F32), ((4, depth, slots), F32)],
        [(long, F32), (long, F32), ((2, *sums), F32)],
        lists, feat_r, feat_l, left, own, recv1, weight, source, back,
    )
    recv2 = around(send2, "col", -1)
    (p2,) = local_call(
        functools.partial(sweep2_kernel, 2),
        [(plane, F32)],
        [(long, F32), (sums, F32)],
        lists, feat_r, feat_l, own, recv1, recv2, weight, source, diag, p1, here,
    )
    recv3 = around(p2, "col", 1)
    (p3,) = local_call(
        functools.partial(sweep3_kernel, 3),
        [(plane, F32)],
        [(long, F32), (sums, F32)],
        lists, feat_r, feat_l, left, own, recv1, recv3, weight, source, diag, p2, back,
    )
    recv4 = around(p3, "col", -1)
    inner = (2, cells, slots)
    pressure, acceleration, velocity_new, offsets_new = local_call(
        functools.partial(force_kernel, 4),
        [(inner, F32), ((2, *inner), F32), ((2, *inner), F32), ((2, *inner), F32)],
        [((4, depth, slots), F32)] * 2
        + [(long, F32)] * 2
        + [
            ((4 * depth, KE, slots), BF16),
            ((2 * depth, KE, slots), BF16),
            ((8 * KE, slots), F32),
            ((3, *sums), F32),
        ],
        lists, feat_r, feat_l, own, recv1, recv2, recv4, left, right, weight, p3, here,
    )
    density_ratio = density_ratio[:, HALO : HALO + cells]
    blocks = leaving_slot.shape[0]
    packed = ((6, blocks, slots), F32)
    upward, downward = local_call(
        leaving_kernel,
        [packed, packed],
        [((3 * counts.size, blocks * slots), BF16)],
        (),
        leaving_slot[:, 0], leaving_count, leaving_side, offsets_new, velocity_new, pressure, live_mass,
    )
    arrived = jnp.stack([from_behind(upward, "col", 1), from_behind(downward, "col", -1)])[:, :, :, None]
    return (density_ratio, pressure, acceleration, velocity_new, offsets_new, arrived)


def solution(mesh):
    return jax.shard_map(
        per_device,
        mesh=mesh,
        in_specs=(
            P(None, "col", "slab", None),
            P(None, "col", "slab", None),
            P("col", "slab", None),
            P("col", "slab", None),
            P("col", "slab"),
            P("col", "slab", None),
            P("col", "slab"),
            P("col", "slab"),
        ),
        out_specs=(
            P("col", "slab", None),
            P("col", "slab", None),
            P(None, "col", "slab", None),
            P(None, "col", "slab", None),
            P(None, "col", "slab", None),
            P(None, None, "col", "slab", None),
        ),
        check_vma=False,
    )
```

```python
import functools

import jax
import jax.numpy as jnp
import numpy as np
from jax import lax
from jax.experimental import pallas as pl
from jax.experimental.pallas import tpu as pltpu
from jax.sharding import PartitionSpec as P

ITERS = 3
TIME_STEP = 0.1
REST_DENSITY = 50.0
COMPRESSION = 2.0
RELAXATION = 0.5
GRAVITY = 1.0

HALO = 8
CLASSES = ((32, 16), (64, 8), (96, 6), (128, 6))
CHUNKS = ((0, 1), (2, 3), (4, 5), (6, 7), (8,))
AHEAD = 2
KP = 32
KD = 48
KE = 16
FAR = -64.0
SHIFTS = [(sx, sz) for sx in (-1, 0, 1) for sz in (-1, 0, 1)]
F32 = jnp.float32
BF16 = jnp.bfloat16
VMEM_LIMIT = 56 * 1024 * 1024


def split3(value):
    high = value.astype(BF16).astype(F32)
    rest = value - high
    mid = rest.astype(BF16).astype(F32)
    return [high, mid, rest - mid]


def left_six(parts):
    h, m, l = parts
    return [h, h, h, m, m, l]


def right_six(parts):
    h, m, l = parts
    return [h, m, l, h, m, h]


def position_rows(x, z):
    one, zero = jnp.ones_like(x), jnp.zeros_like(x)
    x, z = x - 0.5, z - 0.5
    xs, zs = split3(x), split3(z)
    square = x * x + z * z
    x2, z2 = [2.0 * v for v in xs], [2.0 * v for v in zs]
    ones = [one] * 3
    target = (
        left_six(x2) + x2 + ones + left_six(z2) + z2 + ones + split3(1.0 - square) + ones + [one, zero]
    )
    source = (
        right_six(xs) + ones + x2 + right_six(zs) + ones + z2 + ones + split3(-square) + [one, zero]
    )
    return target, source


def position_signs(sx, sz):
    return [1] * 6 + [sx] * 3 + [-sx] * 3 + [1] * 6 + [sz] * 3 + [-sz] * 3 + [1] * 6 + [-(sx * sx + sz * sz), 0]


def velocity_rows(x, z, vx, vz):
    one, zero = jnp.ones_like(x), jnp.zeros_like(x)
    x, z = x - 0.5, z - 0.5
    xs, zs, vxs, vzs = split3(x), split3(z), split3(vx), split3(vz)
    dots = split3(vx * x + vz * z)
    ones = [one] * 3
    pad = [zero] * 6
    minus = lambda rows: [-v for v in rows]
    target = dots + left_six(vxs) + left_six(vzs) + left_six(xs) + left_six(zs) + ones + vxs + vzs + ones + ones + pad
    source = (
        ones
        + minus(right_six(xs) + right_six(zs) + right_six(vxs) + right_six(vzs))
        + dots
        + ones
        + ones
        + vxs
        + vzs
        + pad
    )
    return target, source


def velocity_signs(sx, sz):
    return [1] * 30 + [-sx] * 3 + [-sz] * 3 + [sx] * 3 + [sz] * 3 + [0] * 6


def pressure_rows(weight, lifted, pressure):
    one, zero = jnp.ones_like(weight), jnp.zeros_like(weight)
    pad = [zero] * 7
    target = [one] * 3 + left_six(split3(pressure)) + pad
    source = split3(lifted) + [-v for v in right_six(split3(weight))] + pad
    return target, source


def sign_table(signs):
    table = np.asarray([signs(sx, sz) for sx, sz in SHIFTS], np.float32)
    return jnp.broadcast_to(jnp.asarray(table)[:, :, None], (*table.shape, 128)).astype(BF16)


def position_table(cut_first, cut_second):
    table = np.asarray([position_signs(sx, sz) for sx, sz in SHIFTS] * 2, np.float32)
    constant = np.arange(KP) == KP - 2
    sides = np.asarray([sx for sx, _ in SHIFTS] * 2)
    target = np.repeat([0, 1], 9)
    spots = lambda t, side: jnp.asarray(((target == t) & (sides == side))[:, None] & constant)
    table = jnp.where(spots(0, cut_first[1]) & cut_first[0], FAR, jnp.asarray(table))
    table = jnp.where(spots(1, cut_second[1]) & cut_second[0], FAR, table)
    return jnp.broadcast_to(table[:, :, None], (18, KP, 128)).astype(BF16)


def store_rows(rows, stage, dest, cell):
    count = len(rows)
    for index, value in enumerate(rows):
        stage[pl.ds(index, 8, stride=count), :] = value
    dest[pl.ds(cell, 8)] = stage[...].reshape(8, count, 128).astype(BF16)


def upright(rows):
    rows = [r.astype(F32) for r in rows]
    spare = 128 - sum(r.shape[0] for r in rows)
    if spare:
        rows.append(jnp.zeros((spare, 128), F32))
    return jnp.concatenate(rows, axis=0).T.astype(BF16)


def sources_of(feat, cell, depth, chunk, offset, table=None, first=0):
    parts = []
    count = feat.shape[1]
    for n in chunk:
        part = feat[cell + (n // 3) * depth + n % 3 - 1]
        parts.append(part if table is None else part * table[first + n])
    part = jnp.concatenate(parts, axis=1) if len(parts) > 1 else parts[0]
    blank = lambda rows: [jnp.zeros((rows, part.shape[1]), BF16)] if rows else []
    return jnp.concatenate(blank(offset) + [part] + blank(128 - offset - count), axis=0)


def product(left, right):
    return jnp.dot(left, right, preferred_element_type=F32)


def fold(total):
    slots = total.shape[0]
    parts = jnp.concatenate([v.astype(BF16) for v in split3(total)], axis=1)
    spread = product(parts, jnp.ones((3 * 128, 128), BF16))
    here = lax.broadcasted_iota(jnp.int32, (slots, 128), 0) == lax.broadcasted_iota(
        jnp.int32, (slots, 128), 1
    )
    return jnp.sum(jnp.where(here, spread, 0.0), axis=0, keepdims=True)


def each_target(level, order, bounds, each, features, target):
    share = 128 // each
    for index, (slots, cells) in enumerate(CLASSES):
        start = bounds[level, index]
        steps = (bounds[level, index + 1] - start + cells - 1) // cells

        def step(i, carry, slots=slots, cells=cells, start=start):
            waiting = []
            for u in range(cells):
                if u % share == 0:
                    group = [order[level, start + i * cells + v] for v in range(u, min(u + share, cells))]
                    turned = upright([r for cell in group for r in features(cell)])[:slots]
                offset = (u % share) * each
                issue, consume, finish = target(group[u % share], slots, turned, offset)
                for chunk in CHUNKS:
                    waiting.append((consume, chunk, issue(chunk), finish))
                    if len(waiting) > AHEAD:
                        take(waiting.pop(0))
            for entry in waiting:
                take(entry)
            return carry

        lax.fori_loop(0, steps, step, 0)


def take(entry):
    consume, chunk, products, finish = entry
    consume(chunk, products)
    if chunk is CHUNKS[-1]:
        finish()


def density_kernel(
    level, order, bounds, left, own, right, posc, velc,
    out_r, out_l, out_w, out_density, out_source, out_send,
    stage_p, stage_d, vel_r, vel_l, wide_m, acc,
):
    depth = own.shape[2]
    groups = depth // 8
    blocks = [(left, 0), (left, 1), (own, 0), (own, 1), (right, 0)]

    def prepare(group, carry):
        rows = pl.ds(pl.multiple_of(group * 8, 8), 8)
        for col, (ref, at) in enumerate(blocks):
            x, z, vx, vz = (ref[f, at, rows, :] for f in range(4))
            cell = pl.multiple_of(col * depth + group * 8, 8)
            target, source = position_rows(x, z)
            store_rows(source, stage_p, out_r, cell)
            if 1 <= col <= 3:
                store_rows(target, stage_p, out_l, pl.multiple_of((col - 1) * depth + group * 8, 8))
            if col >= 1:
                target, source = velocity_rows(x, z, vx, vz)
                store_rows(source, stage_d, vel_r, pl.multiple_of((col - 1) * depth + group * 8, 8))
                if 2 <= col <= 3:
                    store_rows(target, stage_d, vel_l, pl.multiple_of((col - 2) * depth + group * 8, 8))
        return carry

    lax.fori_loop(0, groups, prepare, 0)
    acc[...] = jnp.zeros_like(acc)

    wide_m[0:depth] = left[4, 1]
    wide_m[depth : 2 * depth] = own[4, 0]
    wide_m[2 * depth : 3 * depth] = own[4, 1]
    wide_m[3 * depth : 4 * depth] = right[4, 0]

    def features(cell):
        return [out_l[cell + depth], vel_l[cell]]

    def target(cell, slots, turned, offset):
        sign = 9 * (cell >= depth).astype(jnp.int32)
        sums = [jnp.zeros((slots, 128), F32)] * 2

        def issue(chunk):
            return (
                product(turned, sources_of(out_r, cell + depth, depth, chunk, offset, posc, sign)),
                product(turned, sources_of(vel_r, cell, depth, chunk, offset + KP, velc)),
            )

        def consume(chunk, products):
            for i, n in enumerate(chunk):
                lanes = slice(128 * i, 128 * (i + 1))
                s = jnp.maximum(products[0][:, lanes], 0.0)
                q = s * s * wide_m[pl.ds(cell + (n // 3) * depth + n % 3 - 1, 1), :]
                sums[0] = sums[0] + q * s
                sums[1] = sums[1] + q * products[1][:, lanes]

        def finish():
            for i in range(2):
                acc[i, pl.ds(cell, 1), :] = fold(sums[i])

        return issue, consume, finish

    each_target(level, order, bounds, KP + KD, features, target)
    density = acc[0].reshape(2, depth, 128)
    div = -6.0 * acc[1].reshape(2, depth, 128)
    mass = own[4]
    alive = mass > 0.0
    density = jnp.where(alive, density, 0.0)
    weight = jnp.where(alive, mass / jnp.where(alive, density, 1.0), 0.0)
    source = jnp.where(
        alive, (density + TIME_STEP * div - REST_DENSITY) / REST_DENSITY, 0.0
    )
    out_w[...] = weight
    out_density[...] = density / REST_DENSITY
    out_source[...] = source
    out_send[0:2] = weight
    out_send[2] = source[1]


def column_update(alive, pressure, source, pulled, diagonal):
    updated = (1.0 - RELAXATION) * pressure + RELAXATION * (source + 6.0 * pulled) / diagonal
    return jnp.where(alive, updated, 0.0)


def jacobi_sums(level, order, bounds, first_col, feat_r, feat_l, posc, wide_u, acc, depth):
    def features(cell):
        return [feat_l[cell + first_col * depth]]

    def target(cell, slots, turned, offset):
        sign = 9 * (cell >= depth).astype(jnp.int32)
        at = cell + first_col * depth
        sums = [jnp.zeros((slots, 128), F32)]

        def issue(chunk):
            return product(turned, sources_of(feat_r, at, depth, chunk, offset, posc, sign))

        def consume(chunk, products):
            for i, n in enumerate(chunk):
                s = jnp.maximum(products[:, 128 * i : 128 * (i + 1)], 0.0)
                lifted = wide_u[pl.ds(cell + (n // 3) * depth + n % 3 - 1, 1), :]
                sums[0] = sums[0] + s * s * lifted

        def finish():
            acc[pl.ds(cell, 1), :] = fold(sums[0])

        return issue, consume, finish

    acc[...] = jnp.zeros_like(acc)
    each_target(level, order, bounds, KP, features, target)
    return acc[...].reshape(2, depth, 128)


def sweep1_kernel(
    level, order, bounds, feat_r, feat_l, left, own, recv, weight_own, source_own, posc,
    out_p, out_diag, out_send, wide_w, wide_u, acc,
):
    depth = weight_own.shape[1]
    start_l = jnp.where(left[4] > 0.0, left[5], 0.0)
    start_o = jnp.where(own[4] > 0.0, own[5], 0.0)
    for col in range(4):
        rows = slice(col * depth, (col + 1) * depth)
        weight = recv[col] if col < 2 else weight_own[col - 2]
        wide_w[rows] = weight
        wide_u[rows] = weight * (start_l if col < 2 else start_o)[col % 2]
    acc[...] = jnp.zeros_like(acc)

    def features(cell):
        return [feat_l[cell]]

    def target(cell, slots, turned, offset):
        sign = 9 * (cell >= depth).astype(jnp.int32)
        sums = [jnp.zeros((slots, 128), F32)] * 2

        def issue(chunk):
            return product(turned, sources_of(feat_r, cell, depth, chunk, offset, posc, sign))

        def consume(chunk, products):
            for i, n in enumerate(chunk):
                s = jnp.maximum(products[:, 128 * i : 128 * (i + 1)], 0.0)
                q = s * s
                at = pl.ds(cell + (n // 3) * depth + n % 3 - 1, 1)
                sums[0] = sums[0] + q * wide_w[at, :]
                sums[1] = sums[1] + q * wide_u[at, :]

        def finish():
            for i in range(2):
                acc[i, pl.ds(cell, 1), :] = fold(sums[i])

        return issue, consume, finish

    each_target(level, order, bounds, KP, features, target)
    diagonal = COMPRESSION + 6.0 * acc[0].reshape(2, depth, 128)
    pulled = acc[1].reshape(2, depth, 128)
    out_diag[...] = diagonal
    below = column_update(left[4, 1] > 0.0, start_l[1], recv[2], pulled[0], diagonal[0])
    here = column_update(own[4, 0] > 0.0, start_o[0], source_own[0], pulled[1], diagonal[1])
    out_p[0] = below
    out_p[1] = here
    out_send[0] = below
    out_send[1] = here
    out_send[2] = weight_own[0]
    out_send[3] = diagonal[0]


def sweep2_kernel(
    level, order, bounds, feat_r, feat_l, own, recv1, recv2, weight_own, source_own, diag, p1, posc,
    out_p, wide_u, acc,
):
    depth = weight_own.shape[1]
    wide_u[0:depth] = recv1[1] * p1[0]
    wide_u[depth : 2 * depth] = weight_own[0] * p1[1]
    wide_u[2 * depth : 3 * depth] = weight_own[1] * recv2[0]
    wide_u[3 * depth : 4 * depth] = recv2[2] * recv2[1]
    pulled = jacobi_sums(level, order, bounds, 1, feat_r, feat_l, posc, wide_u, acc, depth)
    out_p[0] = column_update(own[4, 0] > 0.0, p1[1], source_own[0], pulled[0], diag[1])
    out_p[1] = column_update(own[4, 1] > 0.0, recv2[0], source_own[1], pulled[1], recv2[3])


def sweep3_kernel(
    level, order, bounds, feat_r, feat_l, left, own, recv1, recv3, weight_own, source_own, diag, p2, posc,
    out_p, wide_u, acc,
):
    depth = weight_own.shape[1]
    wide_u[0 : 2 * depth] = (recv1[0:2] * recv3[...]).reshape(2 * depth, 128)
    wide_u[2 * depth : 4 * depth] = (weight_own[...] * p2[...]).reshape(2 * depth, 128)
    pulled = jacobi_sums(level, order, bounds, 0, feat_r, feat_l, posc, wide_u, acc, depth)
    out_p[0] = column_update(left[4, 1] > 0.0, recv3[1], recv1[2], pulled[0], diag[0])
    out_p[1] = column_update(own[4, 0] > 0.0, p2[0], source_own[0], pulled[1], diag[1])


def force_kernel(
    level, order, bounds, feat_r, feat_l, own, recv1, recv2, recv4, left, right, weight_own, p3, posc,
    out_pressure, out_acc, out_velocity, out_offsets,
    wide_p, wide_w, wide_x, wide_z, pres_r, pres_l, stage, acc,
):
    depth = weight_own.shape[1]
    wide_p[0:2] = p3[...]
    wide_p[2:4] = recv4[...]
    wide_w[0] = recv1[1]
    wide_w[1:3] = weight_own[...]
    wide_w[3] = recv2[2]
    for field, wide in ((0, wide_x), (1, wide_z)):
        wide[0:depth] = left[field, 1] - 0.5
        wide[depth : 3 * depth] = own[field].reshape(2 * depth, 128) - 0.5
        wide[3 * depth : 4 * depth] = right[field, 0] - 0.5

    def prepare(group, carry):
        rows = pl.ds(pl.multiple_of(group * 8, 8), 8)
        for col in range(4):
            pressure, weight = wide_p[col, rows, :], wide_w[col, rows, :]
            target, source = pressure_rows(weight, weight * pressure, pressure)
            store_rows(source, stage, pres_r, pl.multiple_of(col * depth + group * 8, 8))
            if 1 <= col <= 2:
                store_rows(target, stage, pres_l, pl.multiple_of((col - 1) * depth + group * 8, 8))
        return carry

    lax.fori_loop(0, depth // 8, prepare, 0)

    def features(cell):
        return [feat_l[cell + depth], pres_l[cell]]

    def target(cell, slots, turned, offset):
        sign = 9 * (cell >= depth).astype(jnp.int32)
        sums = [jnp.zeros((slots, 128), F32)] * 3

        def issue(chunk):
            return (
                product(turned, sources_of(feat_r, cell + depth, depth, chunk, offset, posc, sign)),
                product(turned, sources_of(pres_r, cell, depth, chunk, offset + KP)),
            )

        def consume(chunk, products):
            for i, n in enumerate(chunk):
                lanes = slice(128 * i, 128 * (i + 1))
                s = jnp.maximum(products[0][:, lanes], 0.0)
                g = s * s * products[1][:, lanes]
                at = pl.ds(cell + (n // 3) * depth + n % 3 - 1, 1)
                sums[0] = sums[0] + g
                sums[1] = sums[1] + g * (wide_x[at, :] + float(n // 3 - 1))
                sums[2] = sums[2] + g * (wide_z[at, :] + float(n % 3 - 1))

        def finish():
            for i in range(3):
                acc[i, pl.ds(cell, 1), :] = fold(sums[i])

        return issue, consume, finish

    acc[...] = jnp.zeros_like(acc)
    each_target(level, order, bounds, KP + KE, features, target)
    sums = acc[...].reshape(3, 2, depth, 128)
    inner = slice(HALO, depth - HALO)
    alive = own[4, :, inner] > 0.0
    out_pressure[0] = p3[1, inner]
    out_pressure[1] = recv4[0, inner]
    for axis, wide, pull in ((0, wide_x, 0.0), (1, wide_z, GRAVITY)):
        here = wide[depth : 3 * depth].reshape(2, depth, 128)
        force = 6.0 * (here[:, inner] * sums[0, :, inner] - sums[axis + 1, :, inner])
        force = jnp.where(alive, force, 0.0)
        velocity = jnp.where(alive, own[axis + 2, :, inner] + TIME_STEP * (force - pull), 0.0)
        out_acc[axis] = force
        out_velocity[axis] = velocity
        out_offsets[axis] = jnp.where(alive, own[axis, :, inner] + TIME_STEP * velocity, 0.0)


def leaving_kernel(
    slot, count, side, offsets, velocity, pressure, mass, out_up, out_down, hot
):
    blocks, slots = slot.shape
    fields = [offsets[0], offsets[1], velocity[0], velocity[1], pressure[...], mass[...]]
    fields = [f.reshape(-1, slots) for f in fields]
    cells = fields[0].shape[0]
    number = lax.broadcasted_iota(jnp.int32, (cells, slots), 0)
    place = lax.broadcasted_iota(jnp.int32, (slots, slots), 0)
    for b in range(blocks):
        one_hot = (number == slot[b : b + 1, :] // slots).astype(F32).astype(BF16)
        for part in range(3):
            hot[part * cells : (part + 1) * cells, b * slots : (b + 1) * slots] = one_hot
    filled = lax.broadcasted_iota(jnp.int32, (blocks, slots), 1) < count[...]
    up = side[...] == 1
    for index, field in enumerate(fields):
        parts = jnp.concatenate([v.astype(BF16) for v in split3(field.T)], axis=1)
        rows = []
        for b in range(blocks):
            picked = product(parts, hot[:, b * slots : (b + 1) * slots])
            here = place == slot[b : b + 1, :] % slots
            rows.append(jnp.sum(jnp.where(here, picked, 0.0), axis=0, keepdims=True))
        block = jnp.where(filled, jnp.concatenate(rows, axis=0), 0.0)
        out_up[index] = jnp.where(up, block, 0.0)
        out_down[index] = jnp.where(up, 0.0, block)


def target_lists(count, cells):
    depth = count.shape[1]
    number = jnp.arange(2 * depth, dtype=jnp.int32)
    kinds = []
    for level in range(1, ITERS + 3):
        window = count[1:3] if level % 2 else count[0:2]
        kind = sum((window > slots).astype(jnp.int32) for slots, _ in CLASSES[:-1])
        reach = ITERS + 2 - level
        row = jnp.arange(depth, dtype=jnp.int32)[None]
        kind = jnp.where((row >= HALO - reach) & (row < HALO + cells + reach), kind, len(CLASSES))
        kinds.append(kind.reshape(-1))
    kinds = jnp.stack(kinds)
    key = kinds * (2 * depth) + number
    rank = jnp.sum((key[:, None, :] < key[:, :, None]).astype(jnp.int32), 2)
    bounds = jnp.stack([jnp.sum((kinds < c).astype(jnp.int32), 1) for c in range(len(CLASSES) + 1)], 1)
    place = jnp.arange(2 * depth + max(c for _, c in CLASSES), dtype=jnp.int32)
    order = jnp.sum(jnp.where(rank[:, None, :] == place[None, :, None], number, 0), 2)
    return jnp.where(place < bounds[:, -1:], order, HALO), bounds


def local_call(kernel, out_shapes, scratch, scalars, *operands):
    vmem = pl.BlockSpec(memory_space=pltpu.VMEM)
    smem = pl.BlockSpec(memory_space=pltpu.SMEM)
    return pl.pallas_call(
        kernel,
        out_shape=[jax.ShapeDtypeStruct(shape, dtype) for shape, dtype in out_shapes],
        in_specs=[smem] * len(scalars) + [vmem] * len(operands),
        out_specs=[vmem] * len(out_shapes),
        scratch_shapes=[pltpu.VMEM(shape, dtype) for shape, dtype in scratch],
        compiler_params=pltpu.CompilerParams(vmem_limit_bytes=VMEM_LIMIT),
    )(*scalars, *operands)


def from_behind(block, axis, distance):
    devices = range(lax.axis_size(axis))
    route = [(i - distance, i) for i in devices if i - distance in devices]
    return lax.ppermute(block, axis, route)


def around(block, axis, distance):
    peers = lax.axis_size(axis)
    return lax.ppermute(block, axis, [(i, (i + distance) % peers) for i in range(peers)])


def per_device(
    offsets, velocity, particle_mass, pressure_start, counts, leaving_slot, leaving_count, leaving_side
):
    cells, slots = counts.shape[1], offsets.shape[-1]
    alive = jnp.arange(slots, dtype=jnp.int32)[None, None, :] < counts[:, :, None]
    live_mass = jnp.where(alive, particle_mass, 0.0)
    base = jnp.concatenate([offsets, velocity, live_mass[None], pressure_start[None]], 0)
    above = from_behind(base[:, :, cells - HALO :], "slab", 1)
    below = from_behind(base[:, :, :HALO], "slab", -1)
    own = jnp.concatenate([above, base, below], 2)
    left = around(own, "col", 1)
    right = around(own[:5, :1], "col", -1)
    depth = cells + 2 * HALO
    first = lax.axis_index("col") == 0
    last = lax.axis_index("col") == lax.axis_size("col") - 1
    here = position_table((first, -1), (last, 1))
    back = position_table((first, 1), (first, -1))
    velc = sign_table(velocity_signs)
    plane = (2, depth, slots)

    live = jnp.stack([left[4, 1], own[4, 0], own[4, 1]]) > 0.0
    lists = target_lists(jnp.sum(live.astype(jnp.int32), -1), cells)
    long = (4 * depth, slots)
    sums = (2 * depth, slots)

    feat_r, feat_l, weight, density_ratio, source, send1 = local_call(
        functools.partial(density_kernel, 0),
        [
            ((5 * depth, KP, slots), BF16),
            ((3 * depth, KP, slots), BF16),
            (plane, F32),
            (plane, F32),
            (plane, F32),
            ((3, depth, slots), F32),
        ],
        [
            ((8 * KP, slots), F32),
            ((8 * KD, slots), F32),
            ((4 * depth, KD, slots), BF16),
            ((2 * depth, KD, slots), BF16),
            (long, F32),
            ((2, *sums), F32),
        ],
        lists, left, own, right, here, velc,
    )
    recv1 = around(send1, "col", 1)
    p1, diag, send2 = local_call(
        functools.partial(sweep1_kernel, 1),
        [(plane, F32), (plane, F32), ((4, depth, slots), F32)],
        [(long, F32), (long, F32), ((2, *sums), F32)],
        lists, feat_r, feat_l, left, own, recv1, weight, source, back,
    )
    recv2 = around(send2, "col", -1)
    (p2,) = local_call(
        functools.partial(sweep2_kernel, 2),
        [(plane, F32)],
        [(long, F32), (sums, F32)],
        lists, feat_r, feat_l, own, recv1, recv2, weight, source, diag, p1, here,
    )
    recv3 = around(p2, "col", 1)
    (p3,) = local_call(
        functools.partial(sweep3_kernel, 3),
        [(plane, F32)],
        [(long, F32), (sums, F32)],
        lists, feat_r, feat_l, left, own, recv1, recv3, weight, source, diag, p2, back,
    )
    recv4 = around(p3, "col", -1)
    inner = (2, cells, slots)
    pressure, acceleration, velocity_new, offsets_new = local_call(
        functools.partial(force_kernel, 4),
        [(inner, F32), ((2, *inner), F32), ((2, *inner), F32), ((2, *inner), F32)],
        [((4, depth, slots), F32)] * 2
        + [(long, F32)] * 2
        + [
            ((4 * depth, KE, slots), BF16),
            ((2 * depth, KE, slots), BF16),
            ((8 * KE, slots), F32),
            ((3, *sums), F32),
        ],
        lists, feat_r, feat_l, own, recv1, recv2, recv4, left, right, weight, p3, here,
    )
    density_ratio = density_ratio[:, HALO : HALO + cells]
    blocks = leaving_slot.shape[0]
    packed = ((6, blocks, slots), F32)
    upward, downward = local_call(
        leaving_kernel,
        [packed, packed],
        [((3 * counts.size, blocks * slots), BF16)],
        (),
        leaving_slot[:, 0], leaving_count, leaving_side, offsets_new, velocity_new, pressure, live_mass,
    )
    arrived = jnp.stack([from_behind(upward, "col", 1), from_behind(downward, "col", -1)])[:, :, :, None]
    return (density_ratio, pressure, acceleration, velocity_new, offsets_new, arrived)


def solution(mesh):
    return jax.shard_map(
        per_device,
        mesh=mesh,
        in_specs=(
            P(None, "col", "slab", None),
            P(None, "col", "slab", None),
            P("col", "slab", None),
            P("col", "slab", None),
            P("col", "slab"),
            P("col", "slab", None),
            P("col", "slab"),
            P("col", "slab"),
        ),
        out_specs=(
            P("col", "slab", None),
            P("col", "slab", None),
            P(None, "col", "slab", None),
            P(None, "col", "slab", None),
            P(None, "col", "slab", None),
            P(None, None, "col", "slab", None),
        ),
        check_vma=False,
    )
```

```python
import functools

import jax
import jax.numpy as jnp
import ml_dtypes
import numpy as np
from jax import lax
from jax.experimental import pallas as pl
from jax.experimental.pallas import tpu as pltpu
from jax.sharding import PartitionSpec as P

ITERS = 3
TIME_STEP = 0.1
REST_DENSITY = 50.0
COMPRESSION = 2.0
RELAXATION = 0.5
GRAVITY = 1.0

HALO = 8
CLASSES = ((32, 16), (64, 8), (96, 6), (128, 6))
CHUNKS = ((0, 1), (2, 3), (4, 5), (6, 7), (8,))
AHEAD = 5
KP = 32
KD = 48
KE = 16
FAR = -64.0
SHIFTS = [(sx, sz) for sx in (-1, 0, 1) for sz in (-1, 0, 1)]
F32 = jnp.float32
BF16 = jnp.bfloat16
VMEM_LIMIT = 56 * 1024 * 1024


def split3(value):
    high = value.astype(BF16).astype(F32)
    rest = value - high
    mid = rest.astype(BF16).astype(F32)
    return [high, mid, rest - mid]


def left_six(parts):
    h, m, l = parts
    return [h, h, h, m, m, l]


def right_six(parts):
    h, m, l = parts
    return [h, m, l, h, m, h]


def position_rows(x, z):
    one, zero = jnp.ones_like(x), jnp.zeros_like(x)
    x, z = x - 0.5, z - 0.5
    xs, zs = split3(x), split3(z)
    square = x * x + z * z
    x2, z2 = [2.0 * v for v in xs], [2.0 * v for v in zs]
    ones = [one] * 3
    target = (
        left_six(x2) + x2 + ones + left_six(z2) + z2 + ones + split3(1.0 - square) + ones + [one, zero]
    )
    source = (
        right_six(xs) + ones + x2 + right_six(zs) + ones + z2 + ones + split3(-square) + [one, zero]
    )
    return target, source


def position_signs(sx, sz):
    return [1] * 6 + [sx] * 3 + [-sx] * 3 + [1] * 6 + [sz] * 3 + [-sz] * 3 + [1] * 6 + [-(sx * sx + sz * sz), 0]


def velocity_rows(x, z, vx, vz):
    one, zero = jnp.ones_like(x), jnp.zeros_like(x)
    x, z = x - 0.5, z - 0.5
    xs, zs, vxs, vzs = split3(x), split3(z), split3(vx), split3(vz)
    dots = split3(vx * x + vz * z)
    ones = [one] * 3
    pad = [zero] * 6
    minus = lambda rows: [-v for v in rows]
    target = dots + left_six(vxs) + left_six(vzs) + left_six(xs) + left_six(zs) + ones + vxs + vzs + ones + ones + pad
    source = (
        ones
        + minus(right_six(xs) + right_six(zs) + right_six(vxs) + right_six(vzs))
        + dots
        + ones
        + ones
        + vxs
        + vzs
        + pad
    )
    return target, source


def velocity_signs(sx, sz):
    return [1] * 30 + [-sx] * 3 + [-sz] * 3 + [sx] * 3 + [sz] * 3 + [0] * 6


def pressure_rows(weight, lifted, pressure):
    one, zero = jnp.ones_like(weight), jnp.zeros_like(weight)
    pad = [zero] * 7
    target = [one] * 3 + left_six(split3(pressure)) + pad
    source = split3(lifted) + [-v for v in right_six(split3(weight))] + pad
    return target, source


def wide_table(table):
    return np.repeat(np.asarray(table, np.float32)[:, :, None], 128, axis=2).astype(ml_dtypes.bfloat16)


def velocity_table():
    return wide_table([velocity_signs(sx, sz) for sx, sz in SHIFTS])


def position_table():
    tables = []
    for cuts in ((), ((0, -1),), ((1, 1),), ((0, 1), (1, -1))):
        for t in range(2):
            for sx, sz in SHIFTS:
                signs = position_signs(sx, sz)
                if (t, sx) in cuts:
                    signs[KP - 2] = FAR
                tables.append(signs)
    return wide_table(tables)


def store_rows(rows, stage, dest, cell):
    count = len(rows)
    for index, value in enumerate(rows):
        stage[pl.ds(index, 8, stride=count), :] = value
    dest[pl.ds(cell, 8)] = stage[...].reshape(8, count, 128).astype(BF16)


def upright(rows, slots):
    return rows.astype(F32).T[:slots].astype(BF16)


def sources_of(feat, cell, depth, chunk, table=None, first=0):
    parts = []
    for n in chunk:
        part = feat[cell + (n // 3) * depth + n % 3 - 1]
        parts.append(part if table is None else part * table[first + n])
    return jnp.concatenate(parts, axis=1) if len(parts) > 1 else parts[0]


def product(left, right):
    return jnp.dot(left, right, preferred_element_type=F32)


def fold(total):
    return jnp.sum(total.T, axis=0, keepdims=True)


def each_target(level, order, bounds, stashes, target):
    for index, (slots, cells) in enumerate(CLASSES):
        start = bounds[level, index]
        steps = (bounds[level, index + 1] - start + cells - 1) // cells

        def step(i, carry, slots=slots, cells=cells, start=start):
            waiting = []
            for u in range(cells):
                issue, consume, finish = target(order[level, start + i * cells + u], slots)
                for chunk in CHUNKS:
                    lanes = slice(128 * chunk[0], 128 * (chunk[-1] + 1))
                    for stash, value in zip(stashes, issue(chunk)):
                        stash[u, 0:slots, lanes] = value
                    waiting.append((u, slots, consume, chunk, finish))
                    if len(waiting) > AHEAD:
                        take(stashes, *waiting.pop(0))
            for entry in waiting:
                take(stashes, *entry)
            return carry

        lax.fori_loop(0, steps, step, 0)


def take(stashes, u, slots, consume, chunk, finish):
    for n in chunk:
        consume(n, *[stash[u, 0:slots, 128 * n : 128 * (n + 1)] for stash in stashes])
    if chunk is CHUNKS[-1]:
        finish()


def stash_shape(slots):
    return ((max(cells for _, cells in CLASSES), slots, 9 * 128), F32)


def density_kernel(
    level, order, bounds, left, own, right, posc, velc,
    out_r, out_l, out_w, out_density, out_source, out_send,
    stage_p, stage_d, vel_r, vel_l, wide_m, acc, stash_a, stash_b,
):
    depth = own.shape[2]
    groups = depth // 8
    blocks = [(left, 0), (left, 1), (own, 0), (own, 1), (right, 0)]

    def prepare(group, carry):
        rows = pl.ds(pl.multiple_of(group * 8, 8), 8)
        for col, (ref, at) in enumerate(blocks):
            x, z, vx, vz = (ref[f, at, rows, :] for f in range(4))
            cell = pl.multiple_of(col * depth + group * 8, 8)
            target, source = position_rows(x, z)
            store_rows(source, stage_p, out_r, cell)
            if 1 <= col <= 3:
                store_rows(target, stage_p, out_l, pl.multiple_of((col - 1) * depth + group * 8, 8))
            if col >= 1:
                target, source = velocity_rows(x, z, vx, vz)
                store_rows(source, stage_d, vel_r, pl.multiple_of((col - 1) * depth + group * 8, 8))
                if 2 <= col <= 3:
                    store_rows(target, stage_d, vel_l, pl.multiple_of((col - 2) * depth + group * 8, 8))
        return carry

    lax.fori_loop(0, groups, prepare, 0)
    acc[...] = jnp.zeros_like(acc)

    wide_m[0:depth] = left[4, 1]
    wide_m[depth : 2 * depth] = own[4, 0]
    wide_m[2 * depth : 3 * depth] = own[4, 1]
    wide_m[3 * depth : 4 * depth] = right[4, 0]

    def target(cell, slots):
        sign = bounds[level, len(CLASSES) + 1] + 9 * (cell >= depth).astype(jnp.int32)
        pos_l, vel_l_t = upright(out_l[cell + depth], slots), upright(vel_l[cell], slots)
        sums = [jnp.zeros((slots, 128), F32)] * 2

        def issue(chunk):
            return (
                product(pos_l, sources_of(out_r, cell + depth, depth, chunk, posc, sign)),
                product(vel_l_t, sources_of(vel_r, cell, depth, chunk, velc)),
            )

        def consume(n, reach, closing):
            s = jnp.maximum(reach, 0.0)
            q = s * s * wide_m[pl.ds(cell + (n // 3) * depth + n % 3 - 1, 1), :]
            sums[0] = sums[0] + q * s
            sums[1] = sums[1] + q * closing

        def finish():
            for i in range(2):
                acc[i, pl.ds(cell, 1), 0:slots] = fold(sums[i])

        return issue, consume, finish

    each_target(level, order, bounds, (stash_a, stash_b), target)
    density = acc[0].reshape(2, depth, 128)
    div = -6.0 * acc[1].reshape(2, depth, 128)
    mass = own[4]
    alive = mass > 0.0
    density = jnp.where(alive, density, 0.0)
    weight = jnp.where(alive, mass / jnp.where(alive, density, 1.0), 0.0)
    source = jnp.where(
        alive, (density + TIME_STEP * div - REST_DENSITY) / REST_DENSITY, 0.0
    )
    out_w[...] = weight
    out_density[...] = density / REST_DENSITY
    out_source[...] = source
    out_send[0:2] = weight
    out_send[2] = source[1]


def column_update(alive, pressure, source, pulled, diagonal):
    updated = (1.0 - RELAXATION) * pressure + RELAXATION * (source + 6.0 * pulled) / diagonal
    return jnp.where(alive, updated, 0.0)


def jacobi_sums(level, order, bounds, first_col, feat_r, feat_l, posc, wide_u, acc, stash, depth):
    def target(cell, slots):
        sign = bounds[level, len(CLASSES) + 1] + 9 * (cell >= depth).astype(jnp.int32)
        at = cell + first_col * depth
        pos_l = upright(feat_l[at], slots)
        sums = [jnp.zeros((slots, 128), F32)]

        def issue(chunk):
            return (product(pos_l, sources_of(feat_r, at, depth, chunk, posc, sign)),)

        def consume(n, reach):
            s = jnp.maximum(reach, 0.0)
            lifted = wide_u[pl.ds(cell + (n // 3) * depth + n % 3 - 1, 1), :]
            sums[0] = sums[0] + s * s * lifted

        def finish():
            acc[pl.ds(cell, 1), 0:slots] = fold(sums[0])

        return issue, consume, finish

    acc[...] = jnp.zeros_like(acc)
    each_target(level, order, bounds, (stash,), target)
    return acc[...].reshape(2, depth, 128)


def sweep1_kernel(
    level, order, bounds, feat_r, feat_l, left, own, recv, weight_own, source_own, posc,
    out_p, out_diag, out_send, wide_w, wide_u, acc, stash,
):
    depth = weight_own.shape[1]
    start_l = jnp.where(left[4] > 0.0, left[5], 0.0)
    start_o = jnp.where(own[4] > 0.0, own[5], 0.0)
    for col in range(4):
        rows = slice(col * depth, (col + 1) * depth)
        weight = recv[col] if col < 2 else weight_own[col - 2]
        wide_w[rows] = weight
        wide_u[rows] = weight * (start_l if col < 2 else start_o)[col % 2]
    acc[...] = jnp.zeros_like(acc)

    def target(cell, slots):
        sign = bounds[level, len(CLASSES) + 1] + 9 * (cell >= depth).astype(jnp.int32)
        pos_l = upright(feat_l[cell], slots)
        sums = [jnp.zeros((slots, 128), F32)] * 2

        def issue(chunk):
            return (product(pos_l, sources_of(feat_r, cell, depth, chunk, posc, sign)),)

        def consume(n, reach):
            s = jnp.maximum(reach, 0.0)
            q = s * s
            at = pl.ds(cell + (n // 3) * depth + n % 3 - 1, 1)
            sums[0] = sums[0] + q * wide_w[at, :]
            sums[1] = sums[1] + q * wide_u[at, :]

        def finish():
            for i in range(2):
                acc[i, pl.ds(cell, 1), 0:slots] = fold(sums[i])

        return issue, consume, finish

    each_target(level, order, bounds, (stash,), target)
    diagonal = COMPRESSION + 6.0 * acc[0].reshape(2, depth, 128)
    pulled = acc[1].reshape(2, depth, 128)
    out_diag[...] = diagonal
    below = column_update(left[4, 1] > 0.0, start_l[1], recv[2], pulled[0], diagonal[0])
    here = column_update(own[4, 0] > 0.0, start_o[0], source_own[0], pulled[1], diagonal[1])
    out_p[0] = below
    out_p[1] = here
    out_send[0] = below
    out_send[1] = here
    out_send[2] = weight_own[0]
    out_send[3] = diagonal[0]


def sweep2_kernel(
    level, order, bounds, feat_r, feat_l, own, recv1, recv2, weight_own, source_own, diag, p1, posc,
    out_p, wide_u, acc, stash,
):
    depth = weight_own.shape[1]
    wide_u[0:depth] = recv1[1] * p1[0]
    wide_u[depth : 2 * depth] = weight_own[0] * p1[1]
    wide_u[2 * depth : 3 * depth] = weight_own[1] * recv2[0]
    wide_u[3 * depth : 4 * depth] = recv2[2] * recv2[1]
    pulled = jacobi_sums(level, order, bounds, 1, feat_r, feat_l, posc, wide_u, acc, stash, depth)
    out_p[0] = column_update(own[4, 0] > 0.0, p1[1], source_own[0], pulled[0], diag[1])
    out_p[1] = column_update(own[4, 1] > 0.0, recv2[0], source_own[1], pulled[1], recv2[3])


def sweep3_kernel(
    level, order, bounds, feat_r, feat_l, left, own, recv1, recv3, weight_own, source_own, diag, p2, posc,
    out_p, wide_u, acc, stash,
):
    depth = weight_own.shape[1]
    wide_u[0 : 2 * depth] = (recv1[0:2] * recv3[...]).reshape(2 * depth, 128)
    wide_u[2 * depth : 4 * depth] = (weight_own[...] * p2[...]).reshape(2 * depth, 128)
    pulled = jacobi_sums(level, order, bounds, 0, feat_r, feat_l, posc, wide_u, acc, stash, depth)
    out_p[0] = column_update(left[4, 1] > 0.0, recv3[1], recv1[2], pulled[0], diag[0])
    out_p[1] = column_update(own[4, 0] > 0.0, p2[0], source_own[0], pulled[1], diag[1])


def force_kernel(
    level, order, bounds, feat_r, feat_l, own, recv1, recv2, recv4, left, right, weight_own, p3, posc,
    out_pressure, out_acc, out_velocity, out_offsets,
    wide_p, wide_w, wide_x, wide_z, pres_r, pres_l, stage, acc, stash_a, stash_b,
):
    depth = weight_own.shape[1]
    wide_p[0:2] = p3[...]
    wide_p[2:4] = recv4[...]
    wide_w[0] = recv1[1]
    wide_w[1:3] = weight_own[...]
    wide_w[3] = recv2[2]
    for field, wide in ((0, wide_x), (1, wide_z)):
        wide[0:depth] = left[field, 1] - 0.5
        wide[depth : 3 * depth] = own[field].reshape(2 * depth, 128) - 0.5
        wide[3 * depth : 4 * depth] = right[field, 0] - 0.5

    def prepare(group, carry):
        rows = pl.ds(pl.multiple_of(group * 8, 8), 8)
        for col in range(4):
            pressure, weight = wide_p[col, rows, :], wide_w[col, rows, :]
            target, source = pressure_rows(weight, weight * pressure, pressure)
            store_rows(source, stage, pres_r, pl.multiple_of(col * depth + group * 8, 8))
            if 1 <= col <= 2:
                store_rows(target, stage, pres_l, pl.multiple_of((col - 1) * depth + group * 8, 8))
        return carry

    lax.fori_loop(0, depth // 8, prepare, 0)

    def target(cell, slots):
        sign = bounds[level, len(CLASSES) + 1] + 9 * (cell >= depth).astype(jnp.int32)
        pos_l, pres_l_t = upright(feat_l[cell + depth], slots), upright(pres_l[cell], slots)
        sums = [jnp.zeros((slots, 128), F32)] * 3

        def issue(chunk):
            return (
                product(pos_l, sources_of(feat_r, cell + depth, depth, chunk, posc, sign)),
                product(pres_l_t, sources_of(pres_r, cell, depth, chunk)),
            )

        def consume(n, reach, lift):
            s = jnp.maximum(reach, 0.0)
            g = s * s * lift
            at = pl.ds(cell + (n // 3) * depth + n % 3 - 1, 1)
            sums[0] = sums[0] + g
            sums[1] = sums[1] + g * (wide_x[at, :] + float(n // 3 - 1))
            sums[2] = sums[2] + g * (wide_z[at, :] + float(n % 3 - 1))

        def finish():
            for i in range(3):
                acc[i, pl.ds(cell, 1), 0:slots] = fold(sums[i])

        return issue, consume, finish

    acc[...] = jnp.zeros_like(acc)
    each_target(level, order, bounds, (stash_a, stash_b), target)
    sums = acc[...].reshape(3, 2, depth, 128)
    inner = slice(HALO, depth - HALO)
    alive = own[4, :, inner] > 0.0
    out_pressure[0] = p3[1, inner]
    out_pressure[1] = recv4[0, inner]
    for axis, wide, pull in ((0, wide_x, 0.0), (1, wide_z, GRAVITY)):
        here = wide[depth : 3 * depth].reshape(2, depth, 128)
        force = 6.0 * (here[:, inner] * sums[0, :, inner] - sums[axis + 1, :, inner])
        force = jnp.where(alive, force, 0.0)
        velocity = jnp.where(alive, own[axis + 2, :, inner] + TIME_STEP * (force - pull), 0.0)
        out_acc[axis] = force
        out_velocity[axis] = velocity
        out_offsets[axis] = jnp.where(alive, own[axis, :, inner] + TIME_STEP * velocity, 0.0)


def leaving_kernel(
    slot, count, side, offsets, velocity, pressure, mass, out_up, out_down, hot
):
    blocks, slots = slot.shape
    fields = [offsets[0], offsets[1], velocity[0], velocity[1], pressure[...], mass[...]]
    fields = [f.reshape(-1, slots) for f in fields]
    cells = fields[0].shape[0]
    number = lax.broadcasted_iota(jnp.int32, (cells, slots), 0)
    place = lax.broadcasted_iota(jnp.int32, (slots, slots), 0)
    for b in range(blocks):
        one_hot = (number == slot[b : b + 1, :] // slots).astype(F32).astype(BF16)
        for part in range(3):
            hot[part * cells : (part + 1) * cells, b * slots : (b + 1) * slots] = one_hot
    filled = lax.broadcasted_iota(jnp.int32, (blocks, slots), 1) < count[...]
    up = side[...] == 1
    for index, field in enumerate(fields):
        parts = jnp.concatenate([v.astype(BF16) for v in split3(field.T)], axis=1)
        rows = []
        for b in range(blocks):
            picked = product(parts, hot[:, b * slots : (b + 1) * slots])
            here = place == slot[b : b + 1, :] % slots
            rows.append(jnp.sum(jnp.where(here, picked, 0.0), axis=0, keepdims=True))
        block = jnp.where(filled, jnp.concatenate(rows, axis=0), 0.0)
        out_up[index] = jnp.where(up, block, 0.0)
        out_down[index] = jnp.where(up, 0.0, block)


def target_lists(count, cells, tables):
    depth = count.shape[1]
    number = jnp.arange(2 * depth, dtype=jnp.int32)
    kinds = []
    for level in range(1, ITERS + 3):
        window = count[1:3] if level % 2 else count[0:2]
        kind = sum((window > slots).astype(jnp.int32) for slots, _ in CLASSES[:-1])
        reach = ITERS + 2 - level
        row = jnp.arange(depth, dtype=jnp.int32)[None]
        kind = jnp.where((row >= HALO - reach) & (row < HALO + cells + reach), kind, len(CLASSES))
        kinds.append(kind.reshape(-1))
    kinds = jnp.stack(kinds)
    key = kinds * (2 * depth) + number
    rank = jnp.sum((key[:, None, :] < key[:, :, None]).astype(jnp.int32), 2)
    steps = jnp.arange(len(CLASSES) + 1, dtype=jnp.int32)
    bounds = jnp.sum((kinds[:, None, :] < steps[None, :, None]).astype(jnp.int32), 2)
    place = jnp.arange(2 * depth + max(c for _, c in CLASSES), dtype=jnp.int32)
    order = jnp.sum(jnp.where(rank[:, None, :] == place[None, :, None], number, 0), 2)
    order = jnp.where(place < bounds[:, -1:], order, HALO)
    return order, jnp.concatenate([bounds, tables[np.arange(ITERS + 2) % 2][:, None]], 1)


def local_call(kernel, out_shapes, scratch, scalars, *operands):
    vmem = pl.BlockSpec(memory_space=pltpu.VMEM)
    smem = pl.BlockSpec(memory_space=pltpu.SMEM)
    return pl.pallas_call(
        kernel,
        out_shape=[jax.ShapeDtypeStruct(shape, dtype) for shape, dtype in out_shapes],
        in_specs=[smem] * len(scalars) + [vmem] * len(operands),
        out_specs=[vmem] * len(out_shapes),
        scratch_shapes=[pltpu.VMEM(shape, dtype) for shape, dtype in scratch],
        compiler_params=pltpu.CompilerParams(vmem_limit_bytes=VMEM_LIMIT),
    )(*scalars, *operands)


def from_behind(block, axis, distance):
    devices = range(lax.axis_size(axis))
    route = [(i - distance, i) for i in devices if i - distance in devices]
    return lax.ppermute(block, axis, route)


def around(block, axis, distance):
    peers = lax.axis_size(axis)
    return lax.ppermute(block, axis, [(i, (i + distance) % peers) for i in range(peers)])


def per_device(
    offsets, velocity, particle_mass, pressure_start, counts, leaving_slot, leaving_count, leaving_side
):
    cells, slots = counts.shape[1], offsets.shape[-1]
    alive = jnp.arange(slots, dtype=jnp.int32)[None, None, :] < counts[:, :, None]
    live_mass = jnp.where(alive, particle_mass, 0.0)
    base = jnp.concatenate([offsets, velocity, live_mass[None], pressure_start[None]], 0)
    above = from_behind(base[:, :, cells - HALO :], "slab", 1)
    below = from_behind(base[:, :, :HALO], "slab", -1)
    own = jnp.concatenate([above, base, below], 2)
    left = around(own, "col", 1)
    right = around(own[:5, :1], "col", -1)
    depth = cells + 2 * HALO
    first = lax.axis_index("col") == 0
    last = lax.axis_index("col") == lax.axis_size("col") - 1
    here = jnp.where(first, 1, jnp.where(last, 2, 0))
    back = jnp.where(first, 3, 0)
    posc, velc = position_table(), velocity_table()
    plane = (2, depth, slots)

    live = jnp.stack([left[4, 1], own[4, 0], own[4, 1]]) > 0.0
    lists = target_lists(jnp.sum(live.astype(jnp.int32), -1), cells, 18 * jnp.stack([here, back]))
    long = (4 * depth, slots)
    sums = (2 * depth, slots)

    feat_r, feat_l, weight, density_ratio, source, send1 = local_call(
        functools.partial(density_kernel, 0),
        [
            ((5 * depth, KP, slots), BF16),
            ((3 * depth, KP, slots), BF16),
            (plane, F32),
            (plane, F32),
            (plane, F32),
            ((3, depth, slots), F32),
        ],
        [
            ((8 * KP, slots), F32),
            ((8 * KD, slots), F32),
            ((4 * depth, KD, slots), BF16),
            ((2 * depth, KD, slots), BF16),
            (long, F32),
            ((2, *sums), F32),
            stash_shape(slots),
            stash_shape(slots),
        ],
        lists, left, own, right, posc, velc,
    )
    recv1 = around(send1, "col", 1)
    p1, diag, send2 = local_call(
        functools.partial(sweep1_kernel, 1),
        [(plane, F32), (plane, F32), ((4, depth, slots), F32)],
        [(long, F32), (long, F32), ((2, *sums), F32), stash_shape(slots)],
        lists, feat_r, feat_l, left, own, recv1, weight, source, posc,
    )
    recv2 = around(send2, "col", -1)
    (p2,) = local_call(
        functools.partial(sweep2_kernel, 2),
        [(plane, F32)],
        [(long, F32), (sums, F32), stash_shape(slots)],
        lists, feat_r, feat_l, own, recv1, recv2, weight, source, diag, p1, posc,
    )
    recv3 = around(p2, "col", 1)
    (p3,) = local_call(
        functools.partial(sweep3_kernel, 3),
        [(plane, F32)],
        [(long, F32), (sums, F32), stash_shape(slots)],
        lists, feat_r, feat_l, left, own, recv1, recv3, weight, source, diag, p2, posc,
    )
    recv4 = around(p3, "col", -1)
    inner = (2, cells, slots)
    pressure, acceleration, velocity_new, offsets_new = local_call(
        functools.partial(force_kernel, 4),
        [(inner, F32), ((2, *inner), F32), ((2, *inner), F32), ((2, *inner), F32)],
        [((4, depth, slots), F32)] * 2
        + [(long, F32)] * 2
        + [
            ((4 * depth, KE, slots), BF16),
            ((2 * depth, KE, slots), BF16),
            ((8 * KE, slots), F32),
            ((3, *sums), F32),
            stash_shape(slots),
            stash_shape(slots),
        ],
        lists, feat_r, feat_l, own, recv1, recv2, recv4, left, right, weight, p3, posc,
    )
    density_ratio = density_ratio[:, HALO : HALO + cells]
    blocks = leaving_slot.shape[0]
    packed = ((6, blocks, slots), F32)
    upward, downward = local_call(
        leaving_kernel,
        [packed, packed],
        [((3 * counts.size, blocks * slots), BF16)],
        (),
        leaving_slot[:, 0], leaving_count, leaving_side, offsets_new, velocity_new, pressure, live_mass,
    )
    arrived = jnp.stack([from_behind(upward, "col", 1), from_behind(downward, "col", -1)])[:, :, :, None]
    return (density_ratio, pressure, acceleration, velocity_new, offsets_new, arrived)


def solution(mesh):
    return jax.shard_map(
        per_device,
        mesh=mesh,
        in_specs=(
            P(None, "col", "slab", None),
            P(None, "col", "slab", None),
            P("col", "slab", None),
            P("col", "slab", None),
            P("col", "slab"),
            P("col", "slab", None),
            P("col", "slab"),
            P("col", "slab"),
        ),
        out_specs=(
            P("col", "slab", None),
            P("col", "slab", None),
            P(None, "col", "slab", None),
            P(None, "col", "slab", None),
            P(None, "col", "slab", None),
            P(None, None, "col", "slab", None),
        ),
        check_vma=False,
    )
```

```python
import functools

import jax
import jax.numpy as jnp
import ml_dtypes
import numpy as np
from jax import lax
from jax.experimental import pallas as pl
from jax.experimental.pallas import tpu as pltpu
from jax.sharding import PartitionSpec as P

ITERS = 3
TIME_STEP = 0.1
REST_DENSITY = 50.0
COMPRESSION = 2.0
RELAXATION = 0.5
GRAVITY = 1.0

HALO = 8
CLASSES = ((32, 16), (64, 8), (96, 6), (128, 6))
CHUNKS = ((0, 1), (2, 3), (4, 5), (6, 7), (8,))
AHEAD = 2
KP = 32
FAR = -64.0
SHIFTS = [(sx, sz) for sx in (-1, 0, 1) for sz in (-1, 0, 1)]
F32 = jnp.float32
BF16 = jnp.bfloat16
VMEM_LIMIT = 56 * 1024 * 1024


def split3(value):
    high = value.astype(BF16).astype(F32)
    rest = value - high
    mid = rest.astype(BF16).astype(F32)
    return [high, mid, rest - mid]


def left_six(parts):
    h, m, l = parts
    return [h, h, h, m, m, l]


def right_six(parts):
    h, m, l = parts
    return [h, m, l, h, m, h]


def position_rows(x, z):
    one, zero = jnp.ones_like(x), jnp.zeros_like(x)
    x, z = x - 0.5, z - 0.5
    xs, zs = split3(x), split3(z)
    square = x * x + z * z
    x2, z2 = [2.0 * v for v in xs], [2.0 * v for v in zs]
    ones = [one] * 3
    target = (
        left_six(x2) + x2 + ones + left_six(z2) + z2 + ones + split3(1.0 - square) + ones + [one, zero]
    )
    source = (
        right_six(xs) + ones + x2 + right_six(zs) + ones + z2 + ones + split3(-square) + [one, zero]
    )
    return target, source


def position_signs(sx, sz):
    return [1] * 6 + [sx] * 3 + [-sx] * 3 + [1] * 6 + [sz] * 3 + [-sz] * 3 + [1] * 6 + [-(sx * sx + sz * sz), 0]


def wide_table(table):
    return np.repeat(np.asarray(table, np.float32)[:, :, None], 128, axis=2).astype(ml_dtypes.bfloat16)


def position_table():
    tables = []
    for cuts in ((), ((0, -1),), ((1, 1),), ((0, 1), (1, -1))):
        for t in range(2):
            for sx, sz in SHIFTS:
                signs = position_signs(sx, sz)
                if (t, sx) in cuts:
                    signs[KP - 2] = FAR
                tables.append(signs)
    return wide_table(tables)


def store_rows(rows, stage, dest, cell):
    count = len(rows)
    for index, value in enumerate(rows):
        stage[pl.ds(index, 8, stride=count), :] = value
    dest[pl.ds(cell, 8)] = stage[...].reshape(8, count, 128).astype(BF16)


def upright(rows, slots):
    return rows.astype(F32).T[:slots].astype(BF16)


def spread(row, slots):
    return jnp.broadcast_to(row, (128, 128)).T[:slots]


def sources_of(feat, cell, depth, chunk, table=None, first=0):
    parts = []
    for n in chunk:
        part = feat[cell + (n // 3) * depth + n % 3 - 1]
        parts.append(part if table is None else part * table[first + n])
    return jnp.concatenate(parts, axis=1) if len(parts) > 1 else parts[0]


def product(left, right):
    return jnp.dot(left, right, preferred_element_type=F32)


def fold(total):
    return jnp.sum(total.T, axis=0, keepdims=True)


def each_target(level, order, bounds, target):
    for index, (slots, cells) in enumerate(CLASSES):
        start = bounds[level, index]
        steps = (bounds[level, index + 1] - start + cells - 1) // cells

        def step(i, carry, slots=slots, cells=cells, start=start):
            waiting = []
            for u in range(cells):
                issue, consume, finish = target(order[level, start + i * cells + u], slots)
                for chunk in CHUNKS:
                    waiting.append((consume, chunk, issue(chunk), finish))
                    if len(waiting) > AHEAD:
                        take(waiting.pop(0))
            for entry in waiting:
                take(entry)
            return carry

        lax.fori_loop(0, steps, step, 0)


def take(entry):
    consume, chunk, products, finish = entry
    consume(chunk, products)
    if chunk is CHUNKS[-1]:
        finish()


def density_kernel(
    level, order, bounds, left, own, right, posc,
    out_r, out_l, out_w, out_density, out_source, out_send,
    stage_p, wide_m, wide_x, wide_z, wide_vx, wide_vz, acc,
):
    depth = own.shape[2]
    groups = depth // 8
    blocks = [(left, 0), (left, 1), (own, 0), (own, 1), (right, 0)]

    def prepare(group, carry):
        rows = pl.ds(pl.multiple_of(group * 8, 8), 8)
        for col, (ref, at) in enumerate(blocks):
            x, z = ref[0, at, rows, :], ref[1, at, rows, :]
            cell = pl.multiple_of(col * depth + group * 8, 8)
            target, source = position_rows(x, z)
            store_rows(source, stage_p, out_r, cell)
            if 1 <= col <= 3:
                store_rows(target, stage_p, out_l, pl.multiple_of((col - 1) * depth + group * 8, 8))
        return carry

    lax.fori_loop(0, groups, prepare, 0)
    acc[...] = jnp.zeros_like(acc)

    wides = (wide_x, wide_z, wide_vx, wide_vz, wide_m)
    for field, wide in enumerate(wides):
        wide[0:depth] = left[field, 1]
        wide[depth : 2 * depth] = own[field, 0]
        wide[2 * depth : 3 * depth] = own[field, 1]
        wide[3 * depth : 4 * depth] = right[field, 0]

    def target(cell, slots):
        sign = bounds[level, len(CLASSES) + 1] + 9 * (cell >= depth).astype(jnp.int32)
        pos_l = upright(out_l[cell + depth], slots)
        x, z, vx, vz = [spread(w[pl.ds(cell + depth, 1), :], slots) for w in wides[:4]]
        sums = [jnp.zeros((slots, 128), F32)] * 2

        def issue(chunk):
            return product(pos_l, sources_of(out_r, cell + depth, depth, chunk, posc, sign))

        def consume(chunk, products):
            for i, n in enumerate(chunk):
                s = jnp.maximum(products[:, 128 * i : 128 * (i + 1)], 0.0)
                at = pl.ds(cell + (n // 3) * depth + n % 3 - 1, 1)
                q = s * s * wide_m[at, :]
                closing = (vx - wide_vx[at, :]) * (x - (wide_x[at, :] + float(n // 3 - 1)))
                closing = closing + (vz - wide_vz[at, :]) * (z - (wide_z[at, :] + float(n % 3 - 1)))
                sums[0] = sums[0] + q * s
                sums[1] = sums[1] + q * closing

        def finish():
            for i in range(2):
                acc[i, pl.ds(cell, 1), 0:slots] = fold(sums[i])

        return issue, consume, finish

    each_target(level, order, bounds, target)
    density = acc[0].reshape(2, depth, 128)
    div = -6.0 * acc[1].reshape(2, depth, 128)
    mass = own[4]
    alive = mass > 0.0
    density = jnp.where(alive, density, 0.0)
    weight = jnp.where(alive, mass / jnp.where(alive, density, 1.0), 0.0)
    source = jnp.where(
        alive, (density + TIME_STEP * div - REST_DENSITY) / REST_DENSITY, 0.0
    )
    out_w[...] = weight
    out_density[...] = density / REST_DENSITY
    out_source[...] = source
    out_send[0:2] = weight
    out_send[2] = source[1]


def column_update(alive, pressure, source, pulled, diagonal):
    updated = (1.0 - RELAXATION) * pressure + RELAXATION * (source + 6.0 * pulled) / diagonal
    return jnp.where(alive, updated, 0.0)


def jacobi_sums(level, order, bounds, first_col, feat_r, feat_l, posc, wide_u, acc, depth):
    def target(cell, slots):
        sign = bounds[level, len(CLASSES) + 1] + 9 * (cell >= depth).astype(jnp.int32)
        at = cell + first_col * depth
        pos_l = upright(feat_l[at], slots)
        sums = [jnp.zeros((slots, 128), F32)]

        def issue(chunk):
            return product(pos_l, sources_of(feat_r, at, depth, chunk, posc, sign))

        def consume(chunk, products):
            for i, n in enumerate(chunk):
                s = jnp.maximum(products[:, 128 * i : 128 * (i + 1)], 0.0)
                lifted = wide_u[pl.ds(cell + (n // 3) * depth + n % 3 - 1, 1), :]
                sums[0] = sums[0] + s * s * lifted

        def finish():
            acc[pl.ds(cell, 1), 0:slots] = fold(sums[0])

        return issue, consume, finish

    acc[...] = jnp.zeros_like(acc)
    each_target(level, order, bounds, target)
    return acc[...].reshape(2, depth, 128)


def sweep1_kernel(
    level, order, bounds, feat_r, feat_l, left, own, recv, weight_own, source_own, posc,
    out_p, out_diag, out_send, wide_w, wide_u, acc,
):
    depth = weight_own.shape[1]
    start_l = jnp.where(left[4] > 0.0, left[5], 0.0)
    start_o = jnp.where(own[4] > 0.0, own[5], 0.0)
    for col in range(4):
        rows = slice(col * depth, (col + 1) * depth)
        weight = recv[col] if col < 2 else weight_own[col - 2]
        wide_w[rows] = weight
        wide_u[rows] = weight * (start_l if col < 2 else start_o)[col % 2]
    acc[...] = jnp.zeros_like(acc)

    def target(cell, slots):
        sign = bounds[level, len(CLASSES) + 1] + 9 * (cell >= depth).astype(jnp.int32)
        pos_l = upright(feat_l[cell], slots)
        sums = [jnp.zeros((slots, 128), F32)] * 2

        def issue(chunk):
            return product(pos_l, sources_of(feat_r, cell, depth, chunk, posc, sign))

        def consume(chunk, products):
            for i, n in enumerate(chunk):
                s = jnp.maximum(products[:, 128 * i : 128 * (i + 1)], 0.0)
                q = s * s
                at = pl.ds(cell + (n // 3) * depth + n % 3 - 1, 1)
                sums[0] = sums[0] + q * wide_w[at, :]
                sums[1] = sums[1] + q * wide_u[at, :]

        def finish():
            for i in range(2):
                acc[i, pl.ds(cell, 1), 0:slots] = fold(sums[i])

        return issue, consume, finish

    each_target(level, order, bounds, target)
    diagonal = COMPRESSION + 6.0 * acc[0].reshape(2, depth, 128)
    pulled = acc[1].reshape(2, depth, 128)
    out_diag[...] = diagonal
    below = column_update(left[4, 1] > 0.0, start_l[1], recv[2], pulled[0], diagonal[0])
    here = column_update(own[4, 0] > 0.0, start_o[0], source_own[0], pulled[1], diagonal[1])
    out_p[0] = below
    out_p[1] = here
    out_send[0] = below
    out_send[1] = here
    out_send[2] = weight_own[0]
    out_send[3] = diagonal[0]


def sweep2_kernel(
    level, order, bounds, feat_r, feat_l, own, recv1, recv2, weight_own, source_own, diag, p1, posc,
    out_p, wide_u, acc,
):
    depth = weight_own.shape[1]
    wide_u[0:depth] = recv1[1] * p1[0]
    wide_u[depth : 2 * depth] = weight_own[0] * p1[1]
    wide_u[2 * depth : 3 * depth] = weight_own[1] * recv2[0]
    wide_u[3 * depth : 4 * depth] = recv2[2] * recv2[1]
    pulled = jacobi_sums(level, order, bounds, 1, feat_r, feat_l, posc, wide_u, acc, depth)
    out_p[0] = column_update(own[4, 0] > 0.0, p1[1], source_own[0], pulled[0], diag[1])
    out_p[1] = column_update(own[4, 1] > 0.0, recv2[0], source_own[1], pulled[1], recv2[3])


def sweep3_kernel(
    level, order, bounds, feat_r, feat_l, left, own, recv1, recv3, weight_own, source_own, diag, p2, posc,
    out_p, wide_u, acc,
):
    depth = weight_own.shape[1]
    wide_u[0 : 2 * depth] = (recv1[0:2] * recv3[...]).reshape(2 * depth, 128)
    wide_u[2 * depth : 4 * depth] = (weight_own[...] * p2[...]).reshape(2 * depth, 128)
    pulled = jacobi_sums(level, order, bounds, 0, feat_r, feat_l, posc, wide_u, acc, depth)
    out_p[0] = column_update(left[4, 1] > 0.0, recv3[1], recv1[2], pulled[0], diag[0])
    out_p[1] = column_update(own[4, 0] > 0.0, p2[0], source_own[0], pulled[1], diag[1])


def force_kernel(
    level, order, bounds, feat_r, feat_l, own, recv1, recv2, recv4, left, right, weight_own, p3, posc,
    out_pressure, out_acc, out_velocity, out_offsets,
    wide_p, wide_w, wide_x, wide_z, acc,
):
    depth = weight_own.shape[1]
    wide_p[0 : 2 * depth] = p3[...].reshape(2 * depth, 128)
    wide_p[2 * depth : 4 * depth] = recv4[...].reshape(2 * depth, 128)
    wide_w[0:depth] = recv1[1]
    wide_w[depth : 3 * depth] = weight_own[...].reshape(2 * depth, 128)
    wide_w[3 * depth : 4 * depth] = recv2[2]
    for field, wide in ((0, wide_x), (1, wide_z)):
        wide[0:depth] = left[field, 1] - 0.5
        wide[depth : 3 * depth] = own[field].reshape(2 * depth, 128) - 0.5
        wide[3 * depth : 4 * depth] = right[field, 0] - 0.5

    def target(cell, slots):
        sign = bounds[level, len(CLASSES) + 1] + 9 * (cell >= depth).astype(jnp.int32)
        pos_l = upright(feat_l[cell + depth], slots)
        here = spread(wide_p[pl.ds(cell + depth, 1), :], slots)
        sums = [jnp.zeros((slots, 128), F32)] * 3

        def issue(chunk):
            return product(pos_l, sources_of(feat_r, cell + depth, depth, chunk, posc, sign))

        def consume(chunk, products):
            for i, n in enumerate(chunk):
                s = jnp.maximum(products[:, 128 * i : 128 * (i + 1)], 0.0)
                at = pl.ds(cell + (n // 3) * depth + n % 3 - 1, 1)
                g = (s * wide_w[at, :]) * (s * (wide_p[at, :] - here))
                sums[0] = sums[0] + g
                sums[1] = sums[1] + g * (wide_x[at, :] + float(n // 3 - 1))
                sums[2] = sums[2] + g * (wide_z[at, :] + float(n % 3 - 1))

        def finish():
            for i in range(3):
                acc[i, pl.ds(cell, 1), 0:slots] = fold(sums[i])

        return issue, consume, finish

    acc[...] = jnp.zeros_like(acc)
    each_target(level, order, bounds, target)
    sums = acc[...].reshape(3, 2, depth, 128)
    inner = slice(HALO, depth - HALO)
    alive = own[4, :, inner] > 0.0
    out_pressure[0] = p3[1, inner]
    out_pressure[1] = recv4[0, inner]
    for axis, wide, pull in ((0, wide_x, 0.0), (1, wide_z, GRAVITY)):
        here = wide[depth : 3 * depth].reshape(2, depth, 128)
        force = 6.0 * (here[:, inner] * sums[0, :, inner] - sums[axis + 1, :, inner])
        force = jnp.where(alive, force, 0.0)
        velocity = jnp.where(alive, own[axis + 2, :, inner] + TIME_STEP * (force - pull), 0.0)
        out_acc[axis] = force
        out_velocity[axis] = velocity
        out_offsets[axis] = jnp.where(alive, own[axis, :, inner] + TIME_STEP * velocity, 0.0)


def leaving_kernel(
    slot, count, side, offsets, velocity, pressure, mass, out_up, out_down, hot
):
    blocks, slots = slot.shape
    fields = [offsets[0], offsets[1], velocity[0], velocity[1], pressure[...], mass[...]]
    fields = [f.reshape(-1, slots) for f in fields]
    cells = fields[0].shape[0]
    number = lax.broadcasted_iota(jnp.int32, (cells, slots), 0)
    place = lax.broadcasted_iota(jnp.int32, (slots, slots), 0)
    for b in range(blocks):
        one_hot = (number == slot[b : b + 1, :] // slots).astype(F32).astype(BF16)
        for part in range(3):
            hot[part * cells : (part + 1) * cells, b * slots : (b + 1) * slots] = one_hot
    filled = lax.broadcasted_iota(jnp.int32, (blocks, slots), 1) < count[...]
    up = side[...] == 1
    for index, field in enumerate(fields):
        parts = jnp.concatenate([v.astype(BF16) for v in split3(field.T)], axis=1)
        rows = []
        for b in range(blocks):
            picked = product(parts, hot[:, b * slots : (b + 1) * slots])
            here = place == slot[b : b + 1, :] % slots
            rows.append(jnp.sum(jnp.where(here, picked, 0.0), axis=0, keepdims=True))
        block = jnp.where(filled, jnp.concatenate(rows, axis=0), 0.0)
        out_up[index] = jnp.where(up, block, 0.0)
        out_down[index] = jnp.where(up, 0.0, block)


def target_lists(count, cells, tables):
    depth = count.shape[1]
    number = jnp.arange(2 * depth, dtype=jnp.int32)
    kinds = []
    for level in range(1, ITERS + 3):
        window = count[1:3] if level % 2 else count[0:2]
        kind = sum((window > slots).astype(jnp.int32) for slots, _ in CLASSES[:-1])
        reach = ITERS + 2 - level
        row = jnp.arange(depth, dtype=jnp.int32)[None]
        kind = jnp.where((row >= HALO - reach) & (row < HALO + cells + reach), kind, len(CLASSES))
        kinds.append(kind.reshape(-1))
    kinds = jnp.stack(kinds)
    key = kinds * (2 * depth) + number
    rank = jnp.sum((key[:, None, :] < key[:, :, None]).astype(jnp.int32), 2)
    steps = jnp.arange(len(CLASSES) + 1, dtype=jnp.int32)
    bounds = jnp.sum((kinds[:, None, :] < steps[None, :, None]).astype(jnp.int32), 2)
    place = jnp.arange(2 * depth + max(c for _, c in CLASSES), dtype=jnp.int32)
    order = jnp.sum(jnp.where(rank[:, None, :] == place[None, :, None], number, 0), 2)
    order = jnp.where(place < bounds[:, -1:], order, HALO)
    return order, jnp.concatenate([bounds, tables[np.arange(ITERS + 2) % 2][:, None]], 1)


def local_call(kernel, out_shapes, scratch, scalars, *operands):
    vmem = pl.BlockSpec(memory_space=pltpu.VMEM)
    smem = pl.BlockSpec(memory_space=pltpu.SMEM)
    return pl.pallas_call(
        kernel,
        out_shape=[jax.ShapeDtypeStruct(shape, dtype) for shape, dtype in out_shapes],
        in_specs=[smem] * len(scalars) + [vmem] * len(operands),
        out_specs=[vmem] * len(out_shapes),
        scratch_shapes=[pltpu.VMEM(shape, dtype) for shape, dtype in scratch],
        compiler_params=pltpu.CompilerParams(vmem_limit_bytes=VMEM_LIMIT),
    )(*scalars, *operands)


def from_behind(block, axis, distance):
    devices = range(lax.axis_size(axis))
    route = [(i - distance, i) for i in devices if i - distance in devices]
    return lax.ppermute(block, axis, route)


def around(block, axis, distance):
    peers = lax.axis_size(axis)
    return lax.ppermute(block, axis, [(i, (i + distance) % peers) for i in range(peers)])


def per_device(
    offsets, velocity, particle_mass, pressure_start, counts, leaving_slot, leaving_count, leaving_side
):
    cells, slots = counts.shape[1], offsets.shape[-1]
    alive = jnp.arange(slots, dtype=jnp.int32)[None, None, :] < counts[:, :, None]
    live_mass = jnp.where(alive, particle_mass, 0.0)
    base = jnp.concatenate([offsets, velocity, live_mass[None], pressure_start[None]], 0)
    above = from_behind(base[:, :, cells - HALO :], "slab", 1)
    below = from_behind(base[:, :, :HALO], "slab", -1)
    own = jnp.concatenate([above, base, below], 2)
    left = around(own, "col", 1)
    right = around(own[:5, :1], "col", -1)
    depth = cells + 2 * HALO
    first = lax.axis_index("col") == 0
    last = lax.axis_index("col") == lax.axis_size("col") - 1
    here = jnp.where(first, 1, jnp.where(last, 2, 0))
    back = jnp.where(first, 3, 0)
    posc = position_table()
    plane = (2, depth, slots)

    live = jnp.stack([left[4, 1], own[4, 0], own[4, 1]]) > 0.0
    lists = target_lists(jnp.sum(live.astype(jnp.int32), -1), cells, 18 * jnp.stack([here, back]))
    long = (4 * depth, slots)
    sums = (2 * depth, slots)

    feat_r, feat_l, weight, density_ratio, source, send1 = local_call(
        functools.partial(density_kernel, 0),
        [
            ((5 * depth, KP, slots), BF16),
            ((3 * depth, KP, slots), BF16),
            (plane, F32),
            (plane, F32),
            (plane, F32),
            ((3, depth, slots), F32),
        ],
        [
            ((8 * KP, slots), F32),
            (long, F32),
            (long, F32),
            (long, F32),
            (long, F32),
            (long, F32),
            ((2, *sums), F32),
        ],
        lists, left, own, right, posc,
    )
    recv1 = around(send1, "col", 1)
    p1, diag, send2 = local_call(
        functools.partial(sweep1_kernel, 1),
        [(plane, F32), (plane, F32), ((4, depth, slots), F32)],
        [(long, F32), (long, F32), ((2, *sums), F32)],
        lists, feat_r, feat_l, left, own, recv1, weight, source, posc,
    )
    recv2 = around(send2, "col", -1)
    (p2,) = local_call(
        functools.partial(sweep2_kernel, 2),
        [(plane, F32)],
        [(long, F32), (sums, F32)],
        lists, feat_r, feat_l, own, recv1, recv2, weight, source, diag, p1, posc,
    )
    recv3 = around(p2, "col", 1)
    (p3,) = local_call(
        functools.partial(sweep3_kernel, 3),
        [(plane, F32)],
        [(long, F32), (sums, F32)],
        lists, feat_r, feat_l, left, own, recv1, recv3, weight, source, diag, p2, posc,
    )
    recv4 = around(p3, "col", -1)
    inner = (2, cells, slots)
    pressure, acceleration, velocity_new, offsets_new = local_call(
        functools.partial(force_kernel, 4),
        [(inner, F32), ((2, *inner), F32), ((2, *inner), F32), ((2, *inner), F32)],
        [(long, F32)] * 4 + [((3, *sums), F32)],
        lists, feat_r, feat_l, own, recv1, recv2, recv4, left, right, weight, p3, posc,
    )
    density_ratio = density_ratio[:, HALO : HALO + cells]
    blocks = leaving_slot.shape[0]
    packed = ((6, blocks, slots), F32)
    upward, downward = local_call(
        leaving_kernel,
        [packed, packed],
        [((3 * counts.size, blocks * slots), BF16)],
        (),
        leaving_slot[:, 0], leaving_count, leaving_side, offsets_new, velocity_new, pressure, live_mass,
    )
    arrived = jnp.stack([from_behind(upward, "col", 1), from_behind(downward, "col", -1)])[:, :, :, None]
    return (density_ratio, pressure, acceleration, velocity_new, offsets_new, arrived)


def solution(mesh):
    return jax.shard_map(
        per_device,
        mesh=mesh,
        in_specs=(
            P(None, "col", "slab", None),
            P(None, "col", "slab", None),
            P("col", "slab", None),
            P("col", "slab", None),
            P("col", "slab"),
            P("col", "slab", None),
            P("col", "slab"),
            P("col", "slab"),
        ),
        out_specs=(
            P("col", "slab", None),
            P("col", "slab", None),
            P(None, "col", "slab", None),
            P(None, "col", "slab", None),
            P(None, "col", "slab", None),
            P(None, None, "col", "slab", None),
        ),
        check_vma=False,
    )
```

```python
import functools

import jax
import jax.numpy as jnp
import ml_dtypes
import numpy as np
from jax import lax
from jax.experimental import pallas as pl
from jax.experimental.pallas import tpu as pltpu
from jax.sharding import PartitionSpec as P

ITERS = 3
TIME_STEP = 0.1
REST_DENSITY = 50.0
COMPRESSION = 2.0
RELAXATION = 0.5
GRAVITY = 1.0

HALO = 8
CLASSES = ((32, 16), (64, 8), (96, 6), (128, 6))
CHUNKS = ((0, 1), (2, 3), (4, 5), (6, 7), (8,))
AHEAD = 2
KP = 32
KD = 48
KE = 16
FAR = -64.0
SHIFTS = [(sx, sz) for sx in (-1, 0, 1) for sz in (-1, 0, 1)]
F32 = jnp.float32
BF16 = jnp.bfloat16
VMEM_LIMIT = 56 * 1024 * 1024


def split3(value):
    high = value.astype(BF16).astype(F32)
    rest = value - high
    mid = rest.astype(BF16).astype(F32)
    return [high, mid, rest - mid]


ORDER = [*range(6), *range(12, 18), *range(24, 28), *range(6, 12), *range(18, 24), *range(28, 32)]


def left_six(parts):
    h, m, l = parts
    return [h, h, h, m, m, l]


def right_six(parts):
    h, m, l = parts
    return [h, m, l, h, m, h]


def position_rows(x, z):
    one, zero = jnp.ones_like(x), jnp.zeros_like(x)
    x, z = x - 0.5, z - 0.5
    xs, zs = split3(x), split3(z)
    square = x * x + z * z
    x2, z2 = [2.0 * v for v in xs], [2.0 * v for v in zs]
    ones = [one] * 3
    target = (
        left_six(x2) + x2 + ones + left_six(z2) + z2 + ones + split3(1.0 - square) + ones + [one, zero]
    )
    source = (
        right_six(xs) + ones + x2 + right_six(zs) + ones + z2 + ones + split3(-square) + [one, zero]
    )
    return [target[i] for i in ORDER], [source[i] for i in ORDER]


def position_signs(sx, sz):
    signs = [1] * 6 + [sx] * 3 + [-sx] * 3 + [1] * 6 + [sz] * 3 + [-sz] * 3 + [1] * 6 + [-(sx * sx + sz * sz), 0]
    return [signs[i] for i in ORDER]


def velocity_rows(x, z, vx, vz):
    one, zero = jnp.ones_like(x), jnp.zeros_like(x)
    x, z = x - 0.5, z - 0.5
    xs, zs, vxs, vzs = split3(x), split3(z), split3(vx), split3(vz)
    dots = split3(vx * x + vz * z)
    ones = [one] * 3
    pad = [zero] * 6
    minus = lambda rows: [-v for v in rows]
    target = dots + left_six(vxs) + left_six(vzs) + left_six(xs) + left_six(zs) + ones + vxs + vzs + ones + ones + pad
    source = (
        ones
        + minus(right_six(xs) + right_six(zs) + right_six(vxs) + right_six(vzs))
        + dots
        + ones
        + ones
        + vxs
        + vzs
        + pad
    )
    return target, source


def velocity_signs(sx, sz):
    return [1] * 30 + [-sx] * 3 + [-sz] * 3 + [sx] * 3 + [sz] * 3 + [0] * 6


def pressure_rows(weight, lifted, pressure):
    one, zero = jnp.ones_like(weight), jnp.zeros_like(weight)
    pad = [zero] * 7
    target = [one] * 3 + left_six(split3(pressure)) + pad
    source = split3(lifted) + [-v for v in right_six(split3(weight))] + pad
    return target, source


def wide_table(table):
    return np.repeat(np.asarray(table, np.float32)[:, :, None], 128, axis=2).astype(ml_dtypes.bfloat16)


def velocity_table():
    return wide_table([velocity_signs(sx, sz) for sx, sz in SHIFTS])[:, 16:]


def position_table():
    tables = []
    for cuts in ((), ((0, -1),), ((1, 1),), ((0, 1), (1, -1))):
        for t in range(2):
            for sx, sz in SHIFTS:
                signs = position_signs(sx, sz)
                if (t, sx) in cuts:
                    signs[KP - 2] = FAR
                tables.append(signs)
    return wide_table(tables)[:, 16:]


def store_rows(rows, stage, dest, cell):
    count = len(rows)
    for index, value in enumerate(rows):
        stage[pl.ds(index, 8, stride=count), :] = value
    dest[pl.ds(cell, 8)] = stage[...].reshape(8, count, 128).astype(BF16)


def upright(rows, slots):
    return rows.astype(F32).T[:slots].astype(BF16)


def sources_of(feat, cell, depth, chunk, table=None, first=0):
    parts = []
    for n in chunk:
        part = feat[cell + (n // 3) * depth + n % 3 - 1]
        if table is not None:
            fixed = part.shape[0] - table.shape[1]
            part = jnp.concatenate([part[:fixed], part[fixed:] * table[first + n]], axis=0)
        parts.append(part)
    return jnp.concatenate(parts, axis=1) if len(parts) > 1 else parts[0]


def product(left, right):
    return jnp.dot(left, right, preferred_element_type=F32)


def fold(total):
    return jnp.sum(total.T, axis=0, keepdims=True)


def each_target(level, order, bounds, target):
    for index, (slots, cells) in enumerate(CLASSES):
        start = bounds[level, index]
        steps = (bounds[level, index + 1] - start + cells - 1) // cells

        def step(i, carry, slots=slots, cells=cells, start=start):
            waiting = []
            for u in range(cells):
                issue, consume, finish = target(order[level, start + i * cells + u], slots)
                for chunk in CHUNKS:
                    waiting.append((consume, chunk, issue(chunk), finish))
                    if len(waiting) > AHEAD:
                        take(waiting.pop(0))
            for entry in waiting:
                take(entry)
            return carry

        lax.fori_loop(0, steps, step, 0)


def take(entry):
    consume, chunk, products, finish = entry
    consume(chunk, products)
    if chunk is CHUNKS[-1]:
        finish()


def density_kernel(
    level, order, bounds, left, own, right, posc, velc,
    out_r, out_l, out_w, out_density, out_source, out_send,
    stage_p, stage_d, vel_r, vel_l, wide_m, acc,
):
    depth = own.shape[2]
    groups = depth // 8
    blocks = [(left, 0), (left, 1), (own, 0), (own, 1), (right, 0)]

    def prepare(group, carry):
        rows = pl.ds(pl.multiple_of(group * 8, 8), 8)
        for col, (ref, at) in enumerate(blocks):
            x, z, vx, vz = (ref[f, at, rows, :] for f in range(4))
            cell = pl.multiple_of(col * depth + group * 8, 8)
            target, source = position_rows(x, z)
            store_rows(source, stage_p, out_r, cell)
            if 1 <= col <= 3:
                store_rows(target, stage_p, out_l, pl.multiple_of((col - 1) * depth + group * 8, 8))
            if col >= 1:
                target, source = velocity_rows(x, z, vx, vz)
                store_rows(source, stage_d, vel_r, pl.multiple_of((col - 1) * depth + group * 8, 8))
                if 2 <= col <= 3:
                    store_rows(target, stage_d, vel_l, pl.multiple_of((col - 2) * depth + group * 8, 8))
        return carry

    lax.fori_loop(0, groups, prepare, 0)
    acc[...] = jnp.zeros_like(acc)

    wide_m[0:depth] = left[4, 1]
    wide_m[depth : 2 * depth] = own[4, 0]
    wide_m[2 * depth : 3 * depth] = own[4, 1]
    wide_m[3 * depth : 4 * depth] = right[4, 0]

    def target(cell, slots):
        sign = bounds[level, len(CLASSES) + 1] + 9 * (cell >= depth).astype(jnp.int32)
        pos_l, vel_l_t = upright(out_l[cell + depth], slots), upright(vel_l[cell], slots)
        sums = [jnp.zeros((slots, 128), F32)] * 2

        def issue(chunk):
            return (
                product(pos_l, sources_of(out_r, cell + depth, depth, chunk, posc, sign)),
                product(vel_l_t, sources_of(vel_r, cell, depth, chunk, velc)),
            )

        def consume(chunk, products):
            for i, n in enumerate(chunk):
                lanes = slice(128 * i, 128 * (i + 1))
                s = jnp.maximum(products[0][:, lanes], 0.0)
                q = s * s * wide_m[pl.ds(cell + (n // 3) * depth + n % 3 - 1, 1), :]
                sums[0] = sums[0] + q * s
                sums[1] = sums[1] + q * products[1][:, lanes]

        def finish():
            for i in range(2):
                acc[i, pl.ds(cell, 1), 0:slots] = fold(sums[i])

        return issue, consume, finish

    each_target(level, order, bounds, target)
    density = acc[0].reshape(2, depth, 128)
    div = -6.0 * acc[1].reshape(2, depth, 128)
    mass = own[4]
    alive = mass > 0.0
    density = jnp.where(alive, density, 0.0)
    weight = jnp.where(alive, mass / jnp.where(alive, density, 1.0), 0.0)
    source = jnp.where(
        alive, (density + TIME_STEP * div - REST_DENSITY) / REST_DENSITY, 0.0
    )
    out_w[...] = weight
    out_density[...] = density / REST_DENSITY
    out_source[...] = source
    out_send[0:2] = weight
    out_send[2] = source[1]


def column_update(alive, pressure, source, pulled, diagonal):
    updated = (1.0 - RELAXATION) * pressure + RELAXATION * (source + 6.0 * pulled) / diagonal
    return jnp.where(alive, updated, 0.0)


def jacobi_sums(level, order, bounds, first_col, feat_r, feat_l, posc, wide_u, acc, depth):
    def target(cell, slots):
        sign = bounds[level, len(CLASSES) + 1] + 9 * (cell >= depth).astype(jnp.int32)
        at = cell + first_col * depth
        pos_l = upright(feat_l[at], slots)
        sums = [jnp.zeros((slots, 128), F32)]

        def issue(chunk):
            return product(pos_l, sources_of(feat_r, at, depth, chunk, posc, sign))

        def consume(chunk, products):
            for i, n in enumerate(chunk):
                s = jnp.maximum(products[:, 128 * i : 128 * (i + 1)], 0.0)
                lifted = wide_u[pl.ds(cell + (n // 3) * depth + n % 3 - 1, 1), :]
                sums[0] = sums[0] + s * s * lifted

        def finish():
            acc[pl.ds(cell, 1), 0:slots] = fold(sums[0])

        return issue, consume, finish

    acc[...] = jnp.zeros_like(acc)
    each_target(level, order, bounds, target)
    return acc[...].reshape(2, depth, 128)


def sweep1_kernel(
    level, order, bounds, feat_r, feat_l, left, own, recv, weight_own, source_own, posc,
    out_p, out_diag, out_send, wide_w, wide_u, acc,
):
    depth = weight_own.shape[1]
    start_l = jnp.where(left[4] > 0.0, left[5], 0.0)
    start_o = jnp.where(own[4] > 0.0, own[5], 0.0)
    for col in range(4):
        rows = slice(col * depth, (col + 1) * depth)
        weight = recv[col] if col < 2 else weight_own[col - 2]
        wide_w[rows] = weight
        wide_u[rows] = weight * (start_l if col < 2 else start_o)[col % 2]
    acc[...] = jnp.zeros_like(acc)

    def target(cell, slots):
        sign = bounds[level, len(CLASSES) + 1] + 9 * (cell >= depth).astype(jnp.int32)
        pos_l = upright(feat_l[cell], slots)
        sums = [jnp.zeros((slots, 128), F32)] * 2

        def issue(chunk):
            return product(pos_l, sources_of(feat_r, cell, depth, chunk, posc, sign))

        def consume(chunk, products):
            for i, n in enumerate(chunk):
                s = jnp.maximum(products[:, 128 * i : 128 * (i + 1)], 0.0)
                q = s * s
                at = pl.ds(cell + (n // 3) * depth + n % 3 - 1, 1)
                sums[0] = sums[0] + q * wide_w[at, :]
                sums[1] = sums[1] + q * wide_u[at, :]

        def finish():
            for i in range(2):
                acc[i, pl.ds(cell, 1), 0:slots] = fold(sums[i])

        return issue, consume, finish

    each_target(level, order, bounds, target)
    diagonal = COMPRESSION + 6.0 * acc[0].reshape(2, depth, 128)
    pulled = acc[1].reshape(2, depth, 128)
    out_diag[...] = diagonal
    below = column_update(left[4, 1] > 0.0, start_l[1], recv[2], pulled[0], diagonal[0])
    here = column_update(own[4, 0] > 0.0, start_o[0], source_own[0], pulled[1], diagonal[1])
    out_p[0] = below
    out_p[1] = here
    out_send[0] = below
    out_send[1] = here
    out_send[2] = weight_own[0]
    out_send[3] = diagonal[0]


def sweep2_kernel(
    level, order, bounds, feat_r, feat_l, own, recv1, recv2, weight_own, source_own, diag, p1, posc,
    out_p, wide_u, acc,
):
    depth = weight_own.shape[1]
    wide_u[0:depth] = recv1[1] * p1[0]
    wide_u[depth : 2 * depth] = weight_own[0] * p1[1]
    wide_u[2 * depth : 3 * depth] = weight_own[1] * recv2[0]
    wide_u[3 * depth : 4 * depth] = recv2[2] * recv2[1]
    pulled = jacobi_sums(level, order, bounds, 1, feat_r, feat_l, posc, wide_u, acc, depth)
    out_p[0] = column_update(own[4, 0] > 0.0, p1[1], source_own[0], pulled[0], diag[1])
    out_p[1] = column_update(own[4, 1] > 0.0, recv2[0], source_own[1], pulled[1], recv2[3])


def sweep3_kernel(
    level, order, bounds, feat_r, feat_l, left, own, recv1, recv3, weight_own, source_own, diag, p2, posc,
    out_p, wide_u, acc,
):
    depth = weight_own.shape[1]
    wide_u[0 : 2 * depth] = (recv1[0:2] * recv3[...]).reshape(2 * depth, 128)
    wide_u[2 * depth : 4 * depth] = (weight_own[...] * p2[...]).reshape(2 * depth, 128)
    pulled = jacobi_sums(level, order, bounds, 0, feat_r, feat_l, posc, wide_u, acc, depth)
    out_p[0] = column_update(left[4, 1] > 0.0, recv3[1], recv1[2], pulled[0], diag[0])
    out_p[1] = column_update(own[4, 0] > 0.0, p2[0], source_own[0], pulled[1], diag[1])


def force_kernel(
    level, order, bounds, feat_r, feat_l, own, recv1, recv2, recv4, left, right, weight_own, p3, posc,
    out_pressure, out_acc, out_velocity, out_offsets,
    wide_p, wide_w, wide_x, wide_z, pres_r, pres_l, stage, acc,
):
    depth = weight_own.shape[1]
    wide_p[0:2] = p3[...]
    wide_p[2:4] = recv4[...]
    wide_w[0] = recv1[1]
    wide_w[1:3] = weight_own[...]
    wide_w[3] = recv2[2]
    for field, wide in ((0, wide_x), (1, wide_z)):
        wide[0:depth] = left[field, 1] - 0.5
        wide[depth : 3 * depth] = own[field].reshape(2 * depth, 128) - 0.5
        wide[3 * depth : 4 * depth] = right[field, 0] - 0.5

    def prepare(group, carry):
        rows = pl.ds(pl.multiple_of(group * 8, 8), 8)
        for col in range(4):
            pressure, weight = wide_p[col, rows, :], wide_w[col, rows, :]
            target, source = pressure_rows(weight, weight * pressure, pressure)
            store_rows(source, stage, pres_r, pl.multiple_of(col * depth + group * 8, 8))
            if 1 <= col <= 2:
                store_rows(target, stage, pres_l, pl.multiple_of((col - 1) * depth + group * 8, 8))
        return carry

    lax.fori_loop(0, depth // 8, prepare, 0)

    def target(cell, slots):
        sign = bounds[level, len(CLASSES) + 1] + 9 * (cell >= depth).astype(jnp.int32)
        pos_l, pres_l_t = upright(feat_l[cell + depth], slots), upright(pres_l[cell], slots)
        sums = [jnp.zeros((slots, 128), F32)] * 3

        def issue(chunk):
            return (
                product(pos_l, sources_of(feat_r, cell + depth, depth, chunk, posc, sign)),
                product(pres_l_t, sources_of(pres_r, cell, depth, chunk)),
            )

        def consume(chunk, products):
            for i, n in enumerate(chunk):
                lanes = slice(128 * i, 128 * (i + 1))
                s = jnp.maximum(products[0][:, lanes], 0.0)
                g = s * s * products[1][:, lanes]
                at = pl.ds(cell + (n // 3) * depth + n % 3 - 1, 1)
                sums[0] = sums[0] + g
                sums[1] = sums[1] + g * (wide_x[at, :] + float(n // 3 - 1))
                sums[2] = sums[2] + g * (wide_z[at, :] + float(n % 3 - 1))

        def finish():
            for i in range(3):
                acc[i, pl.ds(cell, 1), 0:slots] = fold(sums[i])

        return issue, consume, finish

    acc[...] = jnp.zeros_like(acc)
    each_target(level, order, bounds, target)
    sums = acc[...].reshape(3, 2, depth, 128)
    inner = slice(HALO, depth - HALO)
    alive = own[4, :, inner] > 0.0
    out_pressure[0] = p3[1, inner]
    out_pressure[1] = recv4[0, inner]
    for axis, wide, pull in ((0, wide_x, 0.0), (1, wide_z, GRAVITY)):
        here = wide[depth : 3 * depth].reshape(2, depth, 128)
        force = 6.0 * (here[:, inner] * sums[0, :, inner] - sums[axis + 1, :, inner])
        force = jnp.where(alive, force, 0.0)
        velocity = jnp.where(alive, own[axis + 2, :, inner] + TIME_STEP * (force - pull), 0.0)
        out_acc[axis] = force
        out_velocity[axis] = velocity
        out_offsets[axis] = jnp.where(alive, own[axis, :, inner] + TIME_STEP * velocity, 0.0)


def leaving_kernel(
    slot, count, side, offsets, velocity, pressure, mass, out_up, out_down, hot
):
    blocks, slots = slot.shape
    fields = [offsets[0], offsets[1], velocity[0], velocity[1], pressure[...], mass[...]]
    fields = [f.reshape(-1, slots) for f in fields]
    cells = fields[0].shape[0]
    number = lax.broadcasted_iota(jnp.int32, (cells, slots), 0)
    place = lax.broadcasted_iota(jnp.int32, (slots, slots), 0)
    for b in range(blocks):
        one_hot = (number == slot[b : b + 1, :] // slots).astype(F32).astype(BF16)
        for part in range(3):
            hot[part * cells : (part + 1) * cells, b * slots : (b + 1) * slots] = one_hot
    filled = lax.broadcasted_iota(jnp.int32, (blocks, slots), 1) < count[...]
    up = side[...] == 1
    for index, field in enumerate(fields):
        parts = jnp.concatenate([v.astype(BF16) for v in split3(field.T)], axis=1)
        rows = []
        for b in range(blocks):
            picked = product(parts, hot[:, b * slots : (b + 1) * slots])
            here = place == slot[b : b + 1, :] % slots
            rows.append(jnp.sum(jnp.where(here, picked, 0.0), axis=0, keepdims=True))
        block = jnp.where(filled, jnp.concatenate(rows, axis=0), 0.0)
        out_up[index] = jnp.where(up, block, 0.0)
        out_down[index] = jnp.where(up, 0.0, block)


def target_lists(count, cells, tables):
    depth = count.shape[1]
    number = jnp.arange(2 * depth, dtype=jnp.int32)
    kinds = []
    for level in range(1, ITERS + 3):
        window = count[1:3] if level % 2 else count[0:2]
        kind = sum((window > slots).astype(jnp.int32) for slots, _ in CLASSES[:-1])
        reach = ITERS + 2 - level
        row = jnp.arange(depth, dtype=jnp.int32)[None]
        kind = jnp.where((row >= HALO - reach) & (row < HALO + cells + reach), kind, len(CLASSES))
        kinds.append(kind.reshape(-1))
    kinds = jnp.stack(kinds)
    key = kinds * (2 * depth) + number
    rank = jnp.sum((key[:, None, :] < key[:, :, None]).astype(jnp.int32), 2)
    steps = jnp.arange(len(CLASSES) + 1, dtype=jnp.int32)
    bounds = jnp.sum((kinds[:, None, :] < steps[None, :, None]).astype(jnp.int32), 2)
    place = jnp.arange(2 * depth + max(c for _, c in CLASSES), dtype=jnp.int32)
    order = jnp.sum(jnp.where(rank[:, None, :] == place[None, :, None], number, 0), 2)
    order = jnp.where(place < bounds[:, -1:], order, HALO)
    return order, jnp.concatenate([bounds, tables[np.arange(ITERS + 2) % 2][:, None]], 1)


def local_call(kernel, out_shapes, scratch, scalars, *operands):
    vmem = pl.BlockSpec(memory_space=pltpu.VMEM)
    smem = pl.BlockSpec(memory_space=pltpu.SMEM)
    return pl.pallas_call(
        kernel,
        out_shape=[jax.ShapeDtypeStruct(shape, dtype) for shape, dtype in out_shapes],
        in_specs=[smem] * len(scalars) + [vmem] * len(operands),
        out_specs=[vmem] * len(out_shapes),
        scratch_shapes=[pltpu.VMEM(shape, dtype) for shape, dtype in scratch],
        compiler_params=pltpu.CompilerParams(vmem_limit_bytes=VMEM_LIMIT),
    )(*scalars, *operands)


def from_behind(block, axis, distance):
    devices = range(lax.axis_size(axis))
    route = [(i - distance, i) for i in devices if i - distance in devices]
    return lax.ppermute(block, axis, route)


def around(block, axis, distance):
    peers = lax.axis_size(axis)
    return lax.ppermute(block, axis, [(i, (i + distance) % peers) for i in range(peers)])


def per_device(
    offsets, velocity, particle_mass, pressure_start, counts, leaving_slot, leaving_count, leaving_side
):
    cells, slots = counts.shape[1], offsets.shape[-1]
    alive = jnp.arange(slots, dtype=jnp.int32)[None, None, :] < counts[:, :, None]
    live_mass = jnp.where(alive, particle_mass, 0.0)
    base = jnp.concatenate([offsets, velocity, live_mass[None], pressure_start[None]], 0)
    above = from_behind(base[:, :, cells - HALO :], "slab", 1)
    below = from_behind(base[:, :, :HALO], "slab", -1)
    own = jnp.concatenate([above, base, below], 2)
    left = around(own, "col", 1)
    right = around(own[:5, :1], "col", -1)
    depth = cells + 2 * HALO
    first = lax.axis_index("col") == 0
    last = lax.axis_index("col") == lax.axis_size("col") - 1
    here = jnp.where(first, 1, jnp.where(last, 2, 0))
    back = jnp.where(first, 3, 0)
    posc, velc = position_table(), velocity_table()
    plane = (2, depth, slots)

    live = jnp.stack([left[4, 1], own[4, 0], own[4, 1]]) > 0.0
    lists = target_lists(jnp.sum(live.astype(jnp.int32), -1), cells, 18 * jnp.stack([here, back]))
    long = (4 * depth, slots)
    sums = (2 * depth, slots)

    feat_r, feat_l, weight, density_ratio, source, send1 = local_call(
        functools.partial(density_kernel, 0),
        [
            ((5 * depth, KP, slots), BF16),
            ((3 * depth, KP, slots), BF16),
            (plane, F32),
            (plane, F32),
            (plane, F32),
            ((3, depth, slots), F32),
        ],
        [
            ((8 * KP, slots), F32),
            ((8 * KD, slots), F32),
            ((4 * depth, KD, slots), BF16),
            ((2 * depth, KD, slots), BF16),
            (long, F32),
            ((2, *sums), F32),
        ],
        lists, left, own, right, posc, velc,
    )
    recv1 = around(send1, "col", 1)
    p1, diag, send2 = local_call(
        functools.partial(sweep1_kernel, 1),
        [(plane, F32), (plane, F32), ((4, depth, slots), F32)],
        [(long, F32), (long, F32), ((2, *sums), F32)],
        lists, feat_r, feat_l, left, own, recv1, weight, source, posc,
    )
    recv2 = around(send2, "col", -1)
    (p2,) = local_call(
        functools.partial(sweep2_kernel, 2),
        [(plane, F32)],
        [(long, F32), (sums, F32)],
        lists, feat_r, feat_l, own, recv1, recv2, weight, source, diag, p1, posc,
    )
    recv3 = around(p2, "col", 1)
    (p3,) = local_call(
        functools.partial(sweep3_kernel, 3),
        [(plane, F32)],
        [(long, F32), (sums, F32)],
        lists, feat_r, feat_l, left, own, recv1, recv3, weight, source, diag, p2, posc,
    )
    recv4 = around(p3, "col", -1)
    inner = (2, cells, slots)
    pressure, acceleration, velocity_new, offsets_new = local_call(
        functools.partial(force_kernel, 4),
        [(inner, F32), ((2, *inner), F32), ((2, *inner), F32), ((2, *inner), F32)],
        [((4, depth, slots), F32)] * 2
        + [(long, F32)] * 2
        + [
            ((4 * depth, KE, slots), BF16),
            ((2 * depth, KE, slots), BF16),
            ((8 * KE, slots), F32),
            ((3, *sums), F32),
        ],
        lists, feat_r, feat_l, own, recv1, recv2, recv4, left, right, weight, p3, posc,
    )
    density_ratio = density_ratio[:, HALO : HALO + cells]
    blocks = leaving_slot.shape[0]
    packed = ((6, blocks, slots), F32)
    upward, downward = local_call(
        leaving_kernel,
        [packed, packed],
        [((3 * counts.size, blocks * slots), BF16)],
        (),
        leaving_slot[:, 0], leaving_count, leaving_side, offsets_new, velocity_new, pressure, live_mass,
    )
    arrived = jnp.stack([from_behind(upward, "col", 1), from_behind(downward, "col", -1)])[:, :, :, None]
    return (density_ratio, pressure, acceleration, velocity_new, offsets_new, arrived)


def solution(mesh):
    return jax.shard_map(
        per_device,
        mesh=mesh,
        in_specs=(
            P(None, "col", "slab", None),
            P(None, "col", "slab", None),
            P("col", "slab", None),
            P("col", "slab", None),
            P("col", "slab"),
            P("col", "slab", None),
            P("col", "slab"),
            P("col", "slab"),
        ),
        out_specs=(
            P("col", "slab", None),
            P("col", "slab", None),
            P(None, "col", "slab", None),
            P(None, "col", "slab", None),
            P(None, "col", "slab", None),
            P(None, None, "col", "slab", None),
        ),
        check_vma=False,
    )
```
